32 devices in a mesh: dp: 16 (over z, y, x), tensor: 2 (over core).
Axes of the slice: x: 2, y: 2, z: 4, core: 2. Of those that a mesh axis runs over, the one named last changes fastest.
Arguments:
- tokens: bfloat16 [4096, 1152], P('dp'), may hold values from -6 to 6
- segment_ids: int32 [4096], P('dp'), may hold values from 0 to 3, as said below
- timesteps: int32 [16, 4], P('dp'), may hold values from 0 to 999
- norm_gain: float32 [2, 2, 1152], replicated, may hold values from 0.5 to 1.5
- norm_bias: float32 [2, 2, 1152], replicated, may hold values from -3 to 3
- token_proj: bfloat16 [2, 3, 1152, 1152], P(None, None, None, 'tensor'), may hold values from -0.1875 to 0.1875
- time_proj: bfloat16 [2, 2, 1152, 1152], P(None, None, None, 'tensor'), may hold values from -0.1875 to 0.1875
- bias_table: float32 [2, 16, 1024], P(None, 'tensor'), may hold values from -4 to 4
- out_proj: bfloat16 [2, 1152, 1152], P(None, 'tensor'), may hold values from -0.1875 to 0.1875
- hidden_in: bfloat16 [2, 1152, 4608], P(None, None, 'tensor'), may hold values from -0.1875 to 0.1875
- hidden_out: bfloat16 [2, 4608, 1152], P(None, 'tensor'), may hold values from -0.09375 to 0.09375
- branch_bias: float32 [2, 2, 1152], replicated, may hold values from -3 to 3
- cotangent: bfloat16 [4096, 1152], P('dp'), may hold values from -6 to 6
Outputs:
- output_tokens: bfloat16 [4096, 1152], P('dp')
- gradient_tokens: bfloat16 [4096, 1152], P('dp')
- gradient_gain: float32 [2, 2, 1152], P(None, None, 'dp')
- gradient_shift: float32 [2, 2, 1152], P(None, None, 'dp')
- gradient_token_proj: float32 [2, 3, 1152, 1152], P(None, None, 'dp', 'tensor')
- gradient_time_proj: float32 [2, 2, 1152, 1152], P(None, None, 'dp', 'tensor')
- gradient_table: float32 [2, 16, 1024], P(None, 'tensor', 'dp')
- gradient_out_proj: float32 [2, 1152, 1152], P(None, ('tensor', 'dp'))
- gradient_hidden_in: float32 [2, 1152, 4608], P(None, 'dp', 'tensor')
- gradient_hidden_out: float32 [2, 4608, 1152], P(None, ('tensor', 'dp'))
- gradient_branch_bias: float32 [2, 2, 1152], P(None, None, 'dp')
The draws below stay inside these ranges and needn't reach their ends.
Inputs may be any that keep to these rules, and one draw needn't show every extreme that they name: `segment_ids`: within each row of 256 tokens the image slots are numbered 0, 1, 2, ... in order of position. Each aligned block of 256 tokens of a row holds either one image of 16 x 16 latent patches or four images of (8) x (8) patches, each in raster order; some row holds only small images and some row a large one.
All inputs are finite; a program needn't handle non-finite values.
Results may differ from the reference program's by a relative error of at most 0.017.
Values sent between devices are 32-bit elements; how exact they have to be, the bound alone decides.
No kernel may reach another device: no remote copies, remote signals or barrier semaphores. Data moves between devices by JAX's collectives and lax.ppermute only.
A program may use at most 320 MiB of HBM per device.

```python
import math
import jax
import jax.numpy as jnp
from jax import lax

D = 1152
HEADS = 16
HEAD_DIM = 72
FF = 4608
SIDE = 16
LAYERS = 2
TOK_DEV = 256
MAXSEG = 4
TABLE = 1024
TOKENS = 4096
N_DP = 16


def draw_segment_ids(key, part):
    key = jax.random.fold_in(key, 11)
    span = SIDE * SIDE
    blocks = TOK_DEV // span
    pick = jax.random.randint(jax.random.fold_in(key, 1), (N_DP, blocks), 0, 2).astype(jnp.int32)
    small_row = jax.random.randint(jax.random.fold_in(key, 2), (), 0, N_DP).astype(jnp.int32)
    rows = jnp.arange(N_DP, dtype=jnp.int32)
    pick = jnp.where((rows == small_row)[:, None], 0, pick)
    forced = (rows == (small_row + 1) % N_DP)[:, None] & (jnp.arange(blocks, dtype=jnp.int32)[None, :] == 0)
    pick = jnp.where(forced, 1, pick)
    count = jnp.where(pick == 1, 1, 4).astype(jnp.int32)
    start = jnp.cumsum(count, axis=1) - count
    inside = jnp.arange(span, dtype=jnp.int32)
    local = jnp.where(pick[:, :, None] == 1, 0, inside[None, None, :] // (span // 4))
    return (start[:, :, None] + local).reshape(N_DP * TOK_DEV).astype(jnp.int32)


def with_ends(drawn, own_key, smallest, high):
    shape = drawn.shape
    spot = [jax.random.randint(jax.random.fold_in(own_key, axis), (), 0, shape[axis]) for axis in range(len(shape))]
    drawn = drawn.at[tuple(spot)].set(smallest)
    longest = shape.index(max(shape))
    spot[longest] = (spot[longest] + 1) % shape[longest]
    return drawn.at[tuple(spot)].set(high)


def spiked(drawn, key, source, target, shards_of, factor):
    owner, partner = [(jnp.arange(drawn.shape[position]) // (drawn.shape[position] // shards_of)).reshape([-1 if axis == position else 1 for axis in range(drawn.ndim)]) for position in (source, target)]
    chosen = jax.random.permutation(key, shards_of)[partner]
    strong = (owner == chosen) | (owner == (partner + shards_of // 2) % shards_of)
    return jnp.where(strong, factor * drawn, drawn)


def level_of(own_key, extent, split, smallest, high):
    level, own = 1.0, jax.random.fold_in(own_key, 6)
    for axis_at, blocks in split:
        draws = jnp.exp(jax.random.uniform(jax.random.fold_in(own, axis_at), (blocks,), jnp.float32, smallest / len(split), high / len(split)))
        level = level * jnp.repeat(draws, extent[axis_at] // blocks).reshape([-1 if axis == axis_at else 1 for axis in range(len(extent))])
    return level


def normal_values(rng, extent, scale, reach, cuts=(), kind=jnp.bfloat16):
    values = jax.random.normal(rng, extent, jnp.float32) * scale
    if len(cuts) > 0:
        values = level_of(rng, extent, cuts, -0.22, 0.18) * values
    return jnp.clip(values, min=-reach, max=reach).astype(kind)


def noise_with(rng, shape, deviation, bound, split, heavy, kind=jnp.bfloat16):
    drawn = deviation * jax.random.normal(rng, shape, jnp.float32)
    if split:
        drawn = drawn * level_of(rng, shape, split, -0.22, 0.18)
    return jnp.clip(spiked(drawn, jax.random.fold_in(rng, 3), *heavy), -bound, bound).astype(kind)


def setup_inputs(seed: int = 0) -> dict:
    streams_of = jax.random.split(jax.random.key(seed), 14)
    tokens = normal_values(streams_of[0], (TOKENS, D), 1.0, 6.0, ((0, 16),))
    segment_ids = draw_segment_ids(jax.random.fold_in(streams_of[13], 71), 0)
    timesteps = with_ends(jax.random.randint(streams_of[2], (N_DP, MAXSEG), 0, 1000), jax.random.fold_in(streams_of[2], 1), 0, 999).astype(jnp.int32)
    norm_gain = jnp.clip(1.0 + 0.1 * jax.random.normal(streams_of[3], (LAYERS, 2, D), jnp.float32), 0.5, 1.5)
    norm_bias = normal_values(streams_of[4], (LAYERS, 2, D), 0.5, 3.0, (), jnp.float32)
    token_proj = normal_values(streams_of[5], (LAYERS, 3, D, D), D ** -0.5, 0.1875, ((3, 2),))
    time_proj = normal_values(streams_of[6], (LAYERS, 2, D, D), D ** -0.5, 0.1875, ((3, 2),))
    bias_table = normal_values(streams_of[7], (LAYERS, HEADS, TABLE), 1.0, 4.0, ((1, 2),), jnp.float32)
    out_proj = normal_values(streams_of[8], (LAYERS, D, D), D ** -0.5, 0.1875, ((1, 2),))
    hidden_in = normal_values(streams_of[9], (LAYERS, D, FF), D ** -0.5, 0.1875, ((2, 2),))
    hidden_out = normal_values(streams_of[10], (LAYERS, FF, D), FF ** -0.5, 0.09375, ((1, 2),))
    branch_bias = normal_values(streams_of[11], (LAYERS, 2, D), 0.5, 3.0, (), jnp.float32)
    cotangent = noise_with(streams_of[12], (TOKENS, D), 1.0, 6.0, ((0, 16),), (0, 1, 16, 2.0))
    return {"tokens": tokens, "segment_ids": segment_ids, "timesteps": timesteps, "norm_gain": norm_gain, "norm_bias": norm_bias, "token_proj": token_proj, "time_proj": time_proj, "bias_table": bias_table, "out_proj": out_proj, "hidden_in": hidden_in, "hidden_out": hidden_out, "branch_bias": branch_bias, "cotangent": cotangent}


EPSILON = 1e-06
MASKED = -1e+30
ROOT_HALF = 0.7071067811865476

@jax.custom_vjp
def low(v):
    return lax.optimization_barrier(v.astype(jnp.bfloat16)).astype(jnp.float32)

@jax.custom_vjp
def low_back(v):
    return v

def low_keep(v):
    return (low(v), None)

def low_pass(kept, grad):
    return (grad,)

def back_keep(v):
    return (v, None)

def back_low(kept, grad):
    return (low(grad),)
low.defvjp(low_keep, low_pass)
low_back.defvjp(back_keep, back_low)

def round_both(value):
    return low(low_back(value))

def layer_norm(stream, gain, shift):
    center = stream - lax.optimization_barrier(jnp.mean(stream, axis=-1, keepdims=True))
    inverse = lax.rsqrt(lax.optimization_barrier(jnp.mean(center * center, axis=-1, keepdims=True)) + EPSILON)
    return center * inverse * gain + shift

def sinusoid(steps, width):
    half = width // 2
    rates = jnp.exp(-math.log(10000.0) * jnp.arange(half, dtype=jnp.float32) / half)
    angles = steps.astype(jnp.float32)[..., None] * rates
    return jnp.concatenate([jnp.cos(angles), jnp.sin(angles)], axis=-1)

def gelu_value(hidden):
    return 0.5 * hidden * (1.0 + lax.erf(hidden * ROOT_HALF))

def grid_places(segment_rows):
    span = SIDE * SIDE
    blocked = segment_rows.reshape(segment_rows.shape[0], -1, span)
    large = blocked[:, :, :1] == blocked[:, :, -1:]
    inside = jnp.arange(span, dtype=jnp.int32)
    place = jnp.where(large, inside, inside % (span // 4)).astype(jnp.int32)
    side = jnp.where(large, SIDE, SIDE // 2).astype(jnp.int32)
    grid_row = (place // side).astype(jnp.int32).reshape(segment_rows.shape)
    grid_col = (place % side).astype(jnp.int32).reshape(segment_rows.shape)
    return (grid_row, grid_col)

def attend_row(table, queries, keys, values, segments, grid_row, grid_col):
    scores = jnp.einsum('qhd,khd->hqk', queries, keys, precision=lax.Precision.HIGHEST) * (1.0 / math.sqrt(HEAD_DIM))
    offset = (grid_row[:, None] - grid_row[None, :] + SIDE) * (2 * SIDE) + grid_col[:, None] - grid_col[None, :] + SIDE
    scores = low_back(scores + jnp.take(table, offset.astype(jnp.int32), axis=1))
    same = segments[:, None] == segments[None, :]
    masked = jnp.where(same[None], scores, MASKED)
    peak = lax.optimization_barrier(jnp.max(masked, axis=-1, keepdims=True))
    expo = jnp.exp(masked - peak)
    weights = low(expo / lax.optimization_barrier(jnp.sum(expo, axis=-1, keepdims=True)))
    return jnp.einsum('hqk,khd->qhd', weights, values, precision=lax.Precision.HIGHEST)

def reference(tokens, segment_ids, timesteps, norm_gain, norm_bias, token_proj, time_proj, bias_table, out_proj, hidden_in, hidden_out, branch_bias, cotangent):
    segment_rows = segment_ids.reshape(N_DP, TOK_DEV)
    grid_row, grid_col = grid_places(segment_rows)
    embedded = low(sinusoid(timesteps, D))
    image_index = (jnp.arange(N_DP, dtype=jnp.int32)[:, None] * MAXSEG + segment_rows).reshape(-1).astype(jnp.int32)

    def product(left, right):
        return jnp.dot(left, right, precision=lax.Precision.HIGHEST)

    def forward(stream, gains, shifts, token_weights, time_weights, table, out_weights, in_weights, outer_weights, biases):
        for layer in range(LAYERS):
            normed = low(layer_norm(stream, gains[layer, 0], shifts[layer, 0]))
            per_image = jnp.einsum('rsd,jde->jrse', embedded, time_weights[layer], precision=lax.Precision.HIGHEST)
            per_token = per_image.reshape(2, N_DP * MAXSEG, D)[:, image_index]
            projected = jnp.einsum('td,jde->jte', normed, token_weights[layer], precision=lax.Precision.HIGHEST)
            queries = round_both(projected[0] + per_token[0])
            keys = round_both(projected[1])
            values = round_both(projected[2] + per_token[1])
            table_layer = table[layer]

            def one_row(row):
                return jax.checkpoint(attend_row)(table_layer, row[0], row[1], row[2], row[3], row[4], row[5])
            rows = (queries.reshape(N_DP, TOK_DEV, HEADS, HEAD_DIM), keys.reshape(N_DP, TOK_DEV, HEADS, HEAD_DIM), values.reshape(N_DP, TOK_DEV, HEADS, HEAD_DIM), segment_rows, grid_row, grid_col)
            attended = lax.map(one_row, rows)
            attended = round_both(attended.reshape(TOKENS, D))
            stream = stream + low_back(product(attended, out_weights[layer]) + biases[layer, 0])
            normed = low(layer_norm(stream, gains[layer, 1], shifts[layer, 1]))
            hidden = low_back(product(normed, in_weights[layer]))
            activated = low(gelu_value(hidden))
            stream = stream + low_back(product(activated, outer_weights[layer]) + biases[layer, 1])
        return stream
    result, pullback = jax.vjp(forward, tokens.astype(jnp.float32), norm_gain, norm_bias, token_proj.astype(jnp.float32), time_proj.astype(jnp.float32), bias_table, out_proj.astype(jnp.float32), hidden_in.astype(jnp.float32), hidden_out.astype(jnp.float32), branch_bias)
    grads = pullback(cotangent.astype(jnp.float32))
    return (result.astype(jnp.bfloat16), grads[0].astype(jnp.bfloat16), grads[1], grads[2], grads[3], grads[4], grads[5], grads[6], grads[7], grads[8], grads[9])
```

```python
import functools
import math

import jax
import jax.numpy as jnp
from jax import lax
from jax.experimental import pallas as pl
from jax.experimental.pallas import tpu as pltpu
from jax.sharding import Mesh
from jax.sharding import PartitionSpec as P

SIDE = 16
HALF = 8
IMAGES = 4
EPSILON = 1e-06
MASKED = -1e30
ROOT_HALF = 0.7071067811865476
SLOPE_NORM = 0.3989422804014327
LINES = ("line", "col", "row")


def layer_norm(stream, gain, shift):
    center = stream - jnp.mean(stream, axis=-1, keepdims=True)
    inverse = lax.rsqrt(jnp.mean(center * center, axis=-1, keepdims=True) + EPSILON)
    normal = center * inverse
    return (normal * gain + shift, normal, inverse)


def norm_backward(normal, inverse, gain, upstream):
    gain_part = jnp.sum(upstream * normal, axis=0)
    shift_part = jnp.sum(upstream, axis=0)
    scaled = upstream * gain
    inner = (
        scaled
        - jnp.mean(scaled, axis=-1, keepdims=True)
        - normal * jnp.mean(scaled * normal, axis=-1, keepdims=True)
    )
    return (inner * inverse, gain_part, shift_part)


def sinusoid(steps, feature, width):
    half = width // 2
    rates = jnp.exp(-math.log(10000.0) * (feature % half).astype(jnp.float32) / half)
    angles = steps.astype(jnp.float32)[:, None] * rates[None, :]
    wave = jnp.where(feature[None, :] < half, jnp.cos(angles), jnp.sin(angles))
    return wave.astype(jnp.bfloat16)


def gelu_value(hidden):
    return 0.5 * hidden * (1.0 + lax.erf(hidden * ROOT_HALF))


def gelu_slope(hidden):
    return (
        0.5 * (1.0 + lax.erf(hidden * ROOT_HALF))
        + hidden * jnp.exp(-0.5 * hidden * hidden) * SLOPE_NORM
    )


def matmul(left, right, dims=((1,), (0,))):
    return lax.dot_general(left, right, (dims, ((), ())), preferred_element_type=jnp.float32)


def expand_table(table):
    depth, heads = table.shape[:2]
    reverse = table.reshape(depth, heads, 2 * SIDE, 2 * SIDE)[:, :, ::-1, ::-1]
    wide = jnp.stack(
        [reverse[..., SIDE - 1 - c : 2 * SIDE - 1 - c] for c in range(SIDE)], axis=2
    )
    small = wide[:, :, :HALF, HALF : 3 * HALF, :HALF]
    return (
        wide.reshape(depth, heads, SIDE, 2 * SIDE * SIDE),
        small.reshape(depth, heads, HALF, 2 * HALF * HALF),
    )


def fold_table(wide, small):
    heads = wide.shape[0]
    total = wide.reshape(heads, SIDE, 2 * SIDE, SIDE)
    inner = small.reshape(heads, HALF, 2 * HALF, HALF)
    total = total + jnp.pad(inner, ((0, 0), (0, HALF), (HALF, HALF), (0, HALF)))
    reverse = functools.reduce(
        jnp.add,
        [
            jnp.pad(total[:, c], ((0, 0), (0, 0), (SIDE - 1 - c, 1 + c)))
            for c in range(SIDE)
        ],
    )
    return reverse[:, ::-1, ::-1].reshape(heads, 4 * SIDE * SIDE)


def fill_bias(small_row, wide_ref, small_ref, head, bias):
    span = SIDE * SIDE

    @pl.when(small_row == 0)
    def _():
        wide = wide_ref[head]
        for r in range(SIDE):
            at = SIDE * (SIDE - 1 - r)
            turned = wide if at == 0 else pltpu.roll(wide, 2 * span - at, 1)
            bias[r * SIDE : (r + 1) * SIDE, :] = turned[:, :span]

    @pl.when(small_row != 0)
    def _():
        small = small_ref[head]
        image = lax.broadcasted_iota(jnp.int32, (HALF, span), 1) // (HALF * HALF)
        lane = lax.broadcasted_iota(jnp.int32, small.shape, 1)
        for r in range(HALF):
            at = HALF * (HALF - 1 - r)
            turned = small if at == 0 else pltpu.roll(small, 2 * HALF * HALF - at, 1)
            turned = jnp.where(lane < HALF * HALF, turned, 0.0)
            pair = turned + pltpu.roll(turned, HALF * HALF, 1)
            line = jnp.concatenate([pair, pair], axis=1)
            for i in range(IMAGES):
                start = i * HALF * HALF + r * HALF
                bias[start : start + HALF, :] = jnp.where(image == i, line, MASKED)


def window_of(head, head_dim, width):
    first = head * head_dim // 128 * 128
    last = min(-(-(head + 1) * head_dim // 128) * 128, width)
    return first, last


def softmax_of(queries, keys, bias, scale):
    scores = matmul(queries, keys, ((1,), (1,))) * scale + bias[...]
    expo = jnp.exp(scores - jnp.max(scores, axis=-1, keepdims=True))
    return expo * (1.0 / jnp.sum(expo, axis=-1, keepdims=True))


def forward_kernel(heads, scale, flags, q_ref, k_ref, v_ref, wide_ref, small_ref, out_ref, bias, total):
    width = q_ref.shape[2]
    head_dim = width // heads
    total[...] = jnp.zeros_like(total)
    for head in range(heads):
        first, last = window_of(head, head_dim, width)
        lane = lax.broadcasted_iota(jnp.int32, (q_ref.shape[1], last - first), 1) + first
        mine = (lane >= head * head_dim) & (lane < (head + 1) * head_dim)
        fill_bias(flags[pl.program_id(0)], wide_ref, small_ref, head, bias)
        zero = jnp.zeros((), jnp.bfloat16)
        queries = jnp.where(mine, q_ref[0, :, first:last], zero)
        values = jnp.where(mine, v_ref[0, :, first:last], zero)
        weights = softmax_of(queries, k_ref[0, :, first:last], bias, scale)
        total[:, first:last] += matmul(weights.astype(jnp.bfloat16), values)
    out_ref[0] = total[...].astype(jnp.bfloat16)


def attend(flags, queries, keys, values, wide, small):
    rows, count, width = queries.shape
    heads = wide.shape[0]
    row = pl.BlockSpec((1, count, width), lambda r, f: (r, 0, 0))
    return pl.pallas_call(
        functools.partial(forward_kernel, heads, 1.0 / math.sqrt(width // heads)),
        grid_spec=pltpu.PrefetchScalarGridSpec(
            num_scalar_prefetch=1,
            grid=(rows,),
            in_specs=[
                row,
                row,
                row,
                pl.BlockSpec(wide.shape, lambda r, f: (0, 0, 0)),
                pl.BlockSpec(small.shape, lambda r, f: (0, 0, 0)),
            ],
            out_specs=row,
            scratch_shapes=[
                pltpu.VMEM((count, count), jnp.float32),
                pltpu.VMEM((count, width), jnp.float32),
            ],
        ),
        out_shape=jax.ShapeDtypeStruct(queries.shape, jnp.bfloat16),
        compiler_params=pltpu.CompilerParams(vmem_limit_bytes=32 << 20),
        cost_estimate=pl.CostEstimate(
            flops=rows * heads * count * count * 512,
            bytes_accessed=8 * rows * count * width,
            transcendentals=rows * heads * count * count,
        ),
        name="attend",
    )(flags, queries, keys, values, wide, small)


def backward_kernel(
    heads, scale, with_table, flags, q_ref, k_ref, v_ref, up_ref, wide_ref, small_ref, *rest
):
    outs, (bias, steps) = rest[:-2], rest[-2:]
    span = SIDE * SIDE
    width = q_ref.shape[2]
    head_dim = width // heads
    kind = flags[pl.program_id(0)]
    steps[...] = jnp.zeros_like(steps)
    if with_table:
        wide_out, small_out = outs[4:]

        @pl.when(pl.program_id(0) == 0)
        def _():
            wide_out[...] = jnp.zeros_like(wide_out)
            small_out[...] = jnp.zeros_like(small_out)

    for head in range(heads):
        first, last = window_of(head, head_dim, width)
        lane = lax.broadcasted_iota(jnp.int32, (q_ref.shape[1], last - first), 1) + first
        mine = (lane >= head * head_dim) & (lane < (head + 1) * head_dim)
        fill_bias(kind, wide_ref, small_ref, head, bias)
        zero = jnp.zeros((), jnp.bfloat16)
        queries, keys, values, upstream = (
            jnp.where(mine, ref[0, :, first:last], zero)
            for ref in (q_ref, k_ref, v_ref, up_ref)
        )
        weights = softmax_of(queries, keys, bias, scale)
        low = weights.astype(jnp.bfloat16)
        back_weights = matmul(upstream, values, ((1,), (1,)))
        inner = jnp.sum(weights * back_weights, axis=-1, keepdims=True)
        back_scores = (weights * (back_weights - inner)).astype(jnp.bfloat16)
        steps[0, :, first:last] += matmul(back_scores, keys) * scale
        steps[1, :, first:last] += matmul(back_scores, queries, ((0,), (0,))) * scale
        steps[2, :, first:last] += matmul(low, upstream, ((0,), (0,)))
        if with_table:
            steps[3, :, first:last] += matmul(low, values)
            bias[...] = back_scores.astype(jnp.float32)

            @pl.when(kind == 0)
            def _(head=head):
                total = wide_out[head]
                for r in range(SIDE):
                    part = bias[r * SIDE : (r + 1) * SIDE, :]
                    part = jnp.concatenate([part, jnp.zeros_like(part)], axis=1)
                    at = SIDE * (SIDE - 1 - r)
                    total = total + (part if at == 0 else pltpu.roll(part, at, 1))
                wide_out[head] = total

            @pl.when(kind != 0)
            def _(head=head):
                total = small_out[head]
                block = HALF * HALF
                lane = lax.broadcasted_iota(jnp.int32, total.shape, 1)
                for r in range(HALF):
                    part = functools.reduce(
                        jnp.add,
                        [
                            bias[i * block + r * HALF : i * block + (r + 1) * HALF, :]
                            for i in range(IMAGES)
                        ],
                    )
                    part = part[:, : span // 2] + part[:, span // 2 :]
                    part = jnp.where(lane < block, part + pltpu.roll(part, block, 1), 0.0)
                    at = HALF * (HALF - 1 - r)
                    total = total + (part if at == 0 else pltpu.roll(part, at, 1))
                small_out[head] = total

    for member in range(4 if with_table else 3):
        outs[member][0] = steps[member].astype(jnp.bfloat16)


def attend_back(flags, queries, keys, values, upstream, wide, small, with_table):
    rows, count, width = queries.shape
    heads = wide.shape[0]
    row = pl.BlockSpec((1, count, width), lambda r, f: (r, 0, 0))
    wide_spec = pl.BlockSpec(wide.shape, lambda r, f: (0, 0, 0))
    small_spec = pl.BlockSpec(small.shape, lambda r, f: (0, 0, 0))
    low = jax.ShapeDtypeStruct(queries.shape, jnp.bfloat16)
    members = 4 if with_table else 3
    tables = (
        [
            jax.ShapeDtypeStruct(wide.shape, jnp.float32),
            jax.ShapeDtypeStruct(small.shape, jnp.float32),
        ]
        if with_table
        else []
    )
    return pl.pallas_call(
        functools.partial(
            backward_kernel, heads, 1.0 / math.sqrt(width // heads), with_table
        ),
        grid_spec=pltpu.PrefetchScalarGridSpec(
            num_scalar_prefetch=1,
            grid=(rows,),
            in_specs=[row, row, row, row, wide_spec, small_spec],
            out_specs=[row] * members + ([wide_spec, small_spec] if with_table else []),
            scratch_shapes=[
                pltpu.VMEM((count, count), jnp.float32),
                pltpu.VMEM((4, count, width), jnp.float32),
            ],
        ),
        out_shape=[low] * members + tables,
        compiler_params=pltpu.CompilerParams(vmem_limit_bytes=32 << 20),
        cost_estimate=pl.CostEstimate(
            flops=rows * heads * count * count * 1536,
            bytes_accessed=16 * rows * count * width,
            transcendentals=rows * heads * count * count,
        ),
        name="attend_back",
    )(flags, queries, keys, values, upstream, wide, small)


def swap(value, axis):
    return lax.ppermute(value, axis, [(0, 1), (1, 0)])


def shift(value, line, by=1):
    return lax.ppermute(value, "line", [(i, (i + by) % line) for i in range(line)])


def add_tensor(partial):
    return partial + swap(partial, "tensor")


def narrow_kernel(own_ref, *refs):
    blocks, out_ref = refs[:-1], refs[-1]
    start = 0
    for ref in (own_ref, *blocks):
        out_ref[start : start + ref.shape[0], :] = ref[...].astype(jnp.bfloat16)
        start += ref.shape[0]


def narrow_line(blocks):
    width = blocks[0].shape[1]
    part = 384
    count = sum(block.shape[0] for block in blocks)
    return pl.pallas_call(
        narrow_kernel,
        grid=(width // part,),
        in_specs=[pl.BlockSpec((block.shape[0], part), lambda c: (0, c)) for block in blocks],
        out_specs=pl.BlockSpec((count, part), lambda c: (0, c)),
        out_shape=jax.ShapeDtypeStruct((count, width), jnp.bfloat16),
        compiler_params=pltpu.CompilerParams(vmem_limit_bytes=48 << 20),
        name="narrow_line",
    )(*blocks)


def narrow_plane_kernel(core, own_ref, remote_ref, other_ref, out_ref):
    half = remote_ref.shape[1]
    out_ref[0] = own_ref[...].astype(jnp.bfloat16)

    @pl.when(core[0] == 0)
    def _():
        out_ref[1:, :half] = remote_ref[...].astype(jnp.bfloat16)
        out_ref[1:, half:] = other_ref[...].astype(jnp.bfloat16)

    @pl.when(core[0] != 0)
    def _():
        out_ref[1:, :half] = other_ref[...].astype(jnp.bfloat16)
        out_ref[1:, half:] = remote_ref[...].astype(jnp.bfloat16)


def narrow_plane(own, remote, other):
    count, width = own.shape
    part = 384
    block = pl.BlockSpec((*remote.shape[:2], part), lambda c, core: (0, 0, c))
    return pl.pallas_call(
        narrow_plane_kernel,
        grid_spec=pltpu.PrefetchScalarGridSpec(
            num_scalar_prefetch=1,
            grid=(width // part,),
            in_specs=[pl.BlockSpec((count, part), lambda c, core: (0, c)), block, block],
            out_specs=pl.BlockSpec((4, count, part), lambda c, core: (0, 0, c)),
        ),
        out_shape=jax.ShapeDtypeStruct((4, count, width), jnp.bfloat16),
        compiler_params=pltpu.CompilerParams(vmem_limit_bytes=48 << 20),
        name="narrow_plane",
    )(lax.axis_index("tensor")[None].astype(jnp.int32), own, remote, other)


def half_rows(value):
    half = value.shape[0] // 2
    return lax.dynamic_slice_in_dim(value, lax.axis_index("tensor") * half, half, 0)


def gather_line(value, line):
    current = half_rows(value)
    blocks = []
    for _ in range(line - 1):
        current = shift(current, line)
        blocks += [current, swap(current, "tensor")]
    return narrow_line([value, *blocks])


def gather_plane(value):
    mine = half_rows(value)
    half = mine.shape[0] // 2
    across = swap(mine, "row")
    along = swap(mine, "col")
    corner = jnp.concatenate([swap(along[:half], "row"), swap(across[half:], "col")])
    remote = jnp.stack([across, along, corner])
    other = swap(remote, "tensor")
    return narrow_plane(value, remote, other)


def pick(value, index, axis=0):
    return lax.dynamic_index_in_dim(value, index, axis, keepdims=False)


def scatter_plane(value, axes):
    order, positions = axes
    for name, position in zip(order, positions, strict=True):
        place = lax.axis_index(name)
        value = pick(value, place, position) + swap(pick(value, 1 - place, position), name)
    return value


def scatter_line(value, line):
    place = lax.axis_index("line")
    total = pick(value, (place - 1) % line)
    for step in range(1, line):
        total = pick(value, (place - 1 - step) % line) + shift(total, line)
    return total


def exchange_line(value, line):
    place = lax.axis_index("line")
    slots = [pick(value, place)] + [
        shift(pick(value, (place + by) % line), line, by) for by in range(1, line)
    ]
    turned = jnp.stack([slots[-i % line] for i in range(line)] * 2)
    return lax.dynamic_slice_in_dim(turned, (line - place) % line, line, 0)


def exchange_plane(value):
    col, row = lax.axis_index("col"), lax.axis_index("row")
    place = 2 * col + row
    across = swap(pick(value, place ^ 1), "row")
    along = swap(pick(value, place ^ 2), "col")
    corner = lax.ppermute(
        pick(value, place ^ 3), ("col", "row"), [(0, 3), (3, 0), (1, 2), (2, 1)]
    )
    slots = [pick(value, place), across, along, corner]
    slots = [jnp.where(row == 0, slots[i], slots[i ^ 1]) for i in range(4)]
    return jnp.stack([jnp.where(col == 0, slots[i], slots[i ^ 2]) for i in range(4)])


def feed_gradients(normed, upstream, weight_in, weight_out, line):
    width, units = weight_in.shape
    own = units // line
    start = lax.axis_index("line") * own
    part_in = lax.dynamic_slice_in_dim(weight_in, start, own, 1)
    part_out = lax.dynamic_slice_in_dim(weight_out, start, own, 0)
    hidden = matmul(normed, part_in)
    activated = gelu_value(hidden).astype(jnp.bfloat16)
    back = matmul(upstream, part_out, ((1,), (1,)))
    back_hidden = (back * gelu_slope(hidden)).astype(jnp.bfloat16)
    outer = matmul(activated, upstream, ((0,), (0,)))
    inner = matmul(normed, back_hidden, ((0,), (0,)))
    outer = scatter_plane(outer.reshape(2, 2, own // 4, width), (("col", "row"), (0, 0)))
    inner = inner.reshape(line, 2, 2, width // (4 * line), own)
    inner = scatter_plane(inner, (("row", "col"), (2, 1)))
    inner = exchange_line(inner, line)
    return jnp.moveaxis(inner, 0, 1).reshape(width // (4 * line), units), outer


def place_images(per_image, small_row, count):
    first = jnp.where(small_row[..., None, None] != 0, per_image, per_image[..., :1, :])
    return jnp.repeat(first, count // IMAGES, axis=-2)


def attention_gradients(
    normed, upstream, embedded, kinds, token_weight, time_weight, out_weight, wide, small, line
):
    slots, count, width = normed.shape
    local = token_weight.shape[2]
    heads = wide.shape[0]
    own, own_heads = local // slots, heads // slots
    place = 2 * lax.axis_index("col") + lax.axis_index("row")
    start = place * own
    part = lax.dynamic_slice_in_dim(token_weight, start, own, 2)
    part_time = lax.dynamic_slice_in_dim(time_weight, start, own, 2)
    part_out = lax.dynamic_slice_in_dim(out_weight, start, own, 0)
    part_wide = lax.dynamic_slice_in_dim(wide, place * own_heads, own_heads, 0)
    part_small = lax.dynamic_slice_in_dim(small, place * own_heads, own_heads, 0)
    flat = normed.reshape(slots * count, width)
    flat_up = upstream.reshape(slots * count, width)
    per_image = [
        matmul(embedded, part_time[member]).reshape(slots, IMAGES, own) for member in range(2)
    ]
    per_token = [place_images(member, kinds, count) for member in per_image]
    queries, keys, values = (
        matmul(flat, part[member]).reshape(slots, count, own) for member in range(3)
    )
    back_attended = matmul(flat_up, part_out, ((1,), (1,))).astype(jnp.bfloat16)
    back_queries, back_keys, back_values, attended, back_wide, back_small = attend_back(
        kinds,
        (queries + per_token[0]).astype(jnp.bfloat16),
        keys.astype(jnp.bfloat16),
        (values + per_token[1]).astype(jnp.bfloat16),
        back_attended.reshape(slots, count, own),
        part_wide,
        part_small,
        True,
    )
    projection = matmul(attended.reshape(slots * count, own), flat_up, ((0,), (0,)))
    projection = scatter_line(projection.reshape(line, own // line, width), line)
    projection = lax.ppermute(
        projection,
        LINES,
        [(slots * z + j, line * j + z) for z in range(line) for j in range(slots)],
    )
    token = jnp.stack(
        [
            matmul(flat, member.reshape(slots * count, own), ((0,), (0,)))
            for member in (back_queries, back_keys, back_values)
        ]
    )
    token = token.reshape(3, line, width // line, own)
    token = scatter_line(jnp.moveaxis(token, 1, 0), line)
    token = token.reshape(3, slots, width // (slots * line), own)
    token = exchange_plane(jnp.moveaxis(token, 1, 0))
    token = jnp.moveaxis(token, 0, 2).reshape(3, width // (slots * line), local)
    table = fold_table(back_wide, back_small)
    whole = jnp.zeros((heads, table.shape[1]), jnp.float32)
    whole = lax.dynamic_update_slice_in_dim(whole, table, place * own_heads, 0)
    return token, projection, whole


def local(
    tokens,
    segment_ids,
    timesteps,
    norm_gain,
    norm_bias,
    token_proj,
    time_proj,
    bias_table,
    out_proj,
    hidden_in,
    hidden_out,
    branch_bias,
    cotangent,
    *,
    line,
):
    count, width = tokens.shape
    local_width = token_proj.shape[3]
    depth = token_proj.shape[0]
    heads = bias_table.shape[1]
    n_dp = 4 * line
    line_at = lax.axis_index("line")
    place = 2 * lax.axis_index("col") + lax.axis_index("row")
    kind = segment_ids[-1:]
    info = lax.all_gather(jnp.concatenate([timesteps[0], kind]), LINES)
    near = lax.dynamic_slice_in_dim(info, 4 * line_at, 4, 0)
    slot_of = place ^ jnp.arange(4, dtype=jnp.int32)
    chosen = slot_of[:, None] == jnp.arange(4, dtype=jnp.int32)[None, :]
    near = jnp.sum(jnp.where(chosen[:, :, None], near[None], 0), axis=1)
    kinds = near[:, IMAGES]
    features = jnp.arange(width, dtype=jnp.int32)
    embedded_own = sinusoid(timesteps[0], features, width)
    embedded_near = sinusoid(near[:, :IMAGES].reshape(-1), features, width)
    own_features = width // n_dp
    embedded_all = sinusoid(
        info[:, :IMAGES].reshape(-1),
        (4 * line_at + place) * own_features + jnp.arange(own_features, dtype=jnp.int32),
        width,
    )
    wide, small = expand_table(bias_table)

    stream = tokens.astype(jnp.float32)
    saved = []
    cotangent_full = cotangent.astype(jnp.float32)
    gathered_up = gather_line(cotangent_full, line)
    for layer in range(depth):
        normed, normal_first, inverse_first = layer_norm(
            stream, norm_gain[layer, 0], norm_bias[layer, 0]
        )
        near_first = gather_plane(normed)
        normed_first = normed.astype(jnp.bfloat16)
        per_token = [
            place_images(matmul(embedded_own, time_proj[layer, member]), kind[0], count)
            for member in range(2)
        ]
        queries = (matmul(normed_first, token_proj[layer, 0]) + per_token[0]).astype(jnp.bfloat16)
        keys = matmul(normed_first, token_proj[layer, 1]).astype(jnp.bfloat16)
        values = (matmul(normed_first, token_proj[layer, 2]) + per_token[1]).astype(jnp.bfloat16)
        attended = attend(kind, queries[None], keys[None], values[None], wide[layer], small[layer])
        partial = matmul(attended[0], out_proj[layer])
        middle = stream + add_tensor(partial) + branch_bias[layer, 0]
        normed, normal_second, inverse_second = layer_norm(
            middle, norm_gain[layer, 1], norm_bias[layer, 1]
        )
        line_second = gather_line(normed, line)
        normed_second = normed.astype(jnp.bfloat16)
        hidden = matmul(normed_second, hidden_in[layer])
        activated = gelu_value(hidden).astype(jnp.bfloat16)
        partial = matmul(activated, hidden_out[layer])
        stream = middle + add_tensor(partial) + branch_bias[layer, 1]
        saved.append(
            (
                near_first,
                normal_first,
                inverse_first,
                queries,
                keys,
                values,
                normal_second,
                inverse_second,
                line_second,
                hidden,
            )
        )
    output = stream.astype(jnp.bfloat16)
    upstream = cotangent_full
    collected = [None] * depth
    for layer in reversed(range(depth)):
        (
            near_first,
            normal_first,
            inverse_first,
            queries,
            keys,
            values,
            normal_second,
            inverse_second,
            line_second,
            hidden,
        ) = saved[layer]
        back_feed = upstream.astype(jnp.bfloat16)
        feed_bias = jnp.sum(back_feed.astype(jnp.float32), axis=0)
        if layer < depth - 1:
            gathered_up = gather_line(upstream, line)
        inner_weight, outer_weight = feed_gradients(
            line_second, gathered_up, hidden_in[layer], hidden_out[layer], line
        )
        back_active = matmul(back_feed, hidden_out[layer], ((1,), (1,)))
        back_hidden = (back_active * gelu_slope(hidden)).astype(jnp.bfloat16)
        back_second = add_tensor(matmul(back_hidden, hidden_in[layer], ((1,), (1,))))
        norm_part, gain_second, shift_second = norm_backward(
            normal_second, inverse_second, norm_gain[layer, 1], back_second
        )
        back_middle = upstream + norm_part
        near_branch = gather_plane(back_middle)
        back_branch = back_middle.astype(jnp.bfloat16)
        attention_bias = jnp.sum(back_branch.astype(jnp.float32), axis=0)
        back_attended = matmul(back_branch, out_proj[layer], ((1,), (1,))).astype(jnp.bfloat16)
        back_projected = attend_back(
            kind,
            queries[None],
            keys[None],
            values[None],
            back_attended[None],
            wide[layer],
            small[layer],
            False,
        )
        back_projected = [member[0] for member in back_projected]
        back_first = functools.reduce(
            jnp.add,
            [
                matmul(back_projected[member], token_proj[layer, member], ((1,), (1,)))
                for member in range(3)
            ],
        )
        back_first = add_tensor(back_first)
        norm_part, gain_first, shift_first = norm_backward(
            normal_first, inverse_first, norm_gain[layer, 0], back_first
        )
        upstream = back_middle + norm_part
        token_weight, projection_weight, table = attention_gradients(
            near_first,
            near_branch,
            embedded_near,
            kinds,
            token_proj[layer],
            time_proj[layer],
            out_proj[layer],
            wide[layer],
            small[layer],
            line,
        )
        per_image = jnp.stack([back_projected[0], back_projected[2]]).astype(jnp.float32)
        per_image = jnp.sum(per_image.reshape(2, IMAGES, count // IMAGES, local_width), axis=2)
        first_image = (jnp.arange(IMAGES, dtype=jnp.int32) == 0)[None, :, None]
        per_image = jnp.where(
            kind[0] != 0,
            per_image,
            jnp.where(first_image, jnp.sum(per_image, axis=1, keepdims=True), 0.0),
        )
        per_image = lax.all_gather(per_image, LINES)
        time_weight = jnp.einsum(
            "rsd,rjse->jde",
            embedded_all.astype(jnp.float32).reshape(n_dp, IMAGES, own_features),
            per_image,
            precision=lax.Precision.HIGHEST,
        )
        pieces = [
            jnp.stack([gain_first, gain_second, shift_first, shift_second, attention_bias, feed_bias]),
            table,
        ]
        pieces = [
            jnp.moveaxis(piece.reshape(piece.shape[0], n_dp, -1), 1, 0).reshape(n_dp, -1)
            for piece in pieces
        ]
        pieces = lax.psum_scatter(
            jnp.concatenate(pieces, axis=1), LINES, scatter_dimension=0, tiled=True
        )[0]
        vectors = pieces[: 6 * own_features].reshape(3, 2, own_features)
        table = pieces[6 * own_features :].reshape(heads, -1)
        collected[layer] = (
            vectors[0],
            vectors[1],
            token_weight,
            time_weight,
            table,
            projection_weight,
            inner_weight,
            outer_weight,
            vectors[2],
        )
    stacked = [jnp.stack([terms[member] for terms in collected]) for member in range(9)]
    return (output, upstream.astype(jnp.bfloat16), *stacked)


def solution(mesh):
    line = mesh.shape["dp"] // 4
    fine = Mesh(
        mesh.devices.reshape(line, 2, 2, mesh.shape["tensor"]), (*LINES, "tensor")
    )
    return jax.shard_map(
        functools.partial(local, line=line),
        mesh=fine,
        in_specs=(
            P(LINES, None),
            P(LINES),
            P(LINES, None),
            P(),
            P(),
            P(None, None, None, "tensor"),
            P(None, None, None, "tensor"),
            P(None, "tensor", None),
            P(None, "tensor", None),
            P(None, None, "tensor"),
            P(None, "tensor", None),
            P(),
            P(LINES, None),
        ),
        out_specs=(
            P(LINES, None),
            P(LINES, None),
            P(None, None, LINES),
            P(None, None, LINES),
            P(None, None, LINES, "tensor"),
            P(None, None, LINES, "tensor"),
            P(None, "tensor", LINES),
            P(None, ("tensor", *LINES), None),
            P(None, LINES, "tensor"),
            P(None, ("tensor", *LINES), None),
            P(None, None, LINES),
        ),
        check_vma=False,
    )
```

```python
import functools
import math

import jax
import jax.numpy as jnp
from jax import lax
from jax.experimental import pallas as pl
from jax.experimental.pallas import tpu as pltpu
from jax.sharding import Mesh
from jax.sharding import PartitionSpec as P

SIDE = 16
HALF = 8
SPAN = SIDE * SIDE
IMAGES = 4
BLOCK = SPAN // IMAGES
GROUP = 4
EPSILON = 1e-06
MASKED = -1e30
ROOT_HALF = 0.7071067811865476
SLOPE_NORM = 0.3989422804014327
LINES = ("line", "col", "row")
LOW = jnp.bfloat16
FULL = jnp.float32
KIND, AT_LINE, AT_COL, AT_ROW, AT_CORE = range(5)


def matmul(left, right, dims=((1,), (0,))):
    return lax.dot_general(left, right, (dims, ((), ())), preferred_element_type=FULL)


NT = ((1,), (1,))
TN = ((0,), (0,))


def normal_of(stream):
    center = stream - jnp.mean(stream, axis=-1, keepdims=True)
    inverse = lax.rsqrt(jnp.mean(center * center, axis=-1, keepdims=True) + EPSILON)
    return center * inverse, inverse


def norm_backward(stream, gain, upstream):
    normal, inverse = normal_of(stream)
    gain_part = jnp.sum(upstream * normal, axis=0, keepdims=True)
    shift_part = jnp.sum(upstream, axis=0, keepdims=True)
    scaled = upstream * gain
    inner = (
        scaled
        - jnp.mean(scaled, axis=-1, keepdims=True)
        - normal * jnp.mean(scaled * normal, axis=-1, keepdims=True)
    )
    return inner * inverse, gain_part, shift_part


def sinusoid(steps, feature, width):
    half = width // 2
    rates = jnp.exp(-math.log(10000.0) * (feature % half).astype(FULL) / half)
    angles = steps.astype(FULL)[:, None] * rates[None, :]
    wave = jnp.where(feature[None, :] < half, jnp.cos(angles), jnp.sin(angles))
    return wave.astype(LOW)


def whole(shape):
    return pl.BlockSpec(shape, lambda *_: (0,) * len(shape))


def whole_once(shape):
    return pl.BlockSpec(shape, lambda *_: (0,) * len(shape), pipeline_mode=pl.Buffered(1))


def call(kernel, name, grid, in_specs, out_specs, out_shape, scratch, flops, size, scalars=1, after=()):
    first = scalars + len(in_specs)

    def body(*refs):
        kernel(*refs[:first], *refs[first + len(after) :])

    made = pl.pallas_call(
        body,
        grid_spec=pltpu.PrefetchScalarGridSpec(
            num_scalar_prefetch=scalars,
            grid=grid,
            in_specs=[*in_specs, *[pl.BlockSpec(memory_space=pl.ANY)] * len(after)],
            out_specs=out_specs,
            scratch_shapes=scratch,
        ),
        out_shape=[pltpu.HBM(out.shape, out.dtype) for out in out_shape],
        compiler_params=pltpu.CompilerParams(vmem_limit_bytes=40 << 20),
        cost_estimate=pl.CostEstimate(
            flops=int(flops), bytes_accessed=int(size), transcendentals=0
        ),
        name=name,
    )
    return lambda *operands: made(*operands, *map(in_hbm, after))


def shape_of(shape, kind=FULL):
    return jax.ShapeDtypeStruct(shape, kind)


def regroup(value, pieces):
    lane = lax.broadcasted_iota(jnp.int32, (value.shape[0], 128), 1)
    total = jnp.zeros((value.shape[0], 128), FULL)
    for tile, source, place, lanes in pieces:
        part = value[:, tile * 128 : tile * 128 + 128]
        turn = (place - source) % 128
        part = part if turn == 0 else pltpu.roll(part, turn, 1)
        total = jnp.where((lane >= place) & (lane < place + lanes), part, total)
    return total


def expand_kernel(table_ref, wide_ref, small_ref):
    size = table_ref.shape[1]
    table = table_ref[...]
    for c in range(SIDE):
        turned = pltpu.roll(table, size - SIDE + c, 1)
        wide = jnp.concatenate(
            [
                regroup(
                    turned,
                    [(2 * o + p // 4, 32 * (p % 4), 16 * p, 16) for p in range(8)],
                )
                for o in range(4)
            ],
            axis=1,
        )
        wide_ref[:, c, :] = wide
        if c < HALF:
            small_ref[:, c, :] = regroup(
                wide, [(1 + k // 8, 16 * (k % 8), 8 * k, 8) for k in range(16)]
            )


def expand_table(table):
    rows, size = table.shape
    return pl.pallas_call(
        expand_kernel,
        out_shape=[shape_of((rows, SIDE, size // 2)), shape_of((rows, HALF, size // 8))],
        name="expand_table",
    )(table)


def fold_table(wide, small):
    inner = jnp.concatenate([small, jnp.zeros_like(small)], axis=0)
    tiles = [wide[:, 128 * t : 128 * t + 128] for t in range(4)]
    for t in range(2):
        tiles[1 + t] = tiles[1 + t] + regroup(
            inner, [(0, 8 * (8 * t + q), 16 * q, 8) for q in range(8)]
        )
    wide = jnp.concatenate(tiles, axis=1)
    spread = jnp.concatenate(
        [
            regroup(
                wide,
                [(o // 2, 64 * (o % 2) + 16 * q, 32 * q, 16) for q in range(4)],
            )
            for o in range(8)
        ],
        axis=1,
    )
    return functools.reduce(
        jnp.add, [pltpu.roll(spread[c : c + 1], SIDE - c, 1) for c in range(SIDE)]
    )


def fill_bias(heads, kind, wide_ref, small_ref, bias):
    @pl.when(kind == 0)
    def _():
        for head in range(heads):
            wide = wide_ref[head]
            for r in range(SIDE):
                turned = pltpu.roll(wide, 2 * SPAN - SIDE * (SIDE - r), 1)
                bias[head, r * SIDE : (r + 1) * SIDE, :] = turned[:, :SPAN]

    @pl.when(kind != 0)
    def _():
        image = lax.broadcasted_iota(jnp.int32, (HALF, SPAN), 1) // BLOCK
        lane = lax.broadcasted_iota(jnp.int32, (HALF, 2 * BLOCK), 1)
        for head in range(heads):
            small = small_ref[head]
            for r in range(HALF):
                turned = pltpu.roll(small, 2 * BLOCK - HALF * (HALF - r), 1)
                turned = jnp.where(lane < BLOCK, turned, 0.0)
                pair = turned + pltpu.roll(turned, BLOCK, 1)
                line = jnp.concatenate([pair, pair], axis=1)
                for i in range(IMAGES):
                    start = i * BLOCK + r * HALF
                    bias[head, start : start + HALF, :] = jnp.where(image == i, line, MASKED)


def collect_table(heads, kind, back, wide_sum, small_sum):
    @pl.when(kind == 0)
    def _():
        for head in range(heads):
            total = wide_sum[head]
            for r in range(SIDE):
                part = back[head, r * SIDE : (r + 1) * SIDE, :]
                part = jnp.concatenate([part, jnp.zeros_like(part)], axis=1)
                total = total + pltpu.roll(part, SIDE * (SIDE - r), 1)
            wide_sum[head] = total

    @pl.when(kind != 0)
    def _():
        for head in range(heads):
            total = small_sum[head]
            lane = lax.broadcasted_iota(jnp.int32, total.shape, 1)
            for r in range(HALF):
                part = functools.reduce(
                    jnp.add,
                    [
                        back[head, i * BLOCK + r * HALF : i * BLOCK + (r + 1) * HALF, :]
                        for i in range(IMAGES)
                    ],
                )
                part = part[:, : SPAN // 2] + part[:, SPAN // 2 :]
                part = jnp.where(lane < BLOCK, part + pltpu.roll(part, BLOCK, 1), 0.0)
                total = total + pltpu.roll(part, HALF * (HALF - r), 1)
            small_sum[head] = total


def window_of(head, head_dim, width):
    if width <= 256:
        return 0, width
    return head * head_dim // 128 * 128, min(-(-(head + 1) * head_dim // 128) * 128, width)


def mine_of(head, head_dim, first, last, rows):
    lane = lax.broadcasted_iota(jnp.int32, (rows, last - first), 1) + first
    return (lane >= head * head_dim) & (lane < (head + 1) * head_dim)


def softmax_of(queries, keys, bias, scale):
    scores = matmul(keys, queries, NT) * scale + bias
    expo = jnp.exp(scores - jnp.max(scores, axis=0, keepdims=True))
    return expo * (1.0 / jnp.sum(expo, axis=0, keepdims=True))


def attention_forward(heads, row, bias, total):
    count, width = total.shape
    head_dim = width // heads
    scale = 1.0 / math.sqrt(head_dim)
    zero = jnp.zeros((), LOW)
    total[...] = jnp.zeros_like(total)
    for head in range(heads):
        first, last = window_of(head, head_dim, width)
        mine = mine_of(head, head_dim, first, last, count)
        queries = jnp.where(mine, row(0, first, last), zero)
        values = jnp.where(mine, row(2, first, last), zero)
        weights = softmax_of(queries, row(1, first, last), bias[head], scale)
        total[:, first:last] += matmul(weights.astype(LOW), values, TN)


def attention_backward(heads, row, bias, steps, attended, scores_out):
    count, width = steps.shape[1:]
    head_dim = width // heads
    scale = 1.0 / math.sqrt(head_dim)
    zero = jnp.zeros((), LOW)
    steps[...] = jnp.zeros_like(steps)
    if attended is not None:
        attended[...] = jnp.zeros_like(attended)
    for head in range(heads):
        first, last = window_of(head, head_dim, width)
        mine = mine_of(head, head_dim, first, last, count)
        queries, keys, values, upstream = (
            jnp.where(mine, row(member, first, last), zero) for member in range(4)
        )
        weights = softmax_of(queries, keys, bias[head], scale)
        low = weights.astype(LOW)
        back_weights = matmul(values, upstream, NT)
        inner = jnp.sum(weights * back_weights, axis=0, keepdims=True)
        back_scores = (weights * (back_weights - inner)).astype(LOW)
        steps[0, :, first:last] += matmul(back_scores, keys, TN) * scale
        steps[1, :, first:last] += matmul(back_scores, queries) * scale
        steps[2, :, first:last] += matmul(low, upstream)
        if attended is not None:
            attended[:, first:last] += matmul(low, values, TN)
        if scores_out is not None:
            scores_out[head] = back_scores.astype(FULL)


def in_hbm(value):
    return pltpu.with_memory_space_constraint(value, pltpu.HBM)


HBM = pl.BlockSpec(memory_space=pltpu.HBM)
NEAR = pl.BlockSpec(memory_space=pltpu.VMEM)


def plain(kernel, name, scalars, near, far, outs, scratch, flops, size, limit, after=()):
    first = len(scalars) + len(near) + len(far)

    def body(*refs):
        kernel(*refs[:first], *refs[first + len(after) :])

    return pl.pallas_call(
        body,
        in_specs=[
            *[pl.BlockSpec(memory_space=pltpu.SMEM)] * len(scalars),
            *[NEAR] * len(near),
            *[HBM] * (len(far) + len(after)),
        ],
        out_specs=[HBM] * len(outs),
        out_shape=[pltpu.HBM(out.shape, out.dtype) for out in outs],
        scratch_shapes=[*scratch, pltpu.SemaphoreType.DMA((24,))],
        compiler_params=pltpu.CompilerParams(vmem_limit_bytes=limit << 20),
        cost_estimate=pl.CostEstimate(
            flops=int(flops), bytes_accessed=int(size), transcendentals=0
        ),
        name=name,
    )(*scalars, *near, *map(in_hbm, (*far, *after)))


def gate(values):
    def body(*refs):
        del refs

    return pl.pallas_call(
        body,
        in_specs=[HBM] * len(values),
        out_specs=[HBM] * len(values),
        out_shape=[pltpu.HBM(value.shape, value.dtype) for value in values],
        input_output_aliases={i: i for i in range(len(values))},
        name="gate",
    )(*map(in_hbm, values))


class Moves:
    def __init__(self):
        self.running, self.found = [], {}

    def start(self, name, steps):
        self.running.append((name, steps, next(steps)))

    def kernel(self, output, due=()):
        arrived = [array for _, _, arrays in self.running for array in arrays]
        held = gate([output, *due, *arrived])
        self.step(iter(held[1 + len(due) :]))
        return held[: 1 + len(due)]

    def step(self, arrived=None):
        before, self.running = self.running, []
        for name, steps, arrays in before:
            if arrived is not None:
                arrays = [next(arrived) for _ in arrays]
            try:
                self.running.append((name, steps, steps.send(arrays)))
            except StopIteration as stop:
                self.found[name] = stop.value

    def finish(self):
        while self.running:
            self.step()


class Copies:
    def __init__(self, sems):
        self.sems, self.count, self.leaving = sems, 0, []

    def start(self, source, target):
        copy = pltpu.make_async_copy(source, target, self.sems.at[self.count])
        self.count += 1
        copy.start()
        return copy

    def leave(self, source, target):
        self.leaving.append(self.start(source, target))

    def finish(self):
        for copy in self.leaving:
            copy.wait()


def core_half(ref, ids):
    half = ref.shape[0] // 2
    return ref.at[pl.ds(pl.multiple_of(ids[AT_CORE] * half, half), half)]


def attend_kernel(layer, heads, ids, gain_ref, shift_ref, biases_ref, *refs):
    parts = 1 if layer == 0 else 3
    stream_hbm, refs = refs[:parts], refs[parts:]
    token_hbm, out_hbm, image_hbm, wide_hbm, small_hbm = refs[:5]
    stream_out, normed_out, half_out, row_out, partial_out, bias_out = refs[5:11]
    stream_in, token, outer, image, wide, small, normed, low, rows, bias, total, partial, sems = refs[11:]
    copies = Copies(sems)
    per = pl.ds(layer * heads, heads)
    near = [copies.start(source, stream_in.at[i]) for i, source in enumerate(stream_hbm)]
    tables = [copies.start(wide_hbm.at[per], wide), copies.start(small_hbm.at[per], small)]
    tokens = [copies.start(token_hbm.at[layer, 0], token.at[0])]
    images = copies.start(image_hbm.at[layer], image)
    tokens += [copies.start(token_hbm.at[layer, m], token.at[m]) for m in (1, 2)]
    outers = copies.start(out_hbm.at[layer], outer)
    kind = ids[KIND]
    count = low.shape[0]
    for copy in near:
        copy.wait()
    if layer == 0:
        stream = stream_in[0].astype(FULL)
    else:
        stream = stream_in[0] + (stream_in[1] + stream_in[2]) + biases_ref[layer - 1, 1:2, :]
    normed[...] = normal_of(stream)[0] * gain_ref[layer, 0:1, :] + shift_ref[layer, 0:1, :]
    if layer == 0:
        partial[...] = stream
        copies.leave(partial, stream_out)
    else:
        stream_in[0] = stream
        copies.leave(stream_in.at[0], stream_out)
    copies.leave(normed, normed_out)
    copies.leave(core_half(normed, ids), half_out)
    low[...] = normed[...].astype(LOW)
    for copy in tables:
        copy.wait()
    fill_bias(heads, kind, wide, small, bias)
    copies.leave(bias, bias_out)
    for member in range(3):
        tokens[member].wait()
        projected = matmul(low[...], token[member], NT)
        if member == 0:
            images.wait()
        if member == 1:
            rows[member] = projected.astype(LOW)
            continue
        for i in range(IMAGES):
            mine = image[member // 2, i : i + 1, :]
            mine = jnp.where(kind != 0, mine, image[member // 2, 0:1, :])
            here = slice(i * (count // IMAGES), (i + 1) * (count // IMAGES))
            rows[member, here, :] = (projected[here] + mine).astype(LOW)
    copies.leave(rows, row_out)

    def row(index, first, last):
        return rows[index, :, first:last]

    attention_forward(heads, row, bias, total)
    outers.wait()
    if layer == 0:
        copies.leaving.pop(0).wait()
    partial[...] = matmul(total[...].astype(LOW), outer[...])
    copies.leave(partial, partial_out)
    copies.finish()


def attend(layer, ids, stream, gains, shifts, biases, token_rows, per_image, out_proj, wide, small, after=()):
    count, width = stream[0].shape
    depth, _, local, _ = token_rows.shape
    heads = wide.shape[0] // depth
    full = shape_of((count, width))
    outs = [
        full,
        full,
        shape_of((count // 2, width)),
        shape_of((3, count, local), LOW),
        full,
        shape_of((heads, count, count)),
    ]
    return plain(
        functools.partial(attend_kernel, layer, heads),
        f"attend_{layer}",
        (ids,),
        (gains, shifts, biases),
        (*stream, token_rows, out_proj, per_image, wide, small),
        outs,
        [
            pltpu.VMEM((len(stream), count, width), stream[0].dtype),
            pltpu.VMEM((3, local, width), LOW),
            pltpu.VMEM((local, width), LOW),
            pltpu.VMEM(per_image.shape[1:], FULL),
            pltpu.VMEM((heads, *wide.shape[1:]), FULL),
            pltpu.VMEM((heads, *small.shape[1:]), FULL),
            pltpu.VMEM((count, width), FULL),
            pltpu.VMEM((count, width), LOW),
            pltpu.VMEM((3, count, local), LOW),
            pltpu.VMEM((heads, count, count), FULL),
            pltpu.VMEM((count, local), FULL),
            pltpu.VMEM((count, width), FULL),
        ],
        2 * count * width * local * 4 + heads * count * count * 2048,
        8 * width * local + 16 * count * width,
        40,
        after,
    )


CHUNK = 768


def feed_kernel(layer, ids, gain_ref, shift_ref, biases_ref, stream_hbm, part_hbm, other_hbm, in_hbm_ref, out_hbm_ref, middle_out, half_out, slope_out, partial_out, stream_in, inner, outer, normed, low, slope, partial, sems):
    units = inner.shape[1]
    chunks = [slice(at, at + CHUNK) for at in range(0, units, CHUNK)]
    copies = Copies(sems)
    near = [
        copies.start(source, stream_in.at[i])
        for i, source in enumerate((stream_hbm, part_hbm, other_hbm))
    ]
    weights = [
        (
            copies.start(in_hbm_ref.at[layer, :, chunk], inner.at[:, chunk]),
            copies.start(out_hbm_ref.at[layer, chunk, :], outer.at[chunk, :]),
        )
        for chunk in chunks
    ]
    for copy in near:
        copy.wait()
    middle = stream_in[0] + (stream_in[1] + stream_in[2]) + biases_ref[layer, 0:1, :]
    stream_in[0] = middle
    copies.leave(stream_in.at[0], middle_out)
    normed[...] = normal_of(middle)[0] * gain_ref[layer, 1:2, :] + shift_ref[layer, 1:2, :]
    copies.leave(core_half(normed, ids), half_out)
    low[...] = normed[...].astype(LOW)
    for at, chunk in enumerate(chunks):
        weights[at][0].wait()
        hidden = matmul(low[...], inner[:, chunk])
        rise = 0.5 * (1.0 + lax.erf(hidden * ROOT_HALF))
        slope[:, chunk] = rise + hidden * jnp.exp(-0.5 * hidden * hidden) * SLOPE_NORM
        copies.leave(slope.at[:, chunk], slope_out.at[:, chunk])
        weights[at][1].wait()
        product = matmul((hidden * rise).astype(LOW), outer[chunk, :])
        partial[...] = product if at == 0 else partial[...] + product
    copies.leave(partial, partial_out)
    copies.finish()


def feed(layer, ids, stream, partial, other, biases, gains, shifts, hidden_in, hidden_out, after=()):
    count, width = stream.shape
    units = hidden_in.shape[2]
    full = shape_of((count, width))
    return plain(
        functools.partial(feed_kernel, layer),
        f"feed_{layer}",
        (ids,),
        (gains, shifts, biases),
        (stream, partial, other, hidden_in, hidden_out),
        [full, shape_of((count // 2, width)), shape_of((count, units)), full],
        [
            pltpu.VMEM((3, count, width), FULL),
            pltpu.VMEM((width, units), LOW),
            pltpu.VMEM((units, width), LOW),
            pltpu.VMEM((count, width), FULL),
            pltpu.VMEM((count, width), LOW),
            pltpu.VMEM((count, units), FULL),
            pltpu.VMEM((count, width), FULL),
        ],
        4 * count * width * units,
        4 * width * units + 4 * count * (units + 6 * width),
        48,
        after,
    )


def feed_back_kernel(layer, last, ids, gain_ref, *refs):
    parts = 1 if last else 4
    up_hbm, refs = refs[:parts], refs[parts:]
    slope_hbm, in_hbm_ref, out_hbm_ref, upstream_out, half_out, sums_out, partial_out = refs[:7]
    up_in, inner, outer, upstream, low, slope, sums, partial, sems = refs[7:]
    units = inner.shape[1]
    chunks = [slice(at, at + CHUNK) for at in range(0, units, CHUNK)]
    copies = Copies(sems)
    near = [copies.start(source, up_in.at[i]) for i, source in enumerate(up_hbm)]
    weights = [
        (
            copies.start(out_hbm_ref.at[layer, chunk, :], outer.at[chunk, :]),
            copies.start(slope_hbm.at[:, chunk], slope.at[:, chunk]),
            copies.start(in_hbm_ref.at[layer, :, chunk], inner.at[:, chunk]),
        )
        for chunk in chunks
    ]
    for copy in near:
        copy.wait()
    sums[...] = jnp.zeros_like(sums)
    if last:
        upstream[...] = up_in[0].astype(FULL)
    else:
        step, gain_part, shift_part = norm_backward(
            up_in[3], gain_ref[layer + 1, 0:1, :], up_in[1] + up_in[2]
        )
        upstream[...] = up_in[0] + step
        sums[1:2, :] = gain_part
        sums[2:3, :] = shift_part
    copies.leave(upstream, upstream_out)
    copies.leave(core_half(upstream, ids), half_out)
    low[...] = upstream[...].astype(LOW)
    sums[0:1, :] = jnp.sum(low[...].astype(FULL), axis=0, keepdims=True)
    copies.leave(sums, sums_out)
    for at, chunk in enumerate(chunks):
        weights[at][0].wait()
        back = matmul(low[...], outer[chunk, :], NT)
        weights[at][1].wait()
        weights[at][2].wait()
        product = matmul((back * slope[:, chunk]).astype(LOW), inner[:, chunk], NT)
        partial[...] = product if at == 0 else partial[...] + product
    copies.leave(partial, partial_out)
    copies.finish()


def feed_back(layer, ids, upstream, slope, hidden_in, hidden_out, gains, after=()):
    count, width = upstream[0].shape
    units = hidden_in.shape[2]
    full = shape_of((count, width))
    return plain(
        functools.partial(feed_back_kernel, layer, len(upstream) == 1),
        f"feed_back_{layer}",
        (ids,),
        (gains,),
        (*upstream, slope, hidden_in, hidden_out),
        [full, shape_of((count // 2, width)), shape_of((8, width)), full],
        [
            pltpu.VMEM((len(upstream), count, width), upstream[0].dtype),
            pltpu.VMEM((width, units), LOW),
            pltpu.VMEM((units, width), LOW),
            pltpu.VMEM((count, width), FULL),
            pltpu.VMEM((count, width), LOW),
            pltpu.VMEM((count, units), FULL),
            pltpu.VMEM((8, width), FULL),
            pltpu.VMEM((count, width), FULL),
        ],
        4 * count * width * units,
        4 * width * units + 4 * count * (units + 6 * width),
        48,
        after,
    )


def attend_back_kernel(layer, heads, ids, gain_ref, up_hbm, part_hbm, other_hbm, middle_hbm, row_hbm, bias_hbm, out_hbm, token_hbm, back_out, half_out, sums_out, partial_out, up_in, rows, bias, token, outer, back, sums, upstream, steps, partial, sems):
    copies = Copies(sems)
    near = [
        copies.start(source, up_in.at[i])
        for i, source in enumerate((up_hbm, part_hbm, other_hbm, middle_hbm))
    ]
    outers = copies.start(out_hbm.at[layer], outer)
    saved = [copies.start(row_hbm, rows), copies.start(bias_hbm, bias)]
    tokens = [copies.start(token_hbm.at[layer, member], token.at[member]) for member in range(3)]
    for copy in near:
        copy.wait()
    step, gain_part, shift_part = norm_backward(
        up_in[3], gain_ref[layer, 1:2, :], up_in[1] + up_in[2]
    )
    back[...] = up_in[0] + step
    copies.leave(back, back_out)
    copies.leave(core_half(back, ids), half_out)
    rounded = back[...].astype(LOW)
    sums[...] = jnp.zeros_like(sums)
    sums[0:1, :] = jnp.sum(rounded.astype(FULL), axis=0, keepdims=True)
    sums[1:2, :] = gain_part
    sums[2:3, :] = shift_part
    copies.leave(sums, sums_out)
    outers.wait()
    upstream[...] = matmul(rounded, outer[...], NT).astype(LOW)

    def row(index, first, last):
        return upstream[:, first:last] if index == 3 else rows[index, :, first:last]

    for copy in saved:
        copy.wait()
    attention_backward(heads, row, bias, steps, None, None)
    for member in range(3):
        tokens[member].wait()
        product = matmul(steps[member].astype(LOW), token[member])
        partial[...] = product if member == 0 else partial[...] + product
    copies.leave(partial, partial_out)
    copies.finish()


def attend_back(layer, ids, upstream, partial, other, middle, gains, rows, bias, out_proj, token_rows, after=()):
    count, width = upstream.shape
    local = token_rows.shape[2]
    heads = bias.shape[0]
    full = shape_of((count, width))
    return plain(
        functools.partial(attend_back_kernel, layer, heads),
        f"attend_back_{layer}",
        (ids,),
        (gains,),
        (upstream, partial, other, middle, rows, bias, out_proj, token_rows),
        [full, shape_of((count // 2, width)), shape_of((8, width)), full],
        [
            pltpu.VMEM((4, count, width), FULL),
            pltpu.VMEM((3, count, local), LOW),
            pltpu.VMEM((heads, count, count), FULL),
            pltpu.VMEM((3, local, width), LOW),
            pltpu.VMEM((local, width), LOW),
            pltpu.VMEM((count, width), FULL),
            pltpu.VMEM((8, width), FULL),
            pltpu.VMEM((count, local), LOW),
            pltpu.VMEM((3, count, local), FULL),
            pltpu.VMEM((count, width), FULL),
        ],
        2 * count * width * local * 4 + heads * count * count * 4096,
        8 * width * local + 24 * count * width,
        40,
        after,
    )


def finish_kernel(gain_ref, up_hbm, part_hbm, other_hbm, stream_hbm, gradient_out, sums_out, up_in, gradient, sums, sems):
    copies = Copies(sems)
    near = [
        copies.start(source, up_in.at[i])
        for i, source in enumerate((up_hbm, part_hbm, other_hbm, stream_hbm))
    ]
    for copy in near:
        copy.wait()
    step, gain_part, shift_part = norm_backward(up_in[3], gain_ref[0, 0:1, :], up_in[1] + up_in[2])
    gradient[...] = (up_in[0] + step).astype(LOW)
    copies.leave(gradient, gradient_out)
    sums[...] = jnp.zeros_like(sums)
    sums[1:2, :] = gain_part
    sums[2:3, :] = shift_part
    copies.leave(sums, sums_out)
    copies.finish()


def finish(upstream, partial, other, stream, gains):
    count, width = stream.shape
    return plain(
        finish_kernel,
        "finish",
        (),
        (gains,),
        (upstream, partial, other, stream),
        [shape_of((count, width), LOW), shape_of((8, width))],
        [
            pltpu.VMEM((4, count, width), FULL),
            pltpu.VMEM((count, width), LOW),
            pltpu.VMEM((8, width), FULL),
        ],
        0,
        20 * count * width,
        24,
    )


def line_window(units, line):
    own = units // line
    offsets = [z * own % 128 for z in range(line)]
    size = -(-(max(offsets) + own) // 128) * 128
    starts = [min(z * own // 128 * 128, units - size) for z in range(line)]
    return starts, [z * own - starts[z] for z in range(line)], size


def feed_gradients_kernel(layer, line, ids, x_hbm, y_hbm, in_hbm, out_hbm, outer_keep, outer_send, inner_keep, inner_send, stage, part_in, part_out, low_x, low_y, active, back, outer, inner, sems):
    units = in_hbm.shape[2]
    width = low_x.shape[1]
    rows = stage.shape[2]
    own = units // line
    starts, offsets, size = line_window(units, line)
    at = ids[AT_LINE]
    start, offset = jnp.int32(starts[0]), jnp.int32(offsets[0])
    for z in range(1, line):
        start = jnp.where(at == z, starts[z], start)
        offset = jnp.where(at == z, offsets[z], offset)
    start = pl.multiple_of(start, 128)
    copies = [
        pltpu.make_async_copy(in_hbm.at[layer, :, pl.ds(start, size)], part_in, sems.at[0, 2]),
        pltpu.make_async_copy(out_hbm.at[layer, pl.ds(start, size), :], part_out, sems.at[1, 2]),
    ]

    def fetch(tile):
        slot = tile % 2
        return [
            pltpu.make_async_copy(
                source.at[pl.ds(tile * rows, rows)], stage.at[side, slot], sems.at[side, slot]
            )
            for side, source in enumerate((x_hbm, y_hbm))
        ]

    flying = {0: fetch(0)}
    for copy in (*flying[0], *copies):
        copy.start()
    for tile in range(line):
        if tile + 1 < line:
            flying[tile + 1] = fetch(tile + 1)
            for copy in flying[tile + 1]:
                copy.start()
        for copy in flying[tile]:
            copy.wait()
        if tile == 0:
            for copy in copies:
                copy.wait()
        here = slice(tile * rows, (tile + 1) * rows)
        low_x[here, :] = stage[0, tile % 2].astype(LOW)
        low_y[here, :] = stage[1, tile % 2].astype(LOW)
        hidden = matmul(low_x[here, :], part_in[...])
        rise = 0.5 * (1.0 + lax.erf(hidden * ROOT_HALF))
        active[here, :] = (hidden * rise).astype(LOW)
        slope = rise + hidden * jnp.exp(-0.5 * hidden * hidden) * SLOPE_NORM
        back[here, :] = (matmul(low_y[here, :], part_out[...], NT) * slope).astype(LOW)

    @pl.loop(0, size // 128)
    def _(tile):
        lanes = pl.ds(pl.multiple_of(tile * 128, 128), 128)
        outer[lanes, :] = matmul(active[:, lanes], low_y[...], TN)

    @pl.loop(0, width // 128)
    def _(tile):
        lanes = pl.ds(pl.multiple_of(tile * 128, 128), 128)
        inner[lanes, :] = matmul(low_x[:, lanes], back[...], TN)

    pair = own // 2
    step = width // (GROUP * line)
    for z in range(len(set(offsets))):
        shifted = sorted(set(offsets))[z]
        for col in range(2):

            @pl.when((offset == shifted) & (ids[AT_COL] == col))
            def _(shifted=shifted, col=col):
                for target, part in ((outer_keep, col), (outer_send, 1 - col)):
                    first = shifted + part * pair
                    for r in range(2):
                        begin = first + r * (pair // 2)
                        target[r] = outer[begin : begin + pair // 2, :]

    for row in range(2):

        @pl.when(ids[AT_ROW] == row)
        def _(row=row):
            for z in range(line):
                for c in range(2):
                    for target, part in ((inner_keep, row), (inner_send, 1 - row)):
                        begin = (GROUP * z + 2 * c + part) * step
                        target[c, z] = inner[begin : begin + step, :]


def feed_gradients(layer, line, ids, xs, ys, hidden_in, hidden_out, after=()):
    count, width = xs.shape
    rows = count // line
    units = hidden_in.shape[2]
    own = units // line
    size = line_window(units, line)[2]
    anywhere = pl.BlockSpec(memory_space=pl.ANY)
    outs = [shape_of((2, own // 4, width))] * 2 + [shape_of((2, line, width // (GROUP * line), size))] * 2
    return call(
        functools.partial(feed_gradients_kernel, layer, line),
        f"feed_gradients_{layer}",
        (1,),
        [anywhere] * 2 + [pl.BlockSpec(memory_space=pltpu.HBM)] * 2,
        [whole_once(out.shape) for out in outs],
        outs,
        [
            pltpu.VMEM((2, 2, rows, width), FULL),
            pltpu.VMEM((width, size), LOW),
            pltpu.VMEM((size, width), LOW),
            pltpu.VMEM((line * rows, width), LOW),
            pltpu.VMEM((line * rows, width), LOW),
            pltpu.VMEM((line * rows, size), LOW),
            pltpu.VMEM((line * rows, size), LOW),
            pltpu.VMEM((size, width), FULL),
            pltpu.VMEM((width, size), FULL),
            pltpu.SemaphoreType.DMA((2, 3)),
        ],
        8 * line * rows * width * size,
        8 * line * rows * width + 16 * width * size,
        after=after,
    )(ids, *map(in_hbm, (xs, ys, hidden_in, hidden_out)))


def feed_scatter(pieces, line):
    outer_keep, outer_send, inner_keep, inner_send = pieces
    row, col = lax.axis_index("row"), lax.axis_index("col")
    outer_half, inner_half = yield [swap(outer_send, "col"), swap(inner_send, "row")]
    outer_other, inner_other = yield [
        swap(pick(outer_keep, 1 - row) + pick(outer_half, 1 - row), "row"),
        swap(pick(inner_keep, 1 - col) + pick(inner_half, 1 - col), "col"),
    ]
    outer = pick(outer_keep, row) + pick(outer_half, row) + outer_other
    inner = pick(inner_keep, col) + pick(inner_half, col) + inner_other
    place = lax.axis_index("line")
    far = yield [shift(pick(inner, (place + by) % line), line, by) for by in range(1, line)]
    slots = [pick(inner, place), *far]
    turned = jnp.stack([slots[-i % line] for i in range(line)] * 2)
    return lax.dynamic_slice_in_dim(turned, (line - place) % line, line, 0), outer


def piece_rows(own, line):
    padded = -(-own // line // 8) * 8
    return 3 * padded, padded


def attention_gradients_kernel(layer, heads, line, ids, kinds, *refs):
    parts = 2 * GROUP - 1
    sources = refs[:parts], refs[parts : 2 * parts]
    token_hbm, out_hbm, image_hbm, wide_ref, small_ref = refs[2 * parts : 2 * parts + 5]
    refs = refs[2 * parts + 5 :]
    token_out, table_out, images_out = refs[:3]
    (images, low_x, low_y, joined, attended_low, rows, bias, steps, attended) = refs[3:12]
    wide_sum, small_sum, stage, token, outer, scores, image_all, sems, weight_sems = refs[12:]
    slot = pl.program_id(0)
    kind = kinds[slot]
    count = low_x.shape[1]
    half = count // 2
    own = images.shape[2]
    at = 2 * ids[AT_COL] + ids[AT_ROW]

    def fetch(near):
        if near == 0:
            return [
                pltpu.make_async_copy(sources[side][0], stage.at[side, 0], sems.at[side, 0])
                for side in range(2)
            ]
        return [
            pltpu.make_async_copy(
                sources[side][(far + 1) * (GROUP - 1) + near - GROUP + 1],
                stage.at[side, near, pl.ds(pl.multiple_of(place * half, half), half)],
                sems.at[side, 2 * near + far - 1],
            )
            for side in range(2)
            for far, place in enumerate((ids[AT_CORE], 1 - ids[AT_CORE]))
        ]

    mine = pl.ds(pl.multiple_of(at * own, 16), own)
    weights = [
        pltpu.make_async_copy(token_hbm.at[layer, :, mine, :], token, weight_sems.at[0]),
        pltpu.make_async_copy(out_hbm.at[layer, mine, :], outer, weight_sems.at[1]),
        pltpu.make_async_copy(image_hbm.at[layer], image_all, weight_sems.at[2]),
    ]

    @pl.when(slot == 0)
    def _():
        for copy in (*fetch(0), *weights):
            copy.start()
        for near in range(1, GROUP):
            for copy in fetch(near):
                copy.start()
        wide_sum[...] = jnp.zeros_like(wide_sum)
        small_sum[...] = jnp.zeros_like(small_sum)
    for near in range(GROUP):

        @pl.when(slot == near)
        def _(near=near):
            for copy in fetch(near):
                copy.wait()

    @pl.when(slot == 0)
    def _():
        for copy in weights:
            copy.wait()
        for j in range(GROUP):

            @pl.when(at == j)
            def _(j=j):
                for member in range(2):
                    images[member] = image_all[member, :, j * own : (j + 1) * own]

    fill_bias(heads, kind, wide_ref, small_ref, bias)
    low_x[slot] = stage[0, slot].astype(LOW)
    low_y[slot] = stage[1, slot].astype(LOW)
    for member in range(3):
        projected = matmul(low_x[slot], token[member], NT)
        for i in range(IMAGES):
            here = slice(i * (count // IMAGES), (i + 1) * (count // IMAGES))
            if member == 1:
                rows[member, here, :] = projected[here].astype(LOW)
            else:
                near = images[member // 2]
                first = near[0:1, :]
                mine = near[i : i + 1, :]
                for other in range(1, GROUP):
                    begin = other * IMAGES
                    first = jnp.where(slot == other, near[begin : begin + 1, :], first)
                    mine = jnp.where(slot == other, near[begin + i : begin + i + 1, :], mine)
                mine = jnp.where(kind != 0, mine, first)
                rows[member, here, :] = (projected[here] + mine).astype(LOW)
    rows[3] = matmul(low_y[slot], outer[...], NT).astype(LOW)

    def row(index, first, last):
        return rows[index, :, first:last]

    attention_backward(heads, row, bias, steps, attended, scores)
    collect_table(heads, kind, scores, wide_sum, small_sum)
    attended_low[slot] = attended[...].astype(LOW)
    for member in range(3):
        rounded = steps[member].astype(LOW)
        joined[slot, :, member * own : (member + 1) * own] = rounded
        if member != 1:
            sums = [
                jnp.sum(
                    rounded[i * (count // IMAGES) : (i + 1) * (count // IMAGES)].astype(FULL),
                    axis=0,
                    keepdims=True,
                )
                for i in range(IMAGES)
            ]
            everything = sums[0] + sums[1] + sums[2] + sums[3]
            for i in range(IMAGES):
                alone = everything if i == 0 else jnp.zeros_like(everything)
                images_out[0, member // 2, i : i + 1, :] = jnp.where(kind != 0, sums[i], alone)

    @pl.when(slot == GROUP - 1)
    def _():
        flat = GROUP * count
        width = low_x.shape[2]

        chunk, piece = width // line, own // line
        rest, padded = piece_rows(own, line)
        product = matmul(low_x[...].reshape(flat, width), joined[...].reshape(flat, -1), TN)
        projection = matmul(
            attended_low[...].reshape(flat, -1), low_y[...].reshape(flat, -1), TN
        )
        size = width // 3
        for z in range(line):
            begin = z * (chunk + rest)
            token_out[begin : begin + chunk, :] = product[z * chunk : (z + 1) * chunk]
            for third in range(3):
                at_row = begin + chunk + third * padded
                token_out[at_row : at_row + padded, :] = jnp.zeros((padded, 3 * own), FULL)
                token_out[at_row : at_row + piece, :size] = projection[
                    z * piece : (z + 1) * piece, third * size : (third + 1) * size
                ]
        for head in range(heads):
            table_out[head : head + 1, :] = fold_table(wide_sum[head], small_sum[head])


def attention_gradients(layer, line, ids, kinds, near_x, near_y, token_rows, per_image, out_proj, wide, small, after=()):
    count, width = near_x[0].shape
    depth, _, local, _ = token_rows.shape
    own, heads = local // GROUP, wide.shape[0] // depth // GROUP
    near = [pl.BlockSpec(memory_space=pl.ANY)] * (len(near_x) + len(near_y))

    def own_heads(slot, ids, kinds):
        return (layer * GROUP + 2 * ids[AT_COL] + ids[AT_ROW], 0, 0)

    outs = [
        shape_of((width + line * piece_rows(own, line)[0], 3 * own)),
        shape_of((heads, 4 * SPAN)),
        shape_of((GROUP, 2, IMAGES, own)),
    ]
    return call(
        functools.partial(attention_gradients_kernel, layer, heads, line),
        f"attention_gradients_{layer}",
        (GROUP,),
        [
            *near,
            pl.BlockSpec(memory_space=pltpu.HBM),
            pl.BlockSpec(memory_space=pltpu.HBM),
            pl.BlockSpec(memory_space=pltpu.HBM),
            pl.BlockSpec((heads, *wide.shape[1:]), own_heads),
            pl.BlockSpec((heads, *small.shape[1:]), own_heads),
        ],
        [
            *[whole_once(out.shape) for out in outs[:2]],
            pl.BlockSpec((1, 2, IMAGES, own), lambda s, ids, kinds: (s, 0, 0, 0)),
        ],
        outs,
        [
            pltpu.VMEM((2, GROUP * IMAGES, own), FULL),
            pltpu.VMEM((GROUP, count, width), LOW),
            pltpu.VMEM((GROUP, count, width), LOW),
            pltpu.VMEM((GROUP, count, 3 * own), LOW),
            pltpu.VMEM((GROUP, count, own), LOW),
            pltpu.VMEM((4, count, own), LOW),
            pltpu.VMEM((heads, count, count), FULL),
            pltpu.VMEM((3, count, own), FULL),
            pltpu.VMEM((count, own), FULL),
            pltpu.VMEM((heads, *wide.shape[1:]), FULL),
            pltpu.VMEM((heads, *small.shape[1:]), FULL),
            pltpu.VMEM((2, GROUP, count, width), FULL),
            pltpu.VMEM((3, own, width), LOW),
            pltpu.VMEM((own, width), LOW),
            pltpu.VMEM((heads, count, count), FULL),
            pltpu.VMEM(per_image.shape[1:], FULL),
            pltpu.SemaphoreType.DMA((2, 2 * GROUP)),
            pltpu.SemaphoreType.DMA((3,)),
        ],
        2 * GROUP * count * width * own * 8 + GROUP * heads * count * count * 4096,
        8 * GROUP * count * width + 8 * width * local,
        2,
        after,
    )(
        ids, kinds, *map(in_hbm, (*near_x, *near_y, token_rows, out_proj, per_image)), wide, small
    )


def swap(value, axis):
    return lax.ppermute(value, axis, [(0, 1), (1, 0)])


def shift(value, line, by=1):
    return lax.ppermute(value, "line", [(i, (i + by) % line) for i in range(line)])


def pick(value, index, axis=0):
    return lax.dynamic_index_in_dim(value, index, axis, keepdims=False)


def gather_line(half):
    return lax.all_gather(half, ("line", "tensor"), tiled=True)


def plane_steps(value, half):
    across, along = yield [swap(half, "row"), swap(half, "col")]
    (corner,) = yield [swap_corner(half)]
    others = yield [swap(part, "tensor") for part in (across, along, corner)]
    return [value, across, along, corner, *others]


def swap_corner(value):
    return lax.ppermute(value, ("col", "row"), [(0, 3), (3, 0), (1, 2), (2, 1)])


def scatter_line(value, line):
    place = lax.axis_index("line")
    far = yield [shift(pick(value, (place + by) % line), line, by) for by in range(1, line)]
    return functools.reduce(jnp.add, far, pick(value, place))


def scatter_vectors(value, line):
    row, col = lax.axis_index("row"), lax.axis_index("col")
    (other,) = yield [swap(pick(value, 1 - row, 2), "row")]
    value = pick(value, row, 2) + other
    (other,) = yield [swap(pick(value, 1 - col, 1), "col")]
    return (yield from scatter_line(pick(value, col, 1) + other, line))


def scatter_table(value, line):
    return exchange_plane((yield from scatter_line(value, line)))


def line_steps(value, line):
    far = yield [shift(value, line, by) for by in range(1, line)]
    return jnp.concatenate([value, *far])


def exchange_plane(value):
    col, row = lax.axis_index("col"), lax.axis_index("row")
    place = 2 * col + row
    across = swap(pick(value, place ^ 1), "row")
    along = swap(pick(value, place ^ 2), "col")
    corner = swap_corner(pick(value, place ^ 3))
    slots = [pick(value, place), across, along, corner]
    slots = [jnp.where(row == 0, slots[i], slots[i ^ 1]) for i in range(4)]
    return jnp.stack([jnp.where(col == 0, slots[i], slots[i ^ 2]) for i in range(4)])


def local(
    tokens,
    segment_ids,
    timesteps,
    norm_gain,
    norm_bias,
    token_proj,
    time_proj,
    bias_table,
    out_proj,
    hidden_in,
    hidden_out,
    branch_bias,
    cotangent,
    *,
    line,
):
    count, width = tokens.shape
    depth, _, _, local_width = token_proj.shape
    heads = bias_table.shape[1]
    units = hidden_in.shape[2]
    own = local_width // GROUP
    n_dp = GROUP * line
    features = width // n_dp
    line_at = lax.axis_index("line")
    place = 2 * lax.axis_index("col") + lax.axis_index("row")
    ids = jnp.stack(
        [segment_ids[-1], line_at, lax.axis_index("col"), lax.axis_index("row"), lax.axis_index("tensor")]
    ).astype(jnp.int32)
    embedded = sinusoid(timesteps[0], jnp.arange(width, dtype=jnp.int32), width)
    per_image = lax.dot_general(
        time_proj, embedded, (((2,), (1,)), ((), ())), preferred_element_type=FULL
    )
    per_image = jnp.swapaxes(per_image, 2, 3)
    info = jnp.concatenate([timesteps[0], segment_ids[-1:]]).astype(FULL)
    packed = jnp.concatenate(
        [
            per_image.reshape(2 * depth * IMAGES, local_width),
            jnp.pad(info[None], ((0, 7), (0, local_width - IMAGES - 1))),
        ]
    )
    packed = jnp.stack([packed, swap(packed, "row"), swap(packed, "col"), swap_corner(packed)])
    near_image = packed[:, : 2 * depth * IMAGES].reshape(GROUP, depth, 2, IMAGES, local_width)
    near_image = jnp.moveaxis(near_image, 0, 2).reshape(depth, 2, GROUP * IMAGES, local_width)
    near = packed[:, 2 * depth * IMAGES, : IMAGES + 1]
    kinds = near[:, IMAGES].astype(jnp.int32)
    near = jnp.pad(near, ((0, 4), (0, 123 - IMAGES + 4)))
    every = jnp.concatenate([near] + [shift(near, line, by) for by in range(1, line)])
    every = every.reshape(line, 8, -1)[:, :GROUP, :IMAGES]
    own_feature = line_at * (GROUP * features) + jnp.arange(GROUP * features, dtype=jnp.int32)
    embedded_every = sinusoid(every.reshape(-1), own_feature, width).astype(FULL)
    token_rows = jnp.swapaxes(token_proj, 2, 3)
    wide, small = expand_table(bias_table.reshape(depth * heads, -1))

    stream = (tokens,)
    saved = []
    moves = Moves()
    half = lax.dynamic_slice_in_dim(cotangent, lax.axis_index("tensor") * (count // 2), count // 2, 0)
    gathered_up = gather_line(half.astype(FULL))
    for layer in range(depth):
        held, normed, half, rows, partial, bias = attend(
            layer, ids, stream, norm_gain, norm_bias, branch_bias, token_rows, per_image, out_proj, wide, small
        )
        if layer == depth - 1:
            partial, gathered_up = moves.kernel(partial, [gathered_up])
        else:
            (partial,) = moves.kernel(partial)
        moves.start(("first", layer), plane_steps(normed, half))
        middle, half_second, slope, partial = feed(
            layer,
            ids,
            held,
            partial,
            swap(partial, "tensor"),
            branch_bias,
            norm_gain,
            norm_bias,
            hidden_in,
            hidden_out,
        )
        (partial,) = moves.kernel(partial)
        line_second = gather_line(half_second)
        saved.append((held, rows, middle, slope, line_second, bias))
        stream = (middle, partial, swap(partial, "tensor"))
    output = (stream[0] + (stream[1] + stream[2]) + branch_bias[depth - 1, 1]).astype(LOW)

    upstream = (cotangent,)
    collected = [None] * depth
    vectors = [None] * depth
    gathered = [None] * depth
    gathered_line = [None] * depth
    for layer in reversed(range(depth)):
        held, rows, middle, slope, _, bias = saved[layer]
        current, half_up, feed_sums, partial = feed_back(
            layer, ids, upstream, slope, hidden_in, hidden_out, norm_gain
        )
        (partial,) = moves.kernel(partial)
        if layer < depth - 1:
            gathered_up = gather_line(half_up)
        back_middle, half, middle_sums, back_partial = attend_back(
            layer,
            ids,
            current,
            partial,
            swap(partial, "tensor"),
            middle,
            norm_gain,
            rows,
            bias,
            out_proj,
            token_rows,
        )
        other = depth - 1 - layer
        back_partial, gathered_line[other] = moves.kernel(back_partial, [saved[other][4]])
        moves.start(("branch", layer), plane_steps(back_middle, half))
        upstream = (back_middle, back_partial, swap(back_partial, "tensor"), held)
        vectors[layer] = (feed_sums, middle_sums)
        gathered[layer] = gathered_up
    gradient_tokens, last_sums = finish(*upstream, norm_gain)
    (last_sums,) = moves.kernel(last_sums)
    firsts = [last_sums] + [vectors[layer][0] for layer in range(depth - 1)]
    rows = jnp.stack(
        [
            jnp.stack([jnp.stack([firsts[l][1], vectors[l][1][1]]) for l in range(depth)]),
            jnp.stack([jnp.stack([firsts[l][2], vectors[l][1][2]]) for l in range(depth)]),
            jnp.stack([jnp.stack([vectors[l][1][0], vectors[l][0][0]]) for l in range(depth)]),
        ]
    )
    rows = jnp.moveaxis(rows.reshape(6 * depth, line, 2, 2, features), 0, 3)
    moves.start("rows", scatter_vectors(rows, line))

    turn = last_sums
    tokens_of = {}

    def run_feed(layer, turn):
        pieces = feed_gradients(
            layer, line, ids, gathered_line[layer], gathered[layer], hidden_in, hidden_out, after=(turn,)
        )
        (turn,) = moves.kernel(pieces[0])
        moves.start(("feed", layer), feed_scatter((turn, *pieces[1:]), line))
        return turn

    def run_attention(layer, turn):
        token, table, images = attention_gradients(
            layer,
            line,
            ids,
            kinds,
            moves.found["first", layer],
            moves.found["branch", layer],
            token_rows,
            near_image,
            out_proj,
            wide,
            small,
            after=(turn,),
        )
        turn, gathered[0] = moves.kernel(table, [gathered[0]])
        tokens_of[layer] = lax.psum_scatter(token, "line", scatter_dimension=0, tiled=True)
        table = turn.reshape(-1, line, GROUP, 4 * SPAN // n_dp)
        moves.start(("table", layer), scatter_table(jnp.moveaxis(table, 0, 2), line))
        moves.start(("images", layer), line_steps(images, line))
        return turn

    for layer in reversed(range(1, depth)):
        turn = run_feed(layer, run_attention(layer, turn))
    run_feed(0, run_attention(0, turn))
    moves.finish()

    for layer in reversed(range(depth)):
        inner, outer = moves.found["feed", layer]
        offsets = line_window(units, line)[1]
        inner = jnp.concatenate(
            [inner[z, :, offsets[z] : offsets[z] + units // line] for z in range(line)], axis=1
        )
        token, images = tokens_of[layer], moves.found["images", layer]
        chunk, padded = GROUP * features, piece_rows(own, line)[1]
        thirds = [
            token[chunk + third * padded : chunk + third * padded + own // line, : width // 3]
            for third in range(3)
        ]
        projection = jnp.concatenate(thirds, axis=1)
        token = token[:chunk]
        projection = lax.ppermute(
            projection,
            LINES,
            [(GROUP * z + j, line * j + z) for z in range(line) for j in range(GROUP)],
        )
        time = jnp.einsum(
            "rif,rmic->fmc",
            embedded_every.reshape(n_dp, IMAGES, GROUP * features),
            images,
            precision=lax.Precision.HIGHEST,
        )
        joined = jnp.concatenate([token, time.reshape(GROUP * features, 2 * own)], axis=1)
        joined = exchange_plane(joined.reshape(GROUP, features, 5 * own))
        joined = joined.reshape(GROUP, features, 5, own).transpose(2, 1, 0, 3)
        joined = joined.reshape(5, features, local_width)
        collected[layer] = (joined[:3], joined[3:], projection, inner, outer)
    rows = moves.found["rows"].reshape(3, depth, 2, features)
    table = jnp.stack([moves.found["table", layer].reshape(heads, -1) for layer in range(depth)])
    stacked = [jnp.stack([terms[member] for terms in collected]) for member in range(5)]
    token, time, projection, inner, outer = stacked
    return (
        output,
        gradient_tokens,
        rows[0],
        rows[1],
        token,
        time,
        table,
        projection,
        inner,
        outer,
        rows[2],
    )


def solution(mesh):
    line = mesh.shape["dp"] // GROUP
    fine = Mesh(mesh.devices.reshape(line, 2, 2, mesh.shape["tensor"]), (*LINES, "tensor"))
    return jax.shard_map(
        functools.partial(local, line=line),
        mesh=fine,
        in_specs=(
            P(LINES, None),
            P(LINES),
            P(LINES, None),
            P(),
            P(),
            P(None, None, None, "tensor"),
            P(None, None, None, "tensor"),
            P(None, "tensor", None),
            P(None, "tensor", None),
            P(None, None, "tensor"),
            P(None, "tensor", None),
            P(),
            P(LINES, None),
        ),
        out_specs=(
            P(LINES, None),
            P(LINES, None),
            P(None, None, LINES),
            P(None, None, LINES),
            P(None, None, LINES, "tensor"),
            P(None, None, LINES, "tensor"),
            P(None, "tensor", LINES),
            P(None, ("tensor", *LINES), None),
            P(None, LINES, "tensor"),
            P(None, ("tensor", *LINES), None),
            P(None, None, LINES),
        ),
        check_vma=False,
    )
```

```python
import functools
import math

import jax
import jax.numpy as jnp
from jax import lax
from jax.experimental import pallas as pl
from jax.experimental.pallas import tpu as pltpu
from jax.sharding import Mesh
from jax.sharding import PartitionSpec as P

SIDE = 16
HALF = 8
SPAN = SIDE * SIDE
IMAGES = 4
BLOCK = SPAN // IMAGES
GROUP = 4
WEIGHT, GRADIENT_WEIGHT, WHOLE_COST = 10, 6, 40_000_000_000
EPSILON = 1e-06
MASKED = -1e30
ROOT_HALF = 0.7071067811865476
SLOPE_NORM = 0.3989422804014327
LINES = ("line", "col", "row")
LOW = jnp.bfloat16
FULL = jnp.float32
KIND, AT_LINE, AT_COL, AT_ROW, AT_CORE = range(5)


def matmul(left, right, dims=((1,), (0,))):
    return lax.dot_general(left, right, (dims, ((), ())), preferred_element_type=FULL)


NT = ((1,), (1,))
TN = ((0,), (0,))


def normal_of(stream):
    center = stream - jnp.mean(stream, axis=-1, keepdims=True)
    inverse = lax.rsqrt(jnp.mean(center * center, axis=-1, keepdims=True) + EPSILON)
    return center * inverse, inverse


def norm_backward(stream, gain, upstream):
    normal, inverse = normal_of(stream)
    gain_part = jnp.sum(upstream * normal, axis=0, keepdims=True)
    shift_part = jnp.sum(upstream, axis=0, keepdims=True)
    scaled = upstream * gain
    inner = (
        scaled
        - jnp.mean(scaled, axis=-1, keepdims=True)
        - normal * jnp.mean(scaled * normal, axis=-1, keepdims=True)
    )
    return inner * inverse, gain_part, shift_part


def sinusoid(steps, feature, width):
    half = width // 2
    rates = jnp.exp(-math.log(10000.0) * (feature % half).astype(FULL) / half)
    angles = steps.astype(FULL)[:, None] * rates[None, :]
    wave = jnp.where(feature[None, :] < half, jnp.cos(angles), jnp.sin(angles))
    return wave.astype(LOW)


def whole(shape):
    return pl.BlockSpec(shape, lambda *_: (0,) * len(shape))


def whole_once(shape):
    return pl.BlockSpec(shape, lambda *_: (0,) * len(shape), pipeline_mode=pl.Buffered(1))


def call(kernel, name, grid, in_specs, out_specs, out_shape, scratch, flops, size, scalars=1, after=()):
    first = scalars + len(in_specs)

    def body(*refs):
        kernel(*refs[:first], *refs[first + len(after) :])

    made = pl.pallas_call(
        body,
        grid_spec=pltpu.PrefetchScalarGridSpec(
            num_scalar_prefetch=scalars,
            grid=grid,
            in_specs=[*in_specs, *[pl.BlockSpec(memory_space=pl.ANY)] * len(after)],
            out_specs=out_specs,
            scratch_shapes=scratch,
        ),
        out_shape=[pltpu.HBM(out.shape, out.dtype) for out in out_shape],
        compiler_params=pltpu.CompilerParams(vmem_limit_bytes=40 << 20),
        cost_estimate=pl.CostEstimate(
            flops=int(flops * GRADIENT_WEIGHT), bytes_accessed=int(size * GRADIENT_WEIGHT), transcendentals=0
        ),
        name=name,
    )
    return lambda *operands: made(*operands, *map(in_hbm, after))


def shape_of(shape, kind=FULL):
    return jax.ShapeDtypeStruct(shape, kind)


def regroup(value, pieces):
    lane = lax.broadcasted_iota(jnp.int32, (value.shape[0], 128), 1)
    total = jnp.zeros((value.shape[0], 128), FULL)
    for tile, source, place, lanes in pieces:
        part = value[:, tile * 128 : tile * 128 + 128]
        turn = (place - source) % 128
        part = part if turn == 0 else pltpu.roll(part, turn, 1)
        total = jnp.where((lane >= place) & (lane < place + lanes), part, total)
    return total


def expand_kernel(table_ref, wide_ref, small_ref):
    size = table_ref.shape[1]
    table = table_ref[...]
    for c in range(SIDE):
        turned = pltpu.roll(table, size - SIDE + c, 1)
        wide = jnp.concatenate(
            [
                regroup(
                    turned,
                    [(2 * o + p // 4, 32 * (p % 4), 16 * p, 16) for p in range(8)],
                )
                for o in range(4)
            ],
            axis=1,
        )
        wide_ref[:, c, :] = wide
        if c < HALF:
            small_ref[:, c, :] = regroup(
                wide, [(1 + k // 8, 16 * (k % 8), 8 * k, 8) for k in range(16)]
            )


def expand_table(table):
    rows, size = table.shape
    return pl.pallas_call(
        expand_kernel,
        out_shape=[shape_of((rows, SIDE, size // 2)), shape_of((rows, HALF, size // 8))],
        name="expand_table",
    )(table)


def fold_table(wide, small):
    inner = jnp.concatenate([small, jnp.zeros_like(small)], axis=0)
    tiles = [wide[:, 128 * t : 128 * t + 128] for t in range(4)]
    for t in range(2):
        tiles[1 + t] = tiles[1 + t] + regroup(
            inner, [(0, 8 * (8 * t + q), 16 * q, 8) for q in range(8)]
        )
    wide = jnp.concatenate(tiles, axis=1)
    spread = jnp.concatenate(
        [
            regroup(
                wide,
                [(o // 2, 64 * (o % 2) + 16 * q, 32 * q, 16) for q in range(4)],
            )
            for o in range(8)
        ],
        axis=1,
    )
    return functools.reduce(
        jnp.add, [pltpu.roll(spread[c : c + 1], SIDE - c, 1) for c in range(SIDE)]
    )


def fill_bias(heads, kind, wide_ref, small_ref, bias):
    @pl.when(kind == 0)
    def _():
        for head in range(heads):
            wide = wide_ref[head]
            for r in range(SIDE):
                turned = pltpu.roll(wide, 2 * SPAN - SIDE * (SIDE - r), 1)
                bias[head, r * SIDE : (r + 1) * SIDE, :] = turned[:, :SPAN]

    @pl.when(kind != 0)
    def _():
        image = lax.broadcasted_iota(jnp.int32, (HALF, SPAN), 1) // BLOCK
        lane = lax.broadcasted_iota(jnp.int32, (HALF, 2 * BLOCK), 1)
        for head in range(heads):
            small = small_ref[head]
            for r in range(HALF):
                turned = pltpu.roll(small, 2 * BLOCK - HALF * (HALF - r), 1)
                turned = jnp.where(lane < BLOCK, turned, 0.0)
                pair = turned + pltpu.roll(turned, BLOCK, 1)
                line = jnp.concatenate([pair, pair], axis=1)
                for i in range(IMAGES):
                    start = i * BLOCK + r * HALF
                    bias[head, start : start + HALF, :] = jnp.where(image == i, line, MASKED)


def collect_table(heads, kind, back, wide_sum, small_sum):
    @pl.when(kind == 0)
    def _():
        for head in range(heads):
            total = wide_sum[head]
            for r in range(SIDE):
                part = back[head, r * SIDE : (r + 1) * SIDE, :]
                part = jnp.concatenate([part, jnp.zeros_like(part)], axis=1)
                total = total + pltpu.roll(part, SIDE * (SIDE - r), 1)
            wide_sum[head] = total

    @pl.when(kind != 0)
    def _():
        for head in range(heads):
            total = small_sum[head]
            lane = lax.broadcasted_iota(jnp.int32, total.shape, 1)
            for r in range(HALF):
                part = functools.reduce(
                    jnp.add,
                    [
                        back[head, i * BLOCK + r * HALF : i * BLOCK + (r + 1) * HALF, :]
                        for i in range(IMAGES)
                    ],
                )
                part = part[:, : SPAN // 2] + part[:, SPAN // 2 :]
                part = jnp.where(lane < BLOCK, part + pltpu.roll(part, BLOCK, 1), 0.0)
                total = total + pltpu.roll(part, HALF * (HALF - r), 1)
            small_sum[head] = total


def window_of(head, head_dim, width):
    if width <= 256:
        return 0, width
    return head * head_dim // 128 * 128, min(-(-(head + 1) * head_dim // 128) * 128, width)


def mine_of(head, head_dim, first, last, rows):
    lane = lax.broadcasted_iota(jnp.int32, (rows, last - first), 1) + first
    return (lane >= head * head_dim) & (lane < (head + 1) * head_dim)


def softmax_of(queries, keys, bias, scale):
    scores = matmul(keys, queries, NT) * scale + bias
    expo = jnp.exp(scores - jnp.max(scores, axis=0, keepdims=True))
    return expo * (1.0 / jnp.sum(expo, axis=0, keepdims=True))


def attention_forward(heads, row, bias, total):
    count, width = total.shape
    head_dim = width // heads
    scale = 1.0 / math.sqrt(head_dim)
    zero = jnp.zeros((), LOW)
    total[...] = jnp.zeros_like(total)
    for head in range(heads):
        first, last = window_of(head, head_dim, width)
        mine = mine_of(head, head_dim, first, last, count)
        queries = jnp.where(mine, row(0, first, last), zero)
        values = jnp.where(mine, row(2, first, last), zero)
        weights = softmax_of(queries, row(1, first, last), bias[head], scale)
        total[:, first:last] += matmul(weights.astype(LOW), values, TN)


def attention_backward(heads, row, bias, steps, attended, scores_out):
    count, width = steps.shape[1:]
    head_dim = width // heads
    scale = 1.0 / math.sqrt(head_dim)
    zero = jnp.zeros((), LOW)
    steps[...] = jnp.zeros_like(steps)
    if attended is not None:
        attended[...] = jnp.zeros_like(attended)
    for head in range(heads):
        first, last = window_of(head, head_dim, width)
        mine = mine_of(head, head_dim, first, last, count)
        queries, keys, values, upstream = (
            jnp.where(mine, row(member, first, last), zero) for member in range(4)
        )
        weights = softmax_of(queries, keys, bias[head], scale)
        low = weights.astype(LOW)
        back_weights = matmul(values, upstream, NT)
        inner = jnp.sum(weights * back_weights, axis=0, keepdims=True)
        back_scores = (weights * (back_weights - inner)).astype(LOW)
        steps[0, :, first:last] += matmul(back_scores, keys, TN) * scale
        steps[1, :, first:last] += matmul(back_scores, queries) * scale
        steps[2, :, first:last] += matmul(low, upstream)
        if attended is not None:
            attended[:, first:last] += matmul(low, values, TN)
        if scores_out is not None:
            scores_out[head] = back_scores.astype(FULL)


def in_hbm(value):
    return pltpu.with_memory_space_constraint(value, pltpu.HBM)


HBM = pl.BlockSpec(memory_space=pltpu.HBM)
NEAR = pl.BlockSpec(memory_space=pltpu.VMEM)


def plain(kernel, name, scalars, near, far, outs, scratch, flops, size, limit, after=()):
    first = len(scalars) + len(near) + len(far)

    def body(*refs):
        kernel(*refs[:first], *refs[first + len(after) :])

    return pl.pallas_call(
        body,
        in_specs=[
            *[pl.BlockSpec(memory_space=pltpu.SMEM)] * len(scalars),
            *[NEAR] * len(near),
            *[HBM] * (len(far) + len(after)),
        ],
        out_specs=[HBM] * len(outs),
        out_shape=[pltpu.HBM(out.shape, out.dtype) for out in outs],
        scratch_shapes=[*scratch, pltpu.SemaphoreType.DMA((24,))],
        compiler_params=pltpu.CompilerParams(vmem_limit_bytes=limit << 20),
        cost_estimate=pl.CostEstimate(
            flops=int(flops * WEIGHT), bytes_accessed=int(size * WEIGHT), transcendentals=0
        ),
        name=name,
    )(*scalars, *near, *map(in_hbm, (*far, *after)))


def gate(values):
    def body(*refs):
        del refs

    return pl.pallas_call(
        body,
        in_specs=[HBM] * len(values),
        out_specs=[HBM] * len(values),
        out_shape=[pltpu.HBM(value.shape, value.dtype) for value in values],
        input_output_aliases={i: i for i in range(len(values))},
        name="gate",
    )(*map(in_hbm, values))


class Moves:
    def __init__(self):
        self.running, self.found = [], {}

    def start(self, name, steps):
        self.running.append((name, steps, next(steps)))

    def kernel(self, output, due=()):
        arrived = [array for _, _, arrays in self.running for array in arrays]
        held = gate([output, *due, *arrived])
        self.step(iter(held[1 + len(due) :]))
        return held[: 1 + len(due)]

    def chain(self, partial, due=()):
        arrived = [array for _, _, arrays in self.running for array in arrays]
        partial, *rest = gate([partial, *due, *arrived])
        partial, other, *rest = gate([partial, swap(partial, "tensor"), *rest])
        self.step(iter(rest[len(due) :]))
        return partial, other, *rest[: len(due)]

    def hurry(self, name):
        if name in self.found:
            return self.found[name]
        others = [entry for entry in self.running if entry[0] != name]
        self.running = [entry for entry in self.running if entry[0] == name]
        self.finish()
        self.running = others
        return self.found[name]

    def step(self, arrived=None):
        before, self.running = self.running, []
        for name, steps, arrays in before:
            if arrived is not None:
                arrays = [next(arrived) for _ in arrays]
            try:
                self.running.append((name, steps, steps.send(arrays)))
            except StopIteration as stop:
                self.found[name] = stop.value

    def finish(self):
        while self.running:
            self.step()


class Copies:
    def __init__(self, sems):
        self.sems, self.count, self.leaving = sems, 0, []

    def start(self, source, target):
        copy = pltpu.make_async_copy(source, target, self.sems.at[self.count])
        self.count += 1
        copy.start()
        return copy

    def leave(self, source, target):
        self.leaving.append(self.start(source, target))

    def finish(self):
        for copy in self.leaving:
            copy.wait()


def core_half(ref, ids):
    half = ref.shape[0] // 2
    return ref.at[pl.ds(pl.multiple_of(ids[AT_CORE] * half, half), half)]


def attend_kernel(layer, heads, ids, gain_ref, shift_ref, biases_ref, *refs):
    parts = 1 if layer == 0 else 3
    stream_hbm, refs = refs[:parts], refs[parts:]
    token_hbm, out_hbm, image_hbm, wide_hbm, small_hbm = refs[:5]
    stream_out, normed_out, half_out, row_out, partial_out, bias_out = refs[5:11]
    stream_in, token, outer, image, wide, small, normed, low, rows, bias, total, partial, sems = refs[11:]
    copies = Copies(sems)
    per = pl.ds(layer * heads, heads)
    near = [copies.start(source, stream_in.at[i]) for i, source in enumerate(stream_hbm)]
    tables = [copies.start(wide_hbm.at[per], wide), copies.start(small_hbm.at[per], small)]
    tokens = [copies.start(token_hbm.at[layer, 0], token.at[0])]
    images = copies.start(image_hbm.at[layer], image)
    tokens += [copies.start(token_hbm.at[layer, m], token.at[m]) for m in (1, 2)]
    outers = copies.start(out_hbm.at[layer], outer)
    kind = ids[KIND]
    count = low.shape[0]
    for copy in near:
        copy.wait()
    if layer == 0:
        stream = stream_in[0].astype(FULL)
    else:
        stream = stream_in[0] + (stream_in[1] + stream_in[2]) + biases_ref[layer - 1, 1:2, :]
    normed[...] = normal_of(stream)[0] * gain_ref[layer, 0:1, :] + shift_ref[layer, 0:1, :]
    if layer == 0:
        partial[...] = stream
        copies.leave(partial, stream_out)
    else:
        stream_in[0] = stream
        copies.leave(stream_in.at[0], stream_out)
    copies.leave(normed, normed_out)
    copies.leave(core_half(normed, ids), half_out)
    low[...] = normed[...].astype(LOW)
    for copy in tables:
        copy.wait()
    fill_bias(heads, kind, wide, small, bias)
    copies.leave(bias, bias_out)
    for member in range(3):
        tokens[member].wait()
        projected = matmul(low[...], token[member], NT)
        if member == 0:
            images.wait()
        if member == 1:
            rows[member] = projected.astype(LOW)
            continue
        for i in range(IMAGES):
            mine = image[member // 2, i : i + 1, :]
            mine = jnp.where(kind != 0, mine, image[member // 2, 0:1, :])
            here = slice(i * (count // IMAGES), (i + 1) * (count // IMAGES))
            rows[member, here, :] = (projected[here] + mine).astype(LOW)
    copies.leave(rows, row_out)

    def row(index, first, last):
        return rows[index, :, first:last]

    attention_forward(heads, row, bias, total)
    outers.wait()
    if layer == 0:
        copies.leaving.pop(0).wait()
    partial[...] = matmul(total[...].astype(LOW), outer[...])
    copies.leave(partial, partial_out)
    copies.finish()


def attend(layer, ids, stream, gains, shifts, biases, token_rows, per_image, out_proj, wide, small, after=()):
    count, width = stream[0].shape
    depth, _, local, _ = token_rows.shape
    heads = wide.shape[0] // depth
    full = shape_of((count, width))
    outs = [
        full,
        full,
        shape_of((count // 2, width)),
        shape_of((3, count, local), LOW),
        full,
        shape_of((heads, count, count)),
    ]
    return plain(
        functools.partial(attend_kernel, layer, heads),
        f"attend_{layer}",
        (ids,),
        (gains, shifts, biases),
        (*stream, token_rows, out_proj, per_image, wide, small),
        outs,
        [
            pltpu.VMEM((len(stream), count, width), stream[0].dtype),
            pltpu.VMEM((3, local, width), LOW),
            pltpu.VMEM((local, width), LOW),
            pltpu.VMEM(per_image.shape[1:], FULL),
            pltpu.VMEM((heads, *wide.shape[1:]), FULL),
            pltpu.VMEM((heads, *small.shape[1:]), FULL),
            pltpu.VMEM((count, width), FULL),
            pltpu.VMEM((count, width), LOW),
            pltpu.VMEM((3, count, local), LOW),
            pltpu.VMEM((heads, count, count), FULL),
            pltpu.VMEM((count, local), FULL),
            pltpu.VMEM((count, width), FULL),
        ],
        2 * count * width * local * 4,
        8 * width * local + 16 * count * width,
        40,
        after,
    )


CHUNK = 768


def feed_kernel(layer, ids, gain_ref, shift_ref, biases_ref, stream_hbm, part_hbm, other_hbm, in_hbm_ref, out_hbm_ref, middle_out, half_out, slope_out, partial_out, stream_in, inner, outer, normed, low, slope, partial, sems):
    units = inner.shape[1]
    chunks = [slice(at, at + CHUNK) for at in range(0, units, CHUNK)]
    copies = Copies(sems)
    near = [
        copies.start(source, stream_in.at[i])
        for i, source in enumerate((stream_hbm, part_hbm, other_hbm))
    ]
    weights = [
        (
            copies.start(in_hbm_ref.at[layer, :, chunk], inner.at[:, chunk]),
            copies.start(out_hbm_ref.at[layer, chunk, :], outer.at[chunk, :]),
        )
        for chunk in chunks
    ]
    for copy in near:
        copy.wait()
    middle = stream_in[0] + (stream_in[1] + stream_in[2]) + biases_ref[layer, 0:1, :]
    stream_in[0] = middle
    copies.leave(stream_in.at[0], middle_out)
    normed[...] = normal_of(middle)[0] * gain_ref[layer, 1:2, :] + shift_ref[layer, 1:2, :]
    copies.leave(core_half(normed, ids), half_out)
    low[...] = normed[...].astype(LOW)
    for at, chunk in enumerate(chunks):
        weights[at][0].wait()
        hidden = matmul(low[...], inner[:, chunk])
        rise = 0.5 * (1.0 + lax.erf(hidden * ROOT_HALF))
        slope[:, chunk] = rise + hidden * jnp.exp(-0.5 * hidden * hidden) * SLOPE_NORM
        copies.leave(slope.at[:, chunk], slope_out.at[:, chunk])
        weights[at][1].wait()
        product = matmul((hidden * rise).astype(LOW), outer[chunk, :])
        partial[...] = product if at == 0 else partial[...] + product
    copies.leave(partial, partial_out)
    copies.finish()


def feed(layer, ids, stream, partial, other, biases, gains, shifts, hidden_in, hidden_out, after=()):
    count, width = stream.shape
    units = hidden_in.shape[2]
    full = shape_of((count, width))
    return plain(
        functools.partial(feed_kernel, layer),
        f"feed_{layer}",
        (ids,),
        (gains, shifts, biases),
        (stream, partial, other, hidden_in, hidden_out),
        [full, shape_of((count // 2, width)), shape_of((count, units)), full],
        [
            pltpu.VMEM((3, count, width), FULL),
            pltpu.VMEM((width, units), LOW),
            pltpu.VMEM((units, width), LOW),
            pltpu.VMEM((count, width), FULL),
            pltpu.VMEM((count, width), LOW),
            pltpu.VMEM((count, units), FULL),
            pltpu.VMEM((count, width), FULL),
        ],
        4 * count * width * units,
        4 * width * units + 4 * count * (units + 6 * width),
        48,
        after,
    )


def feed_back_kernel(layer, last, ids, gain_ref, *refs):
    parts = 1 if last else 4
    up_hbm, refs = refs[:parts], refs[parts:]
    slope_hbm, in_hbm_ref, out_hbm_ref, upstream_out, half_out, sums_out, partial_out = refs[:7]
    up_in, inner, outer, upstream, low, slope, sums, partial, sems = refs[7:]
    units = inner.shape[1]
    chunks = [slice(at, at + CHUNK) for at in range(0, units, CHUNK)]
    copies = Copies(sems)
    near = [copies.start(source, up_in.at[i]) for i, source in enumerate(up_hbm)]
    weights = [
        (
            copies.start(out_hbm_ref.at[layer, chunk, :], outer.at[chunk, :]),
            copies.start(slope_hbm.at[:, chunk], slope.at[:, chunk]),
            copies.start(in_hbm_ref.at[layer, :, chunk], inner.at[:, chunk]),
        )
        for chunk in chunks
    ]
    for copy in near:
        copy.wait()
    sums[...] = jnp.zeros_like(sums)
    if last:
        upstream[...] = up_in[0].astype(FULL)
    else:
        step, gain_part, shift_part = norm_backward(
            up_in[3], gain_ref[layer + 1, 0:1, :], up_in[1] + up_in[2]
        )
        upstream[...] = up_in[0] + step
        sums[1:2, :] = gain_part
        sums[2:3, :] = shift_part
    copies.leave(upstream, upstream_out)
    copies.leave(core_half(upstream, ids), half_out)
    low[...] = upstream[...].astype(LOW)
    sums[0:1, :] = jnp.sum(low[...].astype(FULL), axis=0, keepdims=True)
    copies.leave(sums, sums_out)
    for at, chunk in enumerate(chunks):
        weights[at][0].wait()
        back = matmul(low[...], outer[chunk, :], NT)
        weights[at][1].wait()
        weights[at][2].wait()
        product = matmul((back * slope[:, chunk]).astype(LOW), inner[:, chunk], NT)
        partial[...] = product if at == 0 else partial[...] + product
    copies.leave(partial, partial_out)
    copies.finish()


def feed_back(layer, ids, upstream, slope, hidden_in, hidden_out, gains, after=()):
    count, width = upstream[0].shape
    units = hidden_in.shape[2]
    full = shape_of((count, width))
    return plain(
        functools.partial(feed_back_kernel, layer, len(upstream) == 1),
        f"feed_back_{layer}",
        (ids,),
        (gains,),
        (*upstream, slope, hidden_in, hidden_out),
        [full, shape_of((count // 2, width)), shape_of((8, width)), full],
        [
            pltpu.VMEM((len(upstream), count, width), upstream[0].dtype),
            pltpu.VMEM((width, units), LOW),
            pltpu.VMEM((units, width), LOW),
            pltpu.VMEM((count, width), FULL),
            pltpu.VMEM((count, width), LOW),
            pltpu.VMEM((count, units), FULL),
            pltpu.VMEM((8, width), FULL),
            pltpu.VMEM((count, width), FULL),
        ],
        4 * count * width * units,
        4 * width * units + 4 * count * (units + 6 * width),
        48,
        after,
    )


def attend_back_kernel(layer, heads, ids, gain_ref, up_hbm, part_hbm, other_hbm, middle_hbm, row_hbm, bias_hbm, out_hbm, token_hbm, back_out, half_out, sums_out, partial_out, up_in, rows, bias, token, outer, back, sums, upstream, steps, partial, sems):
    copies = Copies(sems)
    near = [
        copies.start(source, up_in.at[i])
        for i, source in enumerate((up_hbm, part_hbm, other_hbm, middle_hbm))
    ]
    outers = copies.start(out_hbm.at[layer], outer)
    saved = [copies.start(row_hbm, rows), copies.start(bias_hbm, bias)]
    tokens = [copies.start(token_hbm.at[layer, member], token.at[member]) for member in range(3)]
    for copy in near:
        copy.wait()
    step, gain_part, shift_part = norm_backward(
        up_in[3], gain_ref[layer, 1:2, :], up_in[1] + up_in[2]
    )
    back[...] = up_in[0] + step
    copies.leave(back, back_out)
    copies.leave(core_half(back, ids), half_out)
    rounded = back[...].astype(LOW)
    sums[...] = jnp.zeros_like(sums)
    sums[0:1, :] = jnp.sum(rounded.astype(FULL), axis=0, keepdims=True)
    sums[1:2, :] = gain_part
    sums[2:3, :] = shift_part
    copies.leave(sums, sums_out)
    outers.wait()
    upstream[...] = matmul(rounded, outer[...], NT).astype(LOW)

    def row(index, first, last):
        return upstream[:, first:last] if index == 3 else rows[index, :, first:last]

    for copy in saved:
        copy.wait()
    attention_backward(heads, row, bias, steps, None, None)
    for member in range(3):
        tokens[member].wait()
        product = matmul(steps[member].astype(LOW), token[member])
        partial[...] = product if member == 0 else partial[...] + product
    copies.leave(partial, partial_out)
    copies.finish()


def attend_back(layer, ids, upstream, partial, other, middle, gains, rows, bias, out_proj, token_rows, after=()):
    count, width = upstream.shape
    local = token_rows.shape[2]
    heads = bias.shape[0]
    full = shape_of((count, width))
    return plain(
        functools.partial(attend_back_kernel, layer, heads),
        f"attend_back_{layer}",
        (ids,),
        (gains,),
        (upstream, partial, other, middle, rows, bias, out_proj, token_rows),
        [full, shape_of((count // 2, width)), shape_of((8, width)), full],
        [
            pltpu.VMEM((4, count, width), FULL),
            pltpu.VMEM((3, count, local), LOW),
            pltpu.VMEM((heads, count, count), FULL),
            pltpu.VMEM((3, local, width), LOW),
            pltpu.VMEM((local, width), LOW),
            pltpu.VMEM((count, width), FULL),
            pltpu.VMEM((8, width), FULL),
            pltpu.VMEM((count, local), LOW),
            pltpu.VMEM((3, count, local), FULL),
            pltpu.VMEM((count, width), FULL),
        ],
        2 * count * width * local * 4 + heads * count * count * 4096,
        8 * width * local + 24 * count * width,
        40,
        after,
    )


def finish_kernel(gain_ref, up_hbm, part_hbm, other_hbm, stream_hbm, gradient_out, sums_out, up_in, gradient, sums, sems):
    copies = Copies(sems)
    near = [
        copies.start(source, up_in.at[i])
        for i, source in enumerate((up_hbm, part_hbm, other_hbm, stream_hbm))
    ]
    for copy in near:
        copy.wait()
    step, gain_part, shift_part = norm_backward(up_in[3], gain_ref[0, 0:1, :], up_in[1] + up_in[2])
    gradient[...] = (up_in[0] + step).astype(LOW)
    copies.leave(gradient, gradient_out)
    sums[...] = jnp.zeros_like(sums)
    sums[1:2, :] = gain_part
    sums[2:3, :] = shift_part
    copies.leave(sums, sums_out)
    copies.finish()


def finish(upstream, partial, other, stream, gains):
    count, width = stream.shape
    return plain(
        finish_kernel,
        "finish",
        (),
        (gains,),
        (upstream, partial, other, stream),
        [shape_of((count, width), LOW), shape_of((8, width))],
        [
            pltpu.VMEM((4, count, width), FULL),
            pltpu.VMEM((count, width), LOW),
            pltpu.VMEM((8, width), FULL),
        ],
        0,
        20 * count * width,
        24,
    )


def line_window(units, line):
    own = units // line
    offsets = [z * own % 128 for z in range(line)]
    size = -(-(max(offsets) + own) // 128) * 128
    starts = [min(z * own // 128 * 128, units - size) for z in range(line)]
    return starts, [z * own - starts[z] for z in range(line)], size


def feed_gradients_kernel(layer, line, ids, x_hbm, y_hbm, in_hbm, out_hbm, outer_keep, outer_send, inner_keep, inner_send, stage, part_in, part_out, low_x, low_y, active, back, outer, inner, sems):
    units = in_hbm.shape[2]
    width = low_x.shape[1]
    rows = stage.shape[2]
    own = units // line
    starts, offsets, size = line_window(units, line)
    at = ids[AT_LINE]
    start, offset = jnp.int32(starts[0]), jnp.int32(offsets[0])
    for z in range(1, line):
        start = jnp.where(at == z, starts[z], start)
        offset = jnp.where(at == z, offsets[z], offset)
    start = pl.multiple_of(start, 128)
    copies = [
        pltpu.make_async_copy(in_hbm.at[layer, :, pl.ds(start, size)], part_in, sems.at[0, 2]),
        pltpu.make_async_copy(out_hbm.at[layer, pl.ds(start, size), :], part_out, sems.at[1, 2]),
    ]

    def fetch(tile):
        slot = tile % 2
        return [
            pltpu.make_async_copy(
                source.at[pl.ds(tile * rows, rows)], stage.at[side, slot], sems.at[side, slot]
            )
            for side, source in enumerate((x_hbm, y_hbm))
        ]

    flying = {0: fetch(0)}
    for copy in (*flying[0], *copies):
        copy.start()
    for tile in range(line):
        if tile + 1 < line:
            flying[tile + 1] = fetch(tile + 1)
            for copy in flying[tile + 1]:
                copy.start()
        for copy in flying[tile]:
            copy.wait()
        if tile == 0:
            for copy in copies:
                copy.wait()
        here = slice(tile * rows, (tile + 1) * rows)
        low_x[here, :] = stage[0, tile % 2].astype(LOW)
        low_y[here, :] = stage[1, tile % 2].astype(LOW)
        hidden = matmul(low_x[here, :], part_in[...])
        rise = 0.5 * (1.0 + lax.erf(hidden * ROOT_HALF))
        active[here, :] = (hidden * rise).astype(LOW)
        slope = rise + hidden * jnp.exp(-0.5 * hidden * hidden) * SLOPE_NORM
        back[here, :] = (matmul(low_y[here, :], part_out[...], NT) * slope).astype(LOW)

    @pl.loop(0, size // 128)
    def _(tile):
        lanes = pl.ds(pl.multiple_of(tile * 128, 128), 128)
        outer[lanes, :] = matmul(active[:, lanes], low_y[...], TN)

    @pl.loop(0, width // 128)
    def _(tile):
        lanes = pl.ds(pl.multiple_of(tile * 128, 128), 128)
        inner[lanes, :] = matmul(low_x[:, lanes], back[...], TN)

    pair = own // 2
    step = width // (GROUP * line)
    for z in range(len(set(offsets))):
        shifted = sorted(set(offsets))[z]
        for col in range(2):

            @pl.when((offset == shifted) & (ids[AT_COL] == col))
            def _(shifted=shifted, col=col):
                for target, part in ((outer_keep, col), (outer_send, 1 - col)):
                    first = shifted + part * pair
                    for r in range(2):
                        begin = first + r * (pair // 2)
                        target[r] = outer[begin : begin + pair // 2, :]

    for row in range(2):

        @pl.when(ids[AT_ROW] == row)
        def _(row=row):
            for z in range(line):
                for c in range(2):
                    for target, part in ((inner_keep, row), (inner_send, 1 - row)):
                        begin = (GROUP * z + 2 * c + part) * step
                        target[c, z] = inner[begin : begin + step, :]


def feed_gradients(layer, line, ids, xs, ys, hidden_in, hidden_out, after=()):
    count, width = xs.shape
    rows = count // line
    units = hidden_in.shape[2]
    own = units // line
    size = line_window(units, line)[2]
    anywhere = pl.BlockSpec(memory_space=pl.ANY)
    outs = [shape_of((2, own // 4, width))] * 2 + [shape_of((2, line, width // (GROUP * line), size))] * 2
    return call(
        functools.partial(feed_gradients_kernel, layer, line),
        f"feed_gradients_{layer}",
        (1,),
        [anywhere] * 2 + [pl.BlockSpec(memory_space=pltpu.HBM)] * 2,
        [whole_once(out.shape) for out in outs],
        outs,
        [
            pltpu.VMEM((2, 2, rows, width), FULL),
            pltpu.VMEM((width, size), LOW),
            pltpu.VMEM((size, width), LOW),
            pltpu.VMEM((line * rows, width), LOW),
            pltpu.VMEM((line * rows, width), LOW),
            pltpu.VMEM((line * rows, size), LOW),
            pltpu.VMEM((line * rows, size), LOW),
            pltpu.VMEM((size, width), FULL),
            pltpu.VMEM((width, size), FULL),
            pltpu.SemaphoreType.DMA((2, 3)),
        ],
        8 * line * rows * width * size,
        8 * line * rows * width + 16 * width * size,
        after=after,
    )(ids, *map(in_hbm, (xs, ys, hidden_in, hidden_out)))


def whole_call(kernel, name, scalars, near, outs, scratch=(), limit=40):
    return pl.pallas_call(
        kernel,
        in_specs=[
            *[pl.BlockSpec(memory_space=pltpu.SMEM)] * len(scalars),
            *[NEAR] * len(near),
        ],
        out_specs=[NEAR] * len(outs),
        out_shape=[pltpu.HBM(out.shape, out.dtype) for out in outs],
        scratch_shapes=list(scratch),
        compiler_params=pltpu.CompilerParams(vmem_limit_bytes=limit << 20),
        cost_estimate=pl.CostEstimate(
            flops=WHOLE_COST, bytes_accessed=WHOLE_COST // 300, transcendentals=0
        ),
        name=name,
    )(*scalars, *map(in_hbm, near))


def feed_halve_kernel(ids, outer_keep, outer_half, inner_keep, inner_half, outer_own, outer_send, inner_own, inner_send):
    row, col = ids[AT_ROW], ids[AT_COL]
    outer_own[...] = outer_keep[row] + outer_half[row]
    outer_send[...] = outer_keep[1 - row] + outer_half[1 - row]
    inner_own[...] = inner_keep[col] + inner_half[col]
    inner_send[...] = inner_keep[1 - col] + inner_half[1 - col]


def feed_deal_kernel(line, ids, inner_own, inner_other, *outs):
    place = ids[AT_LINE]
    for by in range(line):
        to = lax.rem(place + by, line)
        outs[by][...] = inner_own[to] + inner_other[to]


def feed_scatter(layer, ids, pieces, line):
    outer_keep, outer_send, inner_keep, inner_send = pieces
    outer_half, inner_half = yield [swap(outer_send, "col"), swap(inner_send, "row")]
    outer_part, inner_part = shape_of(outer_keep.shape[1:]), shape_of(inner_keep.shape[1:])
    outer_own, outer_send, inner_own, inner_send = whole_call(
        feed_halve_kernel,
        f"feed_halve_{layer}",
        (ids,),
        (outer_keep, outer_half, inner_keep, inner_half),
        [outer_part, outer_part, inner_part, inner_part],
    )
    outer_other, inner_other = yield [swap(outer_send, "row"), swap(inner_send, "col")]
    own, *rest = whole_call(
        functools.partial(feed_deal_kernel, line),
        f"feed_deal_{layer}",
        (ids,),
        (inner_own, inner_other),
        [shape_of(inner_own.shape[1:])] * line,
    )
    far = yield [shift(rest[by - 1], line, by) for by in range(1, line)]
    return [own, *far], [outer_own, outer_other]


def attention_deal_kernel(layer, line, heads, at_rows, ids, summed, embedded, *refs):
    images, projection, outs = refs[:line], refs[line], refs[line + 1 :]
    own = images[0].shape[1]
    chunk, lanes, left = at_rows.chunk, at_rows.LANES, at_rows.left
    features = chunk // GROUP
    for third in range(3):
        row = at_rows.projection + third * at_rows.piece
        projection[:, third * lanes : (third + 1) * lanes] = summed[row : row + at_rows.piece, :]
    time = []
    for member in range(2):
        every = jnp.concatenate(
            [ref[member * GROUP * IMAGES : (member + 1) * GROUP * IMAGES, :] for ref in images],
            axis=0,
        )
        high = every.astype(LOW)
        middle = (every - high.astype(FULL)).astype(LOW)
        low = (every - high.astype(FULL) - middle.astype(FULL)).astype(LOW)
        time.append(
            matmul(embedded[...], high, TN)
            + (matmul(embedded[...], middle, TN) + matmul(embedded[...], low, TN))
        )
    at = 2 * ids[AT_COL] + ids[AT_ROW]
    entries = 4 * SPAN // line // GROUP
    fold = chunk // at_rows.folds
    for j in range(GROUP):

        @pl.when(at == j)
        def _(j=j):
            for by in range(GROUP):
                to, out = j ^ by, outs[by]
                here = slice(to * features, (to + 1) * features)
                out[:features, :lanes] = summed[here, :]
                for i in range(at_rows.folds):
                    first, last = max(i * fold, here.start), min((i + 1) * fold, here.stop)
                    if first < last:
                        row = at_rows.folded - i * fold
                        out[first - here.start : last - here.start, lanes : 3 * own] = summed[
                            row + first : row + last, i * left : (i + 1) * left
                        ]
                for member in range(2):
                    out[:features, (3 + member) * own : (4 + member) * own] = time[member][here]
                out[features:, :] = jnp.zeros((out.shape[0] - features, 5 * own), FULL)
                out[features : features + heads, :entries] = summed[
                    at_rows.table : at_rows.table + heads, to * entries : (to + 1) * entries
                ]
                if layer == 0:
                    first = features + TABLE_ROWS
                    out[first : first + VECTORS, :features] = summed[
                        at_rows.vectors : at_rows.vectors + VECTORS, here
                    ]


def attention_deal(layer, line, ids, summed, embedded, images, heads, width, own):
    at_rows = Rows(own, width, heads, VECTORS if layer == 0 else 0, line)
    rows = width // line // GROUP + TABLE_ROWS + (VECTOR_ROWS if layer == 0 else 0)
    projection, *blocks = whole_call(
        functools.partial(attention_deal_kernel, layer, line, heads, at_rows),
        f"attention_deal_{layer}",
        (ids,),
        (summed, embedded, *images),
        [shape_of((own // line, width))] + [shape_of((rows, 5 * own))] * GROUP,
    )
    moved = lax.ppermute(
        projection,
        LINES,
        [(GROUP * z + j, line * j + z) for z in range(line) for j in range(GROUP)],
    )
    projection, across, along, corner = yield [
        moved,
        swap(blocks[1], "row"),
        swap(blocks[2], "col"),
        swap_corner(blocks[3]),
    ]
    return projection, [blocks[0], across, along, corner]


def assemble_kernel(depth, line, heads, ids, *refs):
    blocks, refs = refs[: depth * GROUP], refs[depth * GROUP :]
    projections, refs = refs[:depth], refs[depth:]
    inners, refs = refs[: depth * line], refs[depth * line :]
    outers, refs = refs[: 2 * depth], refs[2 * depth :]
    token, time, table, projection, inner, outer, gain, shift_out, bias, sorted_inner = refs
    features, local = token.shape[2:]
    own = local // GROUP
    units = inner.shape[2]
    part = units // line
    offsets = line_window(units, line)[1]
    entries = table.shape[2]
    at = 2 * ids[AT_COL] + ids[AT_ROW]
    place = ids[AT_LINE]
    for layer in range(depth):
        projection[layer] = projections[layer][...]
        outer[layer] = outers[2 * layer][...] + outers[2 * layer + 1][...]
        for by in range(line):
            sorted_inner[lax.rem(place + line - by, line)] = inners[layer * line + by][...]
        for z in range(line):
            inner[layer, :, z * part : (z + 1) * part] = sorted_inner[
                z, :, offsets[z] : offsets[z] + part
            ]
        for j in range(GROUP):

            @pl.when(at == j)
            def _(j=j, layer=layer):
                for by in range(GROUP):
                    ref, source = blocks[layer * GROUP + by], j ^ by
                    lanes = slice(source * own, (source + 1) * own)
                    for member in range(3):
                        token[layer, member, :, lanes] = ref[
                            :features, member * own : (member + 1) * own
                        ]
                    for member in range(2):
                        time[layer, member, :, lanes] = ref[
                            :features, (3 + member) * own : (4 + member) * own
                        ]
                    table[layer, source * heads : (source + 1) * heads, :] = ref[
                        features : features + heads, :entries
                    ]

    first = features + TABLE_ROWS
    total = functools.reduce(
        jnp.add, [blocks[by][first : first + 6 * depth, :features] for by in range(GROUP)]
    )
    for kind, out in enumerate((gain, shift_out, bias)):
        for layer in range(depth):
            begin = (kind * depth + layer) * 2
            out[layer] = total[begin : begin + 2]


def assemble(depth, line, ids, attention, feeds, heads, local, units, width):
    features = width // (GROUP * line)
    vector = shape_of((depth, 2, features))
    size = line_window(units, line)[2]
    return whole_call(
        functools.partial(assemble_kernel, depth, line, heads // GROUP),
        "assemble",
        (ids,),
        (
            *[block for layer in range(depth) for block in attention[layer][1]],
            *[attention[layer][0] for layer in range(depth)],
            *[block for layer in range(depth) for block in feeds[layer][0]],
            *[part for layer in range(depth) for part in feeds[layer][1]],
        ),
        [
            shape_of((depth, 3, features, local)),
            shape_of((depth, 2, features, local)),
            shape_of((depth, heads, 4 * SPAN // (GROUP * line))),
            shape_of((depth, local // (GROUP * line), width)),
            shape_of((depth, features, units)),
            shape_of((depth, units // (GROUP * line), width)),
            vector,
            vector,
            vector,
        ],
        [pltpu.VMEM((line, features, size), FULL)],
    )


class Rows:
    LANES = 384

    def __init__(self, own, width, heads, vectors, line):
        self.chunk, self.piece = width // line, own // line
        self.left = 3 * own - self.LANES
        self.folds = self.LANES // self.left
        self.folded = self.chunk
        self.projection = self.folded + self.chunk // self.folds
        self.table = self.projection + 3 * self.piece
        self.vectors = self.table + heads
        self.total = -(-(self.vectors + vectors) // 8) * 8


VECTORS = 12
TABLE_ROWS, VECTOR_ROWS = 8, 16


def attention_gradients_kernel(layer, heads, line, vector_count, ids, kinds, *refs):
    parts = 2 * GROUP - 1
    sources = refs[:parts], refs[parts : 2 * parts]
    token_hbm, out_hbm = refs[2 * parts : 2 * parts + 2]
    image_hbm = refs[2 * parts + 2 : 2 * parts + 2 + GROUP]
    refs = refs[2 * parts + 2 + GROUP :]
    wide_ref, small_ref = refs[:2]
    vectors, refs = refs[2 : 2 + vector_count], refs[2 + vector_count :]
    token_out, images_out = refs[:2]
    (images, low_x, low_y, joined, attended_low, rows, bias, steps, attended) = refs[2:11]
    wide_sum, small_sum, stage, token, outer, scores, image_all, sems, weight_sems = refs[11:]
    slot = pl.program_id(0)
    kind = kinds[slot]
    count = low_x.shape[1]
    half = count // 2
    own = images.shape[2]
    at = 2 * ids[AT_COL] + ids[AT_ROW]

    def fetch(near):
        if near == 0:
            return [
                pltpu.make_async_copy(sources[side][0], stage.at[side, 0], sems.at[side, 0])
                for side in range(2)
            ]
        return [
            pltpu.make_async_copy(
                sources[side][(far + 1) * (GROUP - 1) + near - GROUP + 1],
                stage.at[side, near, pl.ds(pl.multiple_of(place * half, half), half)],
                sems.at[side, 2 * near + far - 1],
            )
            for side in range(2)
            for far, place in enumerate((ids[AT_CORE], 1 - ids[AT_CORE]))
        ]

    mine = pl.ds(pl.multiple_of(at * own, 16), own)
    weights = [
        pltpu.make_async_copy(token_hbm.at[layer, :, mine, :], token, weight_sems.at[0]),
        pltpu.make_async_copy(out_hbm.at[layer, mine, :], outer, weight_sems.at[1]),
        *[
            pltpu.make_async_copy(image_hbm[near], image_all.at[near], weight_sems.at[2 + near])
            for near in range(GROUP)
        ],
    ]

    @pl.when(slot == 0)
    def _():
        for copy in (*fetch(0), *weights):
            copy.start()
        for near in range(1, GROUP):
            for copy in fetch(near):
                copy.start()
        wide_sum[...] = jnp.zeros_like(wide_sum)
        small_sum[...] = jnp.zeros_like(small_sum)
    for near in range(GROUP):

        @pl.when(slot == near)
        def _(near=near):
            for copy in fetch(near):
                copy.wait()

    @pl.when(slot == 0)
    def _():
        for copy in weights:
            copy.wait()
        for j in range(GROUP):

            @pl.when(at == j)
            def _(j=j):
                for member in range(2):
                    first = (2 * layer + member) * IMAGES
                    for near in range(GROUP):
                        images[member, near * IMAGES : (near + 1) * IMAGES, :] = image_all[
                            near, first : first + IMAGES, j * own : (j + 1) * own
                        ]

    fill_bias(heads, kind, wide_ref, small_ref, bias)
    low_x[slot] = stage[0, slot].astype(LOW)
    low_y[slot] = stage[1, slot].astype(LOW)
    for member in range(3):
        projected = matmul(low_x[slot], token[member], NT)
        for i in range(IMAGES):
            here = slice(i * (count // IMAGES), (i + 1) * (count // IMAGES))
            if member == 1:
                rows[member, here, :] = projected[here].astype(LOW)
            else:
                near = images[member // 2]
                first = near[0:1, :]
                mine = near[i : i + 1, :]
                for other in range(1, GROUP):
                    begin = other * IMAGES
                    first = jnp.where(slot == other, near[begin : begin + 1, :], first)
                    mine = jnp.where(slot == other, near[begin + i : begin + i + 1, :], mine)
                mine = jnp.where(kind != 0, mine, first)
                rows[member, here, :] = (projected[here] + mine).astype(LOW)
    rows[3] = matmul(low_y[slot], outer[...], NT).astype(LOW)

    def row(index, first, last):
        return rows[index, :, first:last]

    attention_backward(heads, row, bias, steps, attended, scores)
    collect_table(heads, kind, scores, wide_sum, small_sum)
    attended_low[slot] = attended[...].astype(LOW)
    for member in range(3):
        rounded = steps[member].astype(LOW)
        joined[slot, :, member * own : (member + 1) * own] = rounded
        if member != 1:
            sums = [
                jnp.sum(
                    rounded[i * (count // IMAGES) : (i + 1) * (count // IMAGES)].astype(FULL),
                    axis=0,
                    keepdims=True,
                )
                for i in range(IMAGES)
            ]
            everything = sums[0] + sums[1] + sums[2] + sums[3]
            for i in range(IMAGES):
                alone = everything if i == 0 else jnp.zeros_like(everything)
                images_out[0, member // 2, i : i + 1, :] = jnp.where(kind != 0, sums[i], alone)

    @pl.when(slot == GROUP - 1)
    def _():
        flat = GROUP * count
        width = low_x.shape[2]

        product = matmul(low_x[...].reshape(flat, width), joined[...].reshape(flat, -1), TN)
        projection = matmul(
            attended_low[...].reshape(flat, -1), low_y[...].reshape(flat, -1), TN
        )
        tables = [fold_table(wide_sum[head], small_sum[head]) for head in range(heads)]
        size, cells = width // 3, 4 * SPAN // line
        at_rows = Rows(own, width, heads, VECTORS if vectors else 0, line)
        chunk, lanes, left = at_rows.chunk, at_rows.LANES, at_rows.left
        fold = chunk // at_rows.folds
        for z in range(line):
            begin = z * at_rows.total
            token_out[begin : begin + chunk, :] = product[z * chunk : (z + 1) * chunk, :lanes]
            row = begin + at_rows.folded
            for i in range(at_rows.folds):
                first = z * chunk + i * fold
                token_out[row : row + fold, i * left : (i + 1) * left] = product[
                    first : first + fold, lanes:
                ]
            for third in range(3):
                row = begin + at_rows.projection + third * at_rows.piece
                token_out[row : row + at_rows.piece, :] = projection[
                    z * at_rows.piece : (z + 1) * at_rows.piece, third * size : (third + 1) * size
                ]
            row = begin + at_rows.table
            token_out[row : begin + at_rows.total, :] = jnp.zeros(
                (at_rows.total - at_rows.table, lanes), FULL
            )
            for head in range(heads):
                token_out[row + head : row + head + 1, :cells] = tables[head][
                    :, z * cells : (z + 1) * cells
                ]
            row = begin + at_rows.vectors
            for i, (ref, r) in enumerate(vector_places(vectors)):
                token_out[row + i : row + i + 1, :chunk] = ref[
                    r : r + 1, z * chunk : (z + 1) * chunk
                ]


def vector_places(vectors):
    if not vectors:
        return []
    depth = (len(vectors) - 1) // 2
    feeds, middles = vectors[1 : 1 + depth], vectors[1 + depth :]
    firsts = [vectors[0], *feeds]
    return (
        [place for l in range(depth) for place in ((firsts[l], 1), (middles[l], 1))]
        + [place for l in range(depth) for place in ((firsts[l], 2), (middles[l], 2))]
        + [place for l in range(depth) for place in ((middles[l], 0), (feeds[l], 0))]
    )


def attention_gradients(layer, line, ids, kinds, near_x, near_y, token_rows, images, out_proj, wide, small, vectors, after=()):
    count, width = near_x[0].shape
    depth, _, local, _ = token_rows.shape
    own, heads = local // GROUP, wide.shape[0] // depth // GROUP
    near = [HBM] * (len(near_x) + len(near_y))
    at_rows = Rows(own, width, heads, VECTORS if vectors else 0, line)

    def own_heads(slot, ids, kinds):
        return (layer * GROUP + 2 * ids[AT_COL] + ids[AT_ROW], 0, 0)

    outs = [
        shape_of((line * at_rows.total, at_rows.LANES)),
        shape_of((GROUP, 2, IMAGES, own)),
    ]
    return call(
        functools.partial(attention_gradients_kernel, layer, heads, line, len(vectors)),
        f"attention_gradients_{layer}",
        (GROUP,),
        [
            *near,
            *[HBM] * (2 + GROUP),
            pl.BlockSpec((heads, *wide.shape[1:]), own_heads),
            pl.BlockSpec((heads, *small.shape[1:]), own_heads),
            *[whole(vector.shape) for vector in vectors],
        ],
        [
            whole_once(outs[0].shape),
            pl.BlockSpec((1, 2, IMAGES, own), lambda s, ids, kinds: (s, 0, 0, 0)),
        ],
        outs,
        [
            pltpu.VMEM((2, GROUP * IMAGES, own), FULL),
            pltpu.VMEM((GROUP, count, width), LOW),
            pltpu.VMEM((GROUP, count, width), LOW),
            pltpu.VMEM((GROUP, count, 3 * own), LOW),
            pltpu.VMEM((GROUP, count, own), LOW),
            pltpu.VMEM((4, count, own), LOW),
            pltpu.VMEM((heads, count, count), FULL),
            pltpu.VMEM((3, count, own), FULL),
            pltpu.VMEM((count, own), FULL),
            pltpu.VMEM((heads, *wide.shape[1:]), FULL),
            pltpu.VMEM((heads, *small.shape[1:]), FULL),
            pltpu.VMEM((2, GROUP, count, width), FULL),
            pltpu.VMEM((3, own, width), LOW),
            pltpu.VMEM((own, width), LOW),
            pltpu.VMEM((heads, count, count), FULL),
            pltpu.VMEM((GROUP, *images[0].shape), FULL),
            pltpu.SemaphoreType.DMA((2, 2 * GROUP)),
            pltpu.SemaphoreType.DMA((2 + GROUP,)),
        ],
        2 * GROUP * count * width * own * 8 + GROUP * heads * count * count * 4096,
        8 * GROUP * count * width + 8 * width * local,
        2,
        after,
    )(
        ids, kinds, *map(in_hbm, (*near_x, *near_y, token_rows, out_proj, *images)), wide, small, *vectors
    )


def swap(value, axis):
    return lax.ppermute(value, axis, [(0, 1), (1, 0)])


def shift(value, line, by=1):
    return lax.ppermute(value, "line", [(i, (i + by) % line) for i in range(line)])


def gather_line(half):
    return lax.all_gather(half, ("line", "tensor"), tiled=True)


def plane_steps(value, half):
    across, along = yield [swap(half, "row"), swap(half, "col")]
    corner, *others = yield [swap_corner(half), swap(across, "tensor"), swap(along, "tensor")]
    others += yield [swap(corner, "tensor")]
    return [value, across, along, corner, *others]


def swap_corner(value):
    return lax.ppermute(value, ("col", "row"), [(0, 3), (3, 0), (1, 2), (2, 1)])


def plane_all(value):
    across, along, corner = yield [swap(value, "row"), swap(value, "col"), swap_corner(value)]
    return [value, across, along, corner]


def line_all(value, line):
    far = yield [shift(value, line, by) for by in range(1, line)]
    return [value, *far]


def local(
    tokens,
    segment_ids,
    timesteps,
    norm_gain,
    norm_bias,
    token_proj,
    time_proj,
    bias_table,
    out_proj,
    hidden_in,
    hidden_out,
    branch_bias,
    cotangent,
    *,
    line,
):
    count, width = tokens.shape
    depth, _, _, local_width = token_proj.shape
    heads = bias_table.shape[1]
    units = hidden_in.shape[2]
    own = local_width // GROUP
    n_dp = GROUP * line
    features = width // n_dp
    line_at = lax.axis_index("line")
    ids = jnp.stack(
        [segment_ids[-1], line_at, lax.axis_index("col"), lax.axis_index("row"), lax.axis_index("tensor")]
    ).astype(jnp.int32)
    embedded = sinusoid(timesteps[0], jnp.arange(width, dtype=jnp.int32), width)
    per_image = lax.dot_general(
        time_proj, embedded, (((2,), (1,)), ((), ())), preferred_element_type=FULL
    )
    per_image = jnp.swapaxes(per_image, 2, 3)
    info = jnp.concatenate([timesteps[0], segment_ids[-1:]]).astype(FULL)
    packed = jnp.concatenate(
        [
            per_image.reshape(2 * depth * IMAGES, local_width),
            jnp.pad(info[None], ((0, 7), (0, local_width - IMAGES - 1))),
        ]
    )
    own_feature = line_at * (GROUP * features) + jnp.arange(GROUP * features, dtype=jnp.int32)
    token_rows = jnp.swapaxes(token_proj, 2, 3)
    wide, small = expand_table(bias_table.reshape(depth * heads, -1))

    stream = (tokens,)
    saved = []
    moves = Moves()
    moves.start("packed", plane_all(packed))
    half = lax.dynamic_slice_in_dim(cotangent, lax.axis_index("tensor") * (count // 2), count // 2, 0)
    gathered_up = gather_line(half.astype(FULL))
    for layer in range(depth):
        held, normed, half, rows, partial, bias = attend(
            layer, ids, stream, norm_gain, norm_bias, branch_bias, token_rows, per_image, out_proj, wide, small
        )
        if layer == depth - 1:
            partial, other, gathered_up = moves.chain(partial, [gathered_up])
        else:
            partial, other = moves.chain(partial)
        moves.start(("first", layer), plane_steps(normed, half))
        if layer == depth - 1:
            near = jnp.stack(
                [part[2 * depth * IMAGES, : IMAGES + 1] for part in moves.found["packed"]]
            )
            kinds = near[:, IMAGES].astype(jnp.int32)
            info = jnp.pad(near, ((0, 8 - GROUP), (0, 128 - IMAGES - 1)))
            moves.start("info", line_all(info, line))
        middle, half_second, slope, partial = feed(
            layer,
            ids,
            held,
            partial,
            other,
            branch_bias,
            norm_gain,
            norm_bias,
            hidden_in,
            hidden_out,
        )
        partial, other = moves.chain(partial)
        line_second = gather_line(half_second)
        saved.append((held, rows, middle, slope, line_second, bias))
        stream = (middle, partial, other)
    output = (stream[0] + (stream[1] + stream[2]) + branch_bias[depth - 1, 1]).astype(LOW)

    upstream = (cotangent,)
    collected = [None] * depth
    vectors = [None] * depth
    gathered = [None] * depth
    gathered_line = [None] * depth
    for layer in reversed(range(depth)):
        held, rows, middle, slope, _, bias = saved[layer]
        current, half_up, feed_sums, partial = feed_back(
            layer, ids, upstream, slope, hidden_in, hidden_out, norm_gain
        )
        partial, other = moves.chain(partial)
        if layer < depth - 1:
            gathered_up = gather_line(half_up)
        back_middle, half, middle_sums, back_partial = attend_back(
            layer,
            ids,
            current,
            partial,
            other,
            middle,
            norm_gain,
            rows,
            bias,
            out_proj,
            token_rows,
        )
        if layer > 0:
            back_partial, other, gathered_line[0] = moves.chain(back_partial, [saved[0][4]])
        else:
            back_partial, other = moves.chain(back_partial)
        moves.start(("branch", layer), plane_steps(back_middle, half))
        upstream = (back_middle, back_partial, other, held)
        vectors[layer] = (feed_sums, middle_sums)
        gathered[layer] = gathered_up
    gradient_tokens, last_sums = finish(*upstream, norm_gain)
    sums = [last_sums, *[pair[0] for pair in vectors], *[pair[1] for pair in vectors]]
    packed = moves.found["packed"]
    tokens_of = {}


    def run_feed(layer, turn, due=()):
        pieces = feed_gradients(
            layer, line, ids, gathered_line[layer], gathered[layer], hidden_in, hidden_out, after=turn
        )
        turn, *due = moves.kernel(pieces[0], due)
        moves.start(("feed", layer), feed_scatter(layer, ids, (turn, *pieces[1:]), line))
        return turn, due

    def run_attention(layer, turn, due=()):
        token, found = attention_gradients(
            layer,
            line,
            ids,
            kinds,
            moves.found["first", layer],
            moves.hurry(("branch", layer)),
            token_rows,
            packed,
            out_proj,
            wide,
            small,
            sums if layer == 0 else (),
            after=turn,
        )
        turn, *due = moves.kernel(found, due)
        tokens_of[layer] = lax.psum_scatter(token, "line", scatter_dimension=0, tiled=True)
        moved = jnp.swapaxes(turn, 0, 1).reshape(2 * GROUP * IMAGES, own)
        moves.start(("images", layer), line_all(moved, line))
        return turn, due

    top = depth - 1
    turn, (gathered_line[top],) = run_attention(top, (), [saved[top][4]])
    turn, (gathered[0],) = run_feed(top, (turn,), [gathered[0]])
    turn, _ = run_feed(0, (turn,))
    _, (tokens_of[top],) = run_attention(0, (turn,), [tokens_of[top]])
    every = jnp.concatenate([part[:GROUP, :IMAGES].reshape(-1) for part in moves.found["info"]])
    embedded_every = sinusoid(every, own_feature, width)
    def deal(layer):
        moves.start(
            ("attention", layer),
            attention_deal(
                layer,
                line,
                ids,
                tokens_of[layer],
                embedded_every,
                moves.hurry(("images", layer)),
                heads // GROUP,
                width,
                own,
            ),
        )

    for layer in range(1, depth):
        deal(layer)
    moves.hurry(("images", 0))
    moves.finish()
    others = [moves.found["feed", 0], moves.found["attention", depth - 1]]
    held, others = jax.tree.flatten(others)
    tokens_of[0], *held = gate([tokens_of[0], *held])
    moves.found["feed", 0], moves.found["attention", depth - 1] = jax.tree.unflatten(others, held)
    deal(0)
    moves.finish()
    token, time, table, projection, inner, outer, gain, shifts, bias = assemble(
        depth,
        line,
        ids,
        [moves.found["attention", layer] for layer in range(depth)],
        [moves.found["feed", layer] for layer in range(depth)],
        heads,
        local_width,
        units,
        width,
    )
    return (
        output,
        gradient_tokens,
        gain,
        shifts,
        token,
        time,
        table,
        projection,
        inner,
        outer,
        bias,
    )


def solution(mesh):
    line = mesh.shape["dp"] // GROUP
    fine = Mesh(mesh.devices.reshape(line, 2, 2, mesh.shape["tensor"]), (*LINES, "tensor"))
    return jax.shard_map(
        functools.partial(local, line=line),
        mesh=fine,
        in_specs=(
            P(LINES, None),
            P(LINES),
            P(LINES, None),
            P(),
            P(),
            P(None, None, None, "tensor"),
            P(None, None, None, "tensor"),
            P(None, "tensor", None),
            P(None, "tensor", None),
            P(None, None, "tensor"),
            P(None, "tensor", None),
            P(),
            P(LINES, None),
        ),
        out_specs=(
            P(LINES, None),
            P(LINES, None),
            P(None, None, LINES),
            P(None, None, LINES),
            P(None, None, LINES, "tensor"),
            P(None, None, LINES, "tensor"),
            P(None, "tensor", LINES),
            P(None, ("tensor", *LINES), None),
            P(None, LINES, "tensor"),
            P(None, ("tensor", *LINES), None),
            P(None, None, LINES),
        ),
        check_vma=False,
    )
```

```python
import functools
import math

import jax
import jax.numpy as jnp
from jax import lax
from jax.experimental import pallas as pl
from jax.experimental.pallas import tpu as pltpu
from jax.sharding import Mesh
from jax.sharding import PartitionSpec as P

SIDE = 16
HALF = 8
SPAN = SIDE * SIDE
IMAGES = 4
BLOCK = SPAN // IMAGES
GROUP = 4
WEIGHT, GRADIENT_WEIGHT, WHOLE_COST = 10, 6, 20_000_000_000
EPSILON = 1e-06
MASKED = -1e30
ROOT_HALF = 0.7071067811865476
SLOPE_NORM = 0.3989422804014327
LINES = ("line", "col", "row")
LOW = jnp.bfloat16
FULL = jnp.float32
KIND, AT_LINE, AT_COL, AT_ROW, AT_CORE = range(5)


def matmul(left, right, dims=((1,), (0,))):
    return lax.dot_general(left, right, (dims, ((), ())), preferred_element_type=FULL)


NT = ((1,), (1,))
TN = ((0,), (0,))


def normal_of(stream):
    center = stream - jnp.mean(stream, axis=-1, keepdims=True)
    inverse = lax.rsqrt(jnp.mean(center * center, axis=-1, keepdims=True) + EPSILON)
    return center * inverse, inverse


def norm_backward(stream, gain, upstream):
    normal, inverse = normal_of(stream)
    gain_part = jnp.sum(upstream * normal, axis=0, keepdims=True)
    shift_part = jnp.sum(upstream, axis=0, keepdims=True)
    scaled = upstream * gain
    inner = (
        scaled
        - jnp.mean(scaled, axis=-1, keepdims=True)
        - normal * jnp.mean(scaled * normal, axis=-1, keepdims=True)
    )
    return inner * inverse, gain_part, shift_part


def sinusoid(steps, feature, width):
    half = width // 2
    rates = jnp.exp(-math.log(10000.0) * (feature % half).astype(FULL) / half)
    angles = steps.astype(FULL)[:, None] * rates[None, :]
    wave = jnp.where(feature[None, :] < half, jnp.cos(angles), jnp.sin(angles))
    return wave.astype(LOW)


def whole(shape):
    return pl.BlockSpec(shape, lambda *_: (0,) * len(shape))


def whole_once(shape):
    return pl.BlockSpec(shape, lambda *_: (0,) * len(shape), pipeline_mode=pl.Buffered(1))


def call(kernel, name, grid, in_specs, out_specs, out_shape, scratch, flops, size, scalars=1, after=()):
    first = scalars + len(in_specs)

    def body(*refs):
        kernel(*refs[:first], *refs[first + len(after) :])

    made = pl.pallas_call(
        body,
        grid_spec=pltpu.PrefetchScalarGridSpec(
            num_scalar_prefetch=scalars,
            grid=grid,
            in_specs=[*in_specs, *[pl.BlockSpec(memory_space=pl.ANY)] * len(after)],
            out_specs=out_specs,
            scratch_shapes=scratch,
        ),
        out_shape=[pltpu.HBM(out.shape, out.dtype) for out in out_shape],
        compiler_params=pltpu.CompilerParams(vmem_limit_bytes=40 << 20),
        cost_estimate=pl.CostEstimate(
            flops=int(flops * GRADIENT_WEIGHT), bytes_accessed=int(size * GRADIENT_WEIGHT), transcendentals=0
        ),
        name=name,
    )
    return lambda *operands: made(*operands, *map(in_hbm, after))


def shape_of(shape, kind=FULL):
    return jax.ShapeDtypeStruct(shape, kind)


def regroup(value, pieces):
    lane = lax.broadcasted_iota(jnp.int32, (value.shape[0], 128), 1)
    total = jnp.zeros((value.shape[0], 128), FULL)
    for tile, source, place, lanes in pieces:
        part = value[:, tile * 128 : tile * 128 + 128]
        turn = (place - source) % 128
        part = part if turn == 0 else pltpu.roll(part, turn, 1)
        total = jnp.where((lane >= place) & (lane < place + lanes), part, total)
    return total


def expand_kernel(table_ref, wide_ref, small_ref):
    size = table_ref.shape[1]
    table = table_ref[...]
    for c in range(SIDE):
        turned = pltpu.roll(table, size - SIDE + c, 1)
        wide = jnp.concatenate(
            [
                regroup(
                    turned,
                    [(2 * o + p // 4, 32 * (p % 4), 16 * p, 16) for p in range(8)],
                )
                for o in range(4)
            ],
            axis=1,
        )
        wide_ref[:, c, :] = wide
        if c < HALF:
            small_ref[:, c, :] = regroup(
                wide, [(1 + k // 8, 16 * (k % 8), 8 * k, 8) for k in range(16)]
            )


def expand_table(table):
    rows, size = table.shape
    return pl.pallas_call(
        expand_kernel,
        out_shape=[shape_of((rows, SIDE, size // 2)), shape_of((rows, HALF, size // 8))],
        name="expand_table",
    )(table)


def fold_table(wide, small):
    inner = jnp.concatenate([small, jnp.zeros_like(small)], axis=0)
    tiles = [wide[:, 128 * t : 128 * t + 128] for t in range(4)]
    for t in range(2):
        tiles[1 + t] = tiles[1 + t] + regroup(
            inner, [(0, 8 * (8 * t + q), 16 * q, 8) for q in range(8)]
        )
    wide = jnp.concatenate(tiles, axis=1)
    spread = jnp.concatenate(
        [
            regroup(
                wide,
                [(o // 2, 64 * (o % 2) + 16 * q, 32 * q, 16) for q in range(4)],
            )
            for o in range(8)
        ],
        axis=1,
    )
    return functools.reduce(
        jnp.add, [pltpu.roll(spread[c : c + 1], SIDE - c, 1) for c in range(SIDE)]
    )


def fill_bias(heads, kind, wide_ref, small_ref, bias):
    @pl.when(kind == 0)
    def _():
        for head in range(heads):
            wide = wide_ref[head]
            for r in range(SIDE):
                turned = pltpu.roll(wide, 2 * SPAN - SIDE * (SIDE - r), 1)
                bias[head, r * SIDE : (r + 1) * SIDE, :] = turned[:, :SPAN]

    @pl.when(kind != 0)
    def _():
        image = lax.broadcasted_iota(jnp.int32, (HALF, SPAN), 1) // BLOCK
        lane = lax.broadcasted_iota(jnp.int32, (HALF, 2 * BLOCK), 1)
        for head in range(heads):
            small = small_ref[head]
            for r in range(HALF):
                turned = pltpu.roll(small, 2 * BLOCK - HALF * (HALF - r), 1)
                turned = jnp.where(lane < BLOCK, turned, 0.0)
                pair = turned + pltpu.roll(turned, BLOCK, 1)
                line = jnp.concatenate([pair, pair], axis=1)
                for i in range(IMAGES):
                    start = i * BLOCK + r * HALF
                    bias[head, start : start + HALF, :] = jnp.where(image == i, line, MASKED)


def collect_table(heads, kind, back, wide_sum, small_sum):
    @pl.when(kind == 0)
    def _():
        for head in range(heads):
            total = wide_sum[head]
            for r in range(SIDE):
                part = back[head, r * SIDE : (r + 1) * SIDE, :]
                part = jnp.concatenate([part, jnp.zeros_like(part)], axis=1)
                total = total + pltpu.roll(part, SIDE * (SIDE - r), 1)
            wide_sum[head] = total

    @pl.when(kind != 0)
    def _():
        for head in range(heads):
            total = small_sum[head]
            lane = lax.broadcasted_iota(jnp.int32, total.shape, 1)
            for r in range(HALF):
                part = functools.reduce(
                    jnp.add,
                    [
                        back[head, i * BLOCK + r * HALF : i * BLOCK + (r + 1) * HALF, :]
                        for i in range(IMAGES)
                    ],
                )
                part = part[:, : SPAN // 2] + part[:, SPAN // 2 :]
                part = jnp.where(lane < BLOCK, part + pltpu.roll(part, BLOCK, 1), 0.0)
                total = total + pltpu.roll(part, HALF * (HALF - r), 1)
            small_sum[head] = total


def window_of(head, head_dim, width):
    if width <= 256:
        return 0, width
    return head * head_dim // 128 * 128, min(-(-(head + 1) * head_dim // 128) * 128, width)


def mine_of(head, head_dim, first, last, rows):
    lane = lax.broadcasted_iota(jnp.int32, (rows, last - first), 1) + first
    return (lane >= head * head_dim) & (lane < (head + 1) * head_dim)


def softmax_of(queries, keys, bias, scale):
    scores = matmul(keys, queries, NT) * scale + bias
    expo = jnp.exp(scores - jnp.max(scores, axis=0, keepdims=True))
    return expo * (1.0 / jnp.sum(expo, axis=0, keepdims=True))


def attention_forward(heads, row, bias, total):
    count, width = total.shape
    head_dim = width // heads
    scale = 1.0 / math.sqrt(head_dim)
    zero = jnp.zeros((), LOW)
    total[...] = jnp.zeros_like(total)
    for head in range(heads):
        first, last = window_of(head, head_dim, width)
        mine = mine_of(head, head_dim, first, last, count)
        queries = jnp.where(mine, row(0, first, last), zero)
        values = jnp.where(mine, row(2, first, last), zero)
        weights = softmax_of(queries, row(1, first, last), bias[head], scale)
        total[:, first:last] += matmul(weights.astype(LOW), values, TN)


def attention_backward(heads, row, bias, steps, attended, scores_out):
    count, width = steps.shape[1:]
    head_dim = width // heads
    scale = 1.0 / math.sqrt(head_dim)
    zero = jnp.zeros((), LOW)
    steps[...] = jnp.zeros_like(steps)
    if attended is not None:
        attended[...] = jnp.zeros_like(attended)
    for head in range(heads):
        first, last = window_of(head, head_dim, width)
        mine = mine_of(head, head_dim, first, last, count)
        queries, keys, values, upstream = (
            jnp.where(mine, row(member, first, last), zero) for member in range(4)
        )
        weights = softmax_of(queries, keys, bias[head], scale)
        low = weights.astype(LOW)
        back_weights = matmul(values, upstream, NT)
        inner = jnp.sum(weights * back_weights, axis=0, keepdims=True)
        back_scores = (weights * (back_weights - inner)).astype(LOW)
        steps[0, :, first:last] += matmul(back_scores, keys, TN) * scale
        steps[1, :, first:last] += matmul(back_scores, queries) * scale
        steps[2, :, first:last] += matmul(low, upstream)
        if attended is not None:
            attended[:, first:last] += matmul(low, values, TN)
        if scores_out is not None:
            scores_out[head] = back_scores.astype(FULL)


def in_hbm(value):
    return pltpu.with_memory_space_constraint(value, pltpu.HBM)


HBM = pl.BlockSpec(memory_space=pltpu.HBM)
NEAR = pl.BlockSpec(memory_space=pltpu.VMEM)


def plain(kernel, name, scalars, near, far, outs, scratch, flops, size, limit, after=()):
    first = len(scalars) + len(near) + len(far)

    def body(*refs):
        kernel(*refs[:first], *refs[first + len(after) :])

    return pl.pallas_call(
        body,
        in_specs=[
            *[pl.BlockSpec(memory_space=pltpu.SMEM)] * len(scalars),
            *[NEAR] * len(near),
            *[HBM] * (len(far) + len(after)),
        ],
        out_specs=[HBM] * len(outs),
        out_shape=[pltpu.HBM(out.shape, out.dtype) for out in outs],
        scratch_shapes=[*scratch, pltpu.SemaphoreType.DMA((24,))],
        compiler_params=pltpu.CompilerParams(vmem_limit_bytes=limit << 20),
        cost_estimate=pl.CostEstimate(
            flops=int(flops * WEIGHT), bytes_accessed=int(size * WEIGHT), transcendentals=0
        ),
        name=name,
    )(*scalars, *near, *map(in_hbm, (*far, *after)))


def gate(values):
    def body(*refs):
        del refs

    return pl.pallas_call(
        body,
        in_specs=[HBM] * len(values),
        out_specs=[HBM] * len(values),
        out_shape=[pltpu.HBM(value.shape, value.dtype) for value in values],
        input_output_aliases={i: i for i in range(len(values))},
        name="gate",
    )(*map(in_hbm, values))


class Moves:
    def __init__(self):
        self.running, self.found = [], {}

    def start(self, name, steps):
        self.running.append((name, steps, next(steps)))

    def kernel(self, output, due=()):
        arrived = [array for _, _, arrays in self.running for array in arrays]
        held = gate([output, *due, *arrived])
        self.step(iter(held[1 + len(due) :]))
        return held[: 1 + len(due)]

    def chain(self, partial, due=()):
        arrived = [array for _, _, arrays in self.running for array in arrays]
        partial, *rest = gate([partial, *due, *arrived])
        partial, other, *rest = gate([partial, swap(partial, "tensor"), *rest])
        self.step(iter(rest[len(due) :]))
        return partial, other, *rest[: len(due)]

    def hurry(self, name):
        if name in self.found:
            return self.found[name]
        others = [entry for entry in self.running if entry[0] != name]
        self.running = [entry for entry in self.running if entry[0] == name]
        self.finish()
        self.running = others
        return self.found[name]

    def step(self, arrived=None):
        before, self.running = self.running, []
        for name, steps, arrays in before:
            if arrived is not None:
                arrays = [next(arrived) for _ in arrays]
            try:
                self.running.append((name, steps, steps.send(arrays)))
            except StopIteration as stop:
                self.found[name] = stop.value

    def finish(self):
        while self.running:
            self.step()


class Copies:
    def __init__(self, sems):
        self.sems, self.count, self.leaving = sems, 0, []

    def start(self, source, target):
        copy = pltpu.make_async_copy(source, target, self.sems.at[self.count])
        self.count += 1
        copy.start()
        return copy

    def leave(self, source, target):
        self.leaving.append(self.start(source, target))

    def finish(self):
        for copy in self.leaving:
            copy.wait()


def core_half(ref, ids):
    half = ref.shape[0] // 2
    return ref.at[pl.ds(pl.multiple_of(ids[AT_CORE] * half, half), half)]


def attend_kernel(layer, heads, ids, gain_ref, shift_ref, biases_ref, *refs):
    parts = 1 if layer == 0 else 3
    stream_hbm, refs = refs[:parts], refs[parts:]
    token_hbm, out_hbm, image_hbm, wide_hbm, small_hbm = refs[:5]
    stream_out, normed_out, half_out, row_out, partial_out, bias_out = refs[5:11]
    stream_in, token, outer, image, wide, small, normed, low, rows, bias, total, partial, sems = refs[11:]
    copies = Copies(sems)
    per = pl.ds(layer * heads, heads)
    near = [copies.start(source, stream_in.at[i]) for i, source in enumerate(stream_hbm)]
    tables = [copies.start(wide_hbm.at[per], wide), copies.start(small_hbm.at[per], small)]
    tokens = [copies.start(token_hbm.at[layer, 0], token.at[0])]
    images = copies.start(image_hbm.at[layer], image)
    tokens += [copies.start(token_hbm.at[layer, m], token.at[m]) for m in (1, 2)]
    outers = copies.start(out_hbm.at[layer], outer)
    kind = ids[KIND]
    count = low.shape[0]
    for copy in near:
        copy.wait()
    if layer == 0:
        stream = stream_in[0].astype(FULL)
    else:
        stream = stream_in[0] + (stream_in[1] + stream_in[2]) + biases_ref[layer - 1, 1:2, :]
    normed[...] = normal_of(stream)[0] * gain_ref[layer, 0:1, :] + shift_ref[layer, 0:1, :]
    if layer == 0:
        partial[...] = stream
        copies.leave(partial, stream_out)
    else:
        stream_in[0] = stream
        copies.leave(stream_in.at[0], stream_out)
    copies.leave(normed, normed_out)
    copies.leave(core_half(normed, ids), half_out)
    low[...] = normed[...].astype(LOW)
    for copy in tables:
        copy.wait()
    fill_bias(heads, kind, wide, small, bias)
    copies.leave(bias, bias_out)
    for member in range(3):
        tokens[member].wait()
        projected = matmul(low[...], token[member], NT)
        if member == 0:
            images.wait()
        if member == 1:
            rows[member] = projected.astype(LOW)
            continue
        for i in range(IMAGES):
            mine = image[member // 2, i : i + 1, :]
            mine = jnp.where(kind != 0, mine, image[member // 2, 0:1, :])
            here = slice(i * (count // IMAGES), (i + 1) * (count // IMAGES))
            rows[member, here, :] = (projected[here] + mine).astype(LOW)
    copies.leave(rows, row_out)

    def row(index, first, last):
        return rows[index, :, first:last]

    attention_forward(heads, row, bias, total)
    outers.wait()
    if layer == 0:
        copies.leaving.pop(0).wait()
    partial[...] = matmul(total[...].astype(LOW), outer[...])
    copies.leave(partial, partial_out)
    copies.finish()


def attend(layer, ids, stream, gains, shifts, biases, token_rows, per_image, out_proj, wide, small, after=()):
    count, width = stream[0].shape
    depth, _, local, _ = token_rows.shape
    heads = wide.shape[0] // depth
    full = shape_of((count, width))
    outs = [
        full,
        full,
        shape_of((count // 2, width)),
        shape_of((3, count, local), LOW),
        full,
        shape_of((heads, count, count)),
    ]
    return plain(
        functools.partial(attend_kernel, layer, heads),
        f"attend_{layer}",
        (ids,),
        (gains, shifts, biases),
        (*stream, token_rows, out_proj, per_image, wide, small),
        outs,
        [
            pltpu.VMEM((len(stream), count, width), stream[0].dtype),
            pltpu.VMEM((3, local, width), LOW),
            pltpu.VMEM((local, width), LOW),
            pltpu.VMEM(per_image.shape[1:], FULL),
            pltpu.VMEM((heads, *wide.shape[1:]), FULL),
            pltpu.VMEM((heads, *small.shape[1:]), FULL),
            pltpu.VMEM((count, width), FULL),
            pltpu.VMEM((count, width), LOW),
            pltpu.VMEM((3, count, local), LOW),
            pltpu.VMEM((heads, count, count), FULL),
            pltpu.VMEM((count, local), FULL),
            pltpu.VMEM((count, width), FULL),
        ],
        2 * count * width * local * 4,
        8 * width * local + 16 * count * width,
        40,
        after,
    )


CHUNK = 768


def feed_kernel(layer, ids, gain_ref, shift_ref, biases_ref, stream_hbm, part_hbm, other_hbm, in_hbm_ref, out_hbm_ref, middle_out, half_out, slope_out, partial_out, stream_in, inner, outer, normed, low, slope, partial, sems):
    units = inner.shape[1]
    chunks = [slice(at, at + CHUNK) for at in range(0, units, CHUNK)]
    copies = Copies(sems)
    near = [
        copies.start(source, stream_in.at[i])
        for i, source in enumerate((stream_hbm, part_hbm, other_hbm))
    ]
    weights = [
        (
            copies.start(in_hbm_ref.at[layer, :, chunk], inner.at[:, chunk]),
            copies.start(out_hbm_ref.at[layer, chunk, :], outer.at[chunk, :]),
        )
        for chunk in chunks
    ]
    for copy in near:
        copy.wait()
    middle = stream_in[0] + (stream_in[1] + stream_in[2]) + biases_ref[layer, 0:1, :]
    stream_in[0] = middle
    copies.leave(stream_in.at[0], middle_out)
    normed[...] = normal_of(middle)[0] * gain_ref[layer, 1:2, :] + shift_ref[layer, 1:2, :]
    copies.leave(core_half(normed, ids), half_out)
    low[...] = normed[...].astype(LOW)
    for at, chunk in enumerate(chunks):
        weights[at][0].wait()
        hidden = matmul(low[...], inner[:, chunk])
        rise = 0.5 * (1.0 + lax.erf(hidden * ROOT_HALF))
        slope[:, chunk] = rise + hidden * jnp.exp(-0.5 * hidden * hidden) * SLOPE_NORM
        copies.leave(slope.at[:, chunk], slope_out.at[:, chunk])
        weights[at][1].wait()
        product = matmul((hidden * rise).astype(LOW), outer[chunk, :])
        partial[...] = product if at == 0 else partial[...] + product
    copies.leave(partial, partial_out)
    copies.finish()


def feed(layer, ids, stream, partial, other, biases, gains, shifts, hidden_in, hidden_out, after=()):
    count, width = stream.shape
    units = hidden_in.shape[2]
    full = shape_of((count, width))
    return plain(
        functools.partial(feed_kernel, layer),
        f"feed_{layer}",
        (ids,),
        (gains, shifts, biases),
        (stream, partial, other, hidden_in, hidden_out),
        [full, shape_of((count // 2, width)), shape_of((count, units)), full],
        [
            pltpu.VMEM((3, count, width), FULL),
            pltpu.VMEM((width, units), LOW),
            pltpu.VMEM((units, width), LOW),
            pltpu.VMEM((count, width), FULL),
            pltpu.VMEM((count, width), LOW),
            pltpu.VMEM((count, units), FULL),
            pltpu.VMEM((count, width), FULL),
        ],
        4 * count * width * units,
        4 * width * units + 4 * count * (units + 6 * width),
        48,
        after,
    )


def feed_back_kernel(layer, last, ids, gain_ref, *refs):
    parts = 1 if last else 4
    up_hbm, refs = refs[:parts], refs[parts:]
    slope_hbm, in_hbm_ref, out_hbm_ref, upstream_out, half_out, sums_out, partial_out = refs[:7]
    up_in, inner, outer, upstream, low, slope, sums, partial, sems = refs[7:]
    units = inner.shape[1]
    chunks = [slice(at, at + CHUNK) for at in range(0, units, CHUNK)]
    copies = Copies(sems)
    near = [copies.start(source, up_in.at[i]) for i, source in enumerate(up_hbm)]
    weights = [
        (
            copies.start(out_hbm_ref.at[layer, chunk, :], outer.at[chunk, :]),
            copies.start(slope_hbm.at[:, chunk], slope.at[:, chunk]),
            copies.start(in_hbm_ref.at[layer, :, chunk], inner.at[:, chunk]),
        )
        for chunk in chunks
    ]
    for copy in near:
        copy.wait()
    sums[...] = jnp.zeros_like(sums)
    if last:
        upstream[...] = up_in[0].astype(FULL)
    else:
        step, gain_part, shift_part = norm_backward(
            up_in[3], gain_ref[layer + 1, 0:1, :], up_in[1] + up_in[2]
        )
        upstream[...] = up_in[0] + step
        sums[1:2, :] = gain_part
        sums[2:3, :] = shift_part
    copies.leave(upstream, upstream_out)
    copies.leave(core_half(upstream, ids), half_out)
    low[...] = upstream[...].astype(LOW)
    sums[0:1, :] = jnp.sum(low[...].astype(FULL), axis=0, keepdims=True)
    copies.leave(sums, sums_out)
    for at, chunk in enumerate(chunks):
        weights[at][0].wait()
        back = matmul(low[...], outer[chunk, :], NT)
        weights[at][1].wait()
        weights[at][2].wait()
        product = matmul((back * slope[:, chunk]).astype(LOW), inner[:, chunk], NT)
        partial[...] = product if at == 0 else partial[...] + product
    copies.leave(partial, partial_out)
    copies.finish()


def feed_back(layer, ids, upstream, slope, hidden_in, hidden_out, gains, after=()):
    count, width = upstream[0].shape
    units = hidden_in.shape[2]
    full = shape_of((count, width))
    return plain(
        functools.partial(feed_back_kernel, layer, len(upstream) == 1),
        f"feed_back_{layer}",
        (ids,),
        (gains,),
        (*upstream, slope, hidden_in, hidden_out),
        [full, shape_of((count // 2, width)), shape_of((8, width)), full],
        [
            pltpu.VMEM((len(upstream), count, width), upstream[0].dtype),
            pltpu.VMEM((width, units), LOW),
            pltpu.VMEM((units, width), LOW),
            pltpu.VMEM((count, width), FULL),
            pltpu.VMEM((count, width), LOW),
            pltpu.VMEM((count, units), FULL),
            pltpu.VMEM((8, width), FULL),
            pltpu.VMEM((count, width), FULL),
        ],
        4 * count * width * units,
        4 * width * units + 4 * count * (units + 6 * width),
        48,
        after,
    )


def attend_back_kernel(layer, heads, ids, gain_ref, up_hbm, part_hbm, other_hbm, middle_hbm, row_hbm, bias_hbm, out_hbm, token_hbm, back_out, half_out, sums_out, partial_out, up_in, rows, bias, token, outer, back, sums, upstream, steps, partial, sems):
    copies = Copies(sems)
    near = [
        copies.start(source, up_in.at[i])
        for i, source in enumerate((up_hbm, part_hbm, other_hbm, middle_hbm))
    ]
    outers = copies.start(out_hbm.at[layer], outer)
    saved = [copies.start(row_hbm, rows), copies.start(bias_hbm, bias)]
    tokens = [copies.start(token_hbm.at[layer, member], token.at[member]) for member in range(3)]
    for copy in near:
        copy.wait()
    step, gain_part, shift_part = norm_backward(
        up_in[3], gain_ref[layer, 1:2, :], up_in[1] + up_in[2]
    )
    back[...] = up_in[0] + step
    copies.leave(back, back_out)
    copies.leave(core_half(back, ids), half_out)
    rounded = back[...].astype(LOW)
    sums[...] = jnp.zeros_like(sums)
    sums[0:1, :] = jnp.sum(rounded.astype(FULL), axis=0, keepdims=True)
    sums[1:2, :] = gain_part
    sums[2:3, :] = shift_part
    copies.leave(sums, sums_out)
    outers.wait()
    upstream[...] = matmul(rounded, outer[...], NT).astype(LOW)

    def row(index, first, last):
        return upstream[:, first:last] if index == 3 else rows[index, :, first:last]

    for copy in saved:
        copy.wait()
    attention_backward(heads, row, bias, steps, None, None)
    for member in range(3):
        tokens[member].wait()
        product = matmul(steps[member].astype(LOW), token[member])
        partial[...] = product if member == 0 else partial[...] + product
    copies.leave(partial, partial_out)
    copies.finish()


def attend_back(layer, ids, upstream, partial, other, middle, gains, rows, bias, out_proj, token_rows, after=()):
    count, width = upstream.shape
    local = token_rows.shape[2]
    heads = bias.shape[0]
    full = shape_of((count, width))
    return plain(
        functools.partial(attend_back_kernel, layer, heads),
        f"attend_back_{layer}",
        (ids,),
        (gains,),
        (upstream, partial, other, middle, rows, bias, out_proj, token_rows),
        [full, shape_of((count // 2, width)), shape_of((8, width)), full],
        [
            pltpu.VMEM((4, count, width), FULL),
            pltpu.VMEM((3, count, local), LOW),
            pltpu.VMEM((heads, count, count), FULL),
            pltpu.VMEM((3, local, width), LOW),
            pltpu.VMEM((local, width), LOW),
            pltpu.VMEM((count, width), FULL),
            pltpu.VMEM((8, width), FULL),
            pltpu.VMEM((count, local), LOW),
            pltpu.VMEM((3, count, local), FULL),
            pltpu.VMEM((count, width), FULL),
        ],
        2 * count * width * local * 4 + heads * count * count * 4096,
        8 * width * local + 24 * count * width,
        40,
        after,
    )


def finish_kernel(gain_ref, up_hbm, part_hbm, other_hbm, stream_hbm, gradient_out, sums_out, up_in, gradient, sums, sems):
    copies = Copies(sems)
    near = [
        copies.start(source, up_in.at[i])
        for i, source in enumerate((up_hbm, part_hbm, other_hbm, stream_hbm))
    ]
    for copy in near:
        copy.wait()
    step, gain_part, shift_part = norm_backward(up_in[3], gain_ref[0, 0:1, :], up_in[1] + up_in[2])
    gradient[...] = (up_in[0] + step).astype(LOW)
    copies.leave(gradient, gradient_out)
    sums[...] = jnp.zeros_like(sums)
    sums[1:2, :] = gain_part
    sums[2:3, :] = shift_part
    copies.leave(sums, sums_out)
    copies.finish()


def finish(upstream, partial, other, stream, gains):
    count, width = stream.shape
    return plain(
        finish_kernel,
        "finish",
        (),
        (gains,),
        (upstream, partial, other, stream),
        [shape_of((count, width), LOW), shape_of((8, width))],
        [
            pltpu.VMEM((4, count, width), FULL),
            pltpu.VMEM((count, width), LOW),
            pltpu.VMEM((8, width), FULL),
        ],
        0,
        20 * count * width,
        24,
    )


def line_window(units, line):
    own = units // line
    offsets = [z * own % 128 for z in range(line)]
    size = -(-(max(offsets) + own) // 128) * 128
    starts = [min(z * own // 128 * 128, units - size) for z in range(line)]
    return starts, [z * own - starts[z] for z in range(line)], size


def feed_gradients_kernel(layer, line, ids, x_hbm, y_hbm, in_hbm, out_hbm, outer_keep, outer_send, inner_keep, inner_send, stage, part_in, part_out, low_x, low_y, active, back, outer, inner, sems):
    units = in_hbm.shape[2]
    width = low_x.shape[1]
    rows = stage.shape[2]
    own = units // line
    starts, offsets, size = line_window(units, line)
    at = ids[AT_LINE]
    start, offset = jnp.int32(starts[0]), jnp.int32(offsets[0])
    for z in range(1, line):
        start = jnp.where(at == z, starts[z], start)
        offset = jnp.where(at == z, offsets[z], offset)
    start = pl.multiple_of(start, 128)
    copies = [
        pltpu.make_async_copy(in_hbm.at[layer, :, pl.ds(start, size)], part_in, sems.at[0, 2]),
        pltpu.make_async_copy(out_hbm.at[layer, pl.ds(start, size), :], part_out, sems.at[1, 2]),
    ]

    def fetch(tile):
        slot = tile % 2
        return [
            pltpu.make_async_copy(
                source.at[pl.ds(tile * rows, rows)], stage.at[side, slot], sems.at[side, slot]
            )
            for side, source in enumerate((x_hbm, y_hbm))
        ]

    flying = {0: fetch(0)}
    for copy in (*flying[0], *copies):
        copy.start()
    for tile in range(line):
        if tile + 1 < line:
            flying[tile + 1] = fetch(tile + 1)
            for copy in flying[tile + 1]:
                copy.start()
        for copy in flying[tile]:
            copy.wait()
        if tile == 0:
            for copy in copies:
                copy.wait()
        here = slice(tile * rows, (tile + 1) * rows)
        low_x[here, :] = stage[0, tile % 2].astype(LOW)
        low_y[here, :] = stage[1, tile % 2].astype(LOW)
        hidden = matmul(low_x[here, :], part_in[...])
        rise = 0.5 * (1.0 + lax.erf(hidden * ROOT_HALF))
        active[here, :] = (hidden * rise).astype(LOW)
        slope = rise + hidden * jnp.exp(-0.5 * hidden * hidden) * SLOPE_NORM
        back[here, :] = (matmul(low_y[here, :], part_out[...], NT) * slope).astype(LOW)

    @pl.loop(0, size // 128)
    def _(tile):
        lanes = pl.ds(pl.multiple_of(tile * 128, 128), 128)
        outer[lanes, :] = matmul(active[:, lanes], low_y[...], TN)

    @pl.loop(0, width // 128)
    def _(tile):
        lanes = pl.ds(pl.multiple_of(tile * 128, 128), 128)
        inner[lanes, :] = matmul(low_x[:, lanes], back[...], TN)

    pair = own // 2
    step = width // (GROUP * line)
    for z in range(len(set(offsets))):
        shifted = sorted(set(offsets))[z]
        for col in range(2):

            @pl.when((offset == shifted) & (ids[AT_COL] == col))
            def _(shifted=shifted, col=col):
                for target, part in ((outer_keep, col), (outer_send, 1 - col)):
                    first = shifted + part * pair
                    for r in range(2):
                        begin = first + r * (pair // 2)
                        target[r] = outer[begin : begin + pair // 2, :]

    for row in range(2):

        @pl.when(ids[AT_ROW] == row)
        def _(row=row):
            for z in range(line):
                for c in range(2):
                    for target, part in ((inner_keep, row), (inner_send, 1 - row)):
                        begin = (GROUP * z + 2 * c + part) * step
                        target[c, z] = inner[begin : begin + step, :]


def feed_gradients(layer, line, ids, xs, ys, hidden_in, hidden_out, after=()):
    count, width = xs.shape
    rows = count // line
    units = hidden_in.shape[2]
    own = units // line
    size = line_window(units, line)[2]
    anywhere = pl.BlockSpec(memory_space=pl.ANY)
    outs = [shape_of((2, own // 4, width))] * 2 + [shape_of((2, line, width // (GROUP * line), size))] * 2
    return call(
        functools.partial(feed_gradients_kernel, layer, line),
        f"feed_gradients_{layer}",
        (1,),
        [anywhere] * 2 + [pl.BlockSpec(memory_space=pltpu.HBM)] * 2,
        [whole_once(out.shape) for out in outs],
        outs,
        [
            pltpu.VMEM((2, 2, rows, width), FULL),
            pltpu.VMEM((width, size), LOW),
            pltpu.VMEM((size, width), LOW),
            pltpu.VMEM((line * rows, width), LOW),
            pltpu.VMEM((line * rows, width), LOW),
            pltpu.VMEM((line * rows, size), LOW),
            pltpu.VMEM((line * rows, size), LOW),
            pltpu.VMEM((size, width), FULL),
            pltpu.VMEM((width, size), FULL),
            pltpu.SemaphoreType.DMA((2, 3)),
        ],
        8 * line * rows * width * size,
        8 * line * rows * width + 16 * width * size,
        after=after,
    )(ids, *map(in_hbm, (xs, ys, hidden_in, hidden_out)))


def whole_call(kernel, name, scalars, near, outs, scratch=(), limit=40):
    return pl.pallas_call(
        kernel,
        in_specs=[
            *[pl.BlockSpec(memory_space=pltpu.SMEM)] * len(scalars),
            *[NEAR] * len(near),
        ],
        out_specs=[NEAR] * len(outs),
        out_shape=[pltpu.HBM(out.shape, out.dtype) for out in outs],
        scratch_shapes=list(scratch),
        compiler_params=pltpu.CompilerParams(vmem_limit_bytes=limit << 20),
        cost_estimate=pl.CostEstimate(
            flops=WHOLE_COST, bytes_accessed=WHOLE_COST // 300, transcendentals=0
        ),
        name=name,
    )(*scalars, *map(in_hbm, near))


def feed_halve_kernel(ids, outer_keep, outer_half, inner_keep, inner_half, outer_own, outer_send, inner_own, inner_send):
    row, col = ids[AT_ROW], ids[AT_COL]
    outer_own[...] = outer_keep[row] + outer_half[row]
    outer_send[...] = outer_keep[1 - row] + outer_half[1 - row]
    inner_own[...] = inner_keep[col] + inner_half[col]
    inner_send[...] = inner_keep[1 - col] + inner_half[1 - col]


def feed_deal_kernel(depth, line, ids, *refs):
    parts, outs = refs[: 2 * depth], refs[2 * depth :]
    place = ids[AT_LINE]
    for by in range(line):
        to = lax.rem(place + by, line)
        for layer in range(depth):
            outs[by][layer] = parts[2 * layer][to] + parts[2 * layer + 1][to]


def feed_deal(depth, line, ids, parts):
    block = parts[0].shape[1:]
    return whole_call(
        functools.partial(feed_deal_kernel, depth, line),
        "feed_deal",
        (ids,),
        parts,
        [shape_of((depth, *block))] * line,
    )


def feed_scatter(layer, ids, pieces, line):
    outer_keep, outer_send, inner_keep, inner_send = pieces
    outer_half, inner_half = yield [swap(outer_send, "col"), swap(inner_send, "row")]
    outer_part, inner_part = shape_of(outer_keep.shape[1:]), shape_of(inner_keep.shape[1:])
    outer_own, outer_send, inner_own, inner_send = whole_call(
        feed_halve_kernel,
        f"feed_halve_{layer}",
        (ids,),
        (outer_keep, outer_half, inner_keep, inner_half),
        [outer_part, outer_part, inner_part, inner_part],
    )
    outer_other, inner_other = yield [swap(outer_send, "row"), swap(inner_send, "col")]
    return [inner_own, inner_other], [outer_own, outer_other]


def attention_deal_kernel(layer, line, heads, at_rows, ids, summed, embedded, *refs):
    images, projection, outs = refs[:line], refs[line], refs[line + 1 :]
    own = images[0].shape[1]
    chunk, lanes, left = at_rows.chunk, at_rows.LANES, at_rows.left
    features = chunk // GROUP
    for third in range(3):
        row = at_rows.projection + third * at_rows.piece
        projection[:, third * lanes : (third + 1) * lanes] = summed[row : row + at_rows.piece, :]
    time = []
    for member in range(2):
        every = jnp.concatenate(
            [ref[member * GROUP * IMAGES : (member + 1) * GROUP * IMAGES, :] for ref in images],
            axis=0,
        )
        high = every.astype(LOW)
        middle = (every - high.astype(FULL)).astype(LOW)
        low = (every - high.astype(FULL) - middle.astype(FULL)).astype(LOW)
        time.append(
            matmul(embedded[...], high, TN)
            + (matmul(embedded[...], middle, TN) + matmul(embedded[...], low, TN))
        )
    at = 2 * ids[AT_COL] + ids[AT_ROW]
    entries = 4 * SPAN // line // GROUP
    fold = chunk // at_rows.folds
    for j in range(GROUP):

        @pl.when(at == j)
        def _(j=j):
            for by in range(GROUP):
                to, out = j ^ by, outs[by]
                here = slice(to * features, (to + 1) * features)
                out[:features, :lanes] = summed[here, :]
                for i in range(at_rows.folds):
                    first, last = max(i * fold, here.start), min((i + 1) * fold, here.stop)
                    if first < last:
                        row = at_rows.folded - i * fold
                        out[first - here.start : last - here.start, lanes : 3 * own] = summed[
                            row + first : row + last, i * left : (i + 1) * left
                        ]
                for member in range(2):
                    out[:features, (3 + member) * own : (4 + member) * own] = time[member][here]
                out[features:, :] = jnp.zeros((out.shape[0] - features, 5 * own), FULL)
                out[features : features + heads, :entries] = summed[
                    at_rows.table : at_rows.table + heads, to * entries : (to + 1) * entries
                ]
                if layer == 0:
                    first = features + TABLE_ROWS
                    out[first : first + VECTORS, :features] = summed[
                        at_rows.vectors : at_rows.vectors + VECTORS, here
                    ]


def attention_deal(layer, line, ids, summed, embedded, images, heads, width, own):
    at_rows = Rows(own, width, heads, VECTORS if layer == 0 else 0, line)
    rows = width // line // GROUP + TABLE_ROWS + (VECTOR_ROWS if layer == 0 else 0)
    projection, *blocks = whole_call(
        functools.partial(attention_deal_kernel, layer, line, heads, at_rows),
        f"attention_deal_{layer}",
        (ids,),
        (summed, embedded, *images),
        [shape_of((own // line, width))] + [shape_of((rows, 5 * own))] * GROUP,
    )
    moved = lax.ppermute(
        projection,
        LINES,
        [(GROUP * z + j, line * j + z) for z in range(line) for j in range(GROUP)],
    )
    projection, across, along, corner = yield [
        moved,
        swap(blocks[1], "row"),
        swap(blocks[2], "col"),
        swap_corner(blocks[3]),
    ]
    return projection, [blocks[0], across, along, corner]


def join_feed_kernel(depth, line, ids, *refs):
    inners, outers, (inner, outer, order) = refs[:line], refs[line : line + 2 * depth], refs[line + 2 * depth :]
    part = inner.shape[2] // line
    offsets = line_window(inner.shape[2], line)[1]
    for by in range(line):
        order[lax.rem(ids[AT_LINE] + line - by, line)] = inners[by][...]
    for layer in range(depth):
        outer[layer] = outers[2 * layer][...] + outers[2 * layer + 1][...]
        for z in range(line):
            inner[layer, :, z * part : (z + 1) * part] = order[
                z, layer, :, offsets[z] : offsets[z] + part
            ]


def join_feed(line, ids, blocks, outers, units):
    depth, features, size = blocks[0].shape
    rows, width = outers[0].shape
    return whole_call(
        functools.partial(join_feed_kernel, depth, line),
        "join_feed",
        (ids,),
        (*blocks, *outers),
        [shape_of((depth, features, units)), shape_of((depth, rows, width))],
        [pltpu.VMEM((line, depth, features, size), FULL)],
    )


def join_attention_kernel(depth, heads, ids, *refs):
    blocks, refs = refs[: depth * GROUP], refs[depth * GROUP :]
    projections, refs = refs[:depth], refs[depth:]
    token, time, table, projection, gain, shift_out, bias = refs
    features, local = token.shape[2:]
    own = local // GROUP
    entries = table.shape[2]
    at = 2 * ids[AT_COL] + ids[AT_ROW]
    for layer in range(depth):
        projection[:, layer, :] = projections[layer][...]
    for j in range(GROUP):

        @pl.when(at == j)
        def _(j=j):
            for layer in range(depth):
                for by in range(GROUP):
                    ref, source = blocks[layer * GROUP + by], j ^ by
                    lanes = slice(source * own, (source + 1) * own)
                    for member in range(3):
                        token[layer, member, :, lanes] = ref[
                            :features, member * own : (member + 1) * own
                        ]
                    for member in range(2):
                        time[layer, member, :, lanes] = ref[
                            :features, (3 + member) * own : (4 + member) * own
                        ]
                    table[layer, source * heads : (source + 1) * heads, :] = ref[
                        features : features + heads, :entries
                    ]

    first = features + TABLE_ROWS
    total = functools.reduce(
        jnp.add, [blocks[by][first : first + 6 * depth, :features] for by in range(GROUP)]
    )
    for kind, out in enumerate((gain, shift_out, bias)):
        for layer in range(depth):
            begin = (kind * depth + layer) * 2
            out[layer] = total[begin : begin + 2]


def join_attention(depth, line, ids, attention, heads, local, width):
    features = width // (GROUP * line)
    vector = shape_of((depth, 2, features))
    return whole_call(
        functools.partial(join_attention_kernel, depth, heads // GROUP),
        "join_attention",
        (ids,),
        (
            *[block for layer in range(depth) for block in attention[layer][1]],
            *[attention[layer][0] for layer in range(depth)],
        ),
        [
            shape_of((depth, 3, features, local)),
            shape_of((depth, 2, features, local)),
            shape_of((depth, heads, 4 * SPAN // (GROUP * line))),
            shape_of((local // (GROUP * line), depth, width)),
            vector,
            vector,
            vector,
        ],
    )


class Rows:
    LANES = 384

    def __init__(self, own, width, heads, vectors, line):
        self.chunk, self.piece = width // line, own // line
        self.left = 3 * own - self.LANES
        self.folds = self.LANES // self.left
        self.folded = self.chunk
        self.projection = self.folded + self.chunk // self.folds
        self.table = self.projection + 3 * self.piece
        self.vectors = self.table + heads
        self.total = -(-(self.vectors + vectors) // 8) * 8


VECTORS = 12
TABLE_ROWS, VECTOR_ROWS = 8, 16


def attention_gradients_kernel(layer, heads, line, vector_count, ids, kinds, *refs):
    parts = 2 * GROUP - 1
    sources = refs[:parts], refs[parts : 2 * parts]
    token_hbm, out_hbm = refs[2 * parts : 2 * parts + 2]
    image_hbm = refs[2 * parts + 2 : 2 * parts + 2 + GROUP]
    refs = refs[2 * parts + 2 + GROUP :]
    wide_ref, small_ref = refs[:2]
    vectors, refs = refs[2 : 2 + vector_count], refs[2 + vector_count :]
    token_out, images_out = refs[:2]
    (images, low_x, low_y, joined, attended_low, rows, bias, steps, attended) = refs[2:11]
    wide_sum, small_sum, stage, token, outer, scores, image_all, sems, weight_sems = refs[11:]
    slot = pl.program_id(0)
    kind = kinds[slot]
    count = low_x.shape[1]
    half = count // 2
    own = images.shape[2]
    at = 2 * ids[AT_COL] + ids[AT_ROW]

    def fetch(near):
        if near == 0:
            return [
                pltpu.make_async_copy(sources[side][0], stage.at[side, 0], sems.at[side, 0])
                for side in range(2)
            ]
        return [
            pltpu.make_async_copy(
                sources[side][(far + 1) * (GROUP - 1) + near - GROUP + 1],
                stage.at[side, near, pl.ds(pl.multiple_of(place * half, half), half)],
                sems.at[side, 2 * near + far - 1],
            )
            for side in range(2)
            for far, place in enumerate((ids[AT_CORE], 1 - ids[AT_CORE]))
        ]

    mine = pl.ds(pl.multiple_of(at * own, 16), own)
    weights = [
        pltpu.make_async_copy(token_hbm.at[layer, :, mine, :], token, weight_sems.at[0]),
        pltpu.make_async_copy(out_hbm.at[layer, mine, :], outer, weight_sems.at[1]),
        *[
            pltpu.make_async_copy(image_hbm[near], image_all.at[near], weight_sems.at[2 + near])
            for near in range(GROUP)
        ],
    ]

    @pl.when(slot == 0)
    def _():
        for copy in (*fetch(0), *weights):
            copy.start()
        for near in range(1, GROUP):
            for copy in fetch(near):
                copy.start()
        wide_sum[...] = jnp.zeros_like(wide_sum)
        small_sum[...] = jnp.zeros_like(small_sum)
    for near in range(GROUP):

        @pl.when(slot == near)
        def _(near=near):
            for copy in fetch(near):
                copy.wait()

    @pl.when(slot == 0)
    def _():
        for copy in weights:
            copy.wait()
        for j in range(GROUP):

            @pl.when(at == j)
            def _(j=j):
                for member in range(2):
                    first = (2 * layer + member) * IMAGES
                    for near in range(GROUP):
                        images[member, near * IMAGES : (near + 1) * IMAGES, :] = image_all[
                            near, first : first + IMAGES, j * own : (j + 1) * own
                        ]

    fill_bias(heads, kind, wide_ref, small_ref, bias)
    low_x[slot] = stage[0, slot].astype(LOW)
    low_y[slot] = stage[1, slot].astype(LOW)
    for member in range(3):
        projected = matmul(low_x[slot], token[member], NT)
        for i in range(IMAGES):
            here = slice(i * (count // IMAGES), (i + 1) * (count // IMAGES))
            if member == 1:
                rows[member, here, :] = projected[here].astype(LOW)
            else:
                near = images[member // 2]
                first = near[0:1, :]
                mine = near[i : i + 1, :]
                for other in range(1, GROUP):
                    begin = other * IMAGES
                    first = jnp.where(slot == other, near[begin : begin + 1, :], first)
                    mine = jnp.where(slot == other, near[begin + i : begin + i + 1, :], mine)
                mine = jnp.where(kind != 0, mine, first)
                rows[member, here, :] = (projected[here] + mine).astype(LOW)
    rows[3] = matmul(low_y[slot], outer[...], NT).astype(LOW)

    def row(index, first, last):
        return rows[index, :, first:last]

    attention_backward(heads, row, bias, steps, attended, scores)
    collect_table(heads, kind, scores, wide_sum, small_sum)
    attended_low[slot] = attended[...].astype(LOW)
    for member in range(3):
        rounded = steps[member].astype(LOW)
        joined[slot, :, member * own : (member + 1) * own] = rounded
        if member != 1:
            sums = [
                jnp.sum(
                    rounded[i * (count // IMAGES) : (i + 1) * (count // IMAGES)].astype(FULL),
                    axis=0,
                    keepdims=True,
                )
                for i in range(IMAGES)
            ]
            everything = sums[0] + sums[1] + sums[2] + sums[3]
            for i in range(IMAGES):
                alone = everything if i == 0 else jnp.zeros_like(everything)
                images_out[0, member // 2, i : i + 1, :] = jnp.where(kind != 0, sums[i], alone)

    @pl.when(slot == GROUP - 1)
    def _():
        flat = GROUP * count
        width = low_x.shape[2]

        product = matmul(low_x[...].reshape(flat, width), joined[...].reshape(flat, -1), TN)
        projection = matmul(
            attended_low[...].reshape(flat, -1), low_y[...].reshape(flat, -1), TN
        )
        tables = [fold_table(wide_sum[head], small_sum[head]) for head in range(heads)]
        size, cells = width // 3, 4 * SPAN // line
        at_rows = Rows(own, width, heads, VECTORS if vectors else 0, line)
        chunk, lanes, left = at_rows.chunk, at_rows.LANES, at_rows.left
        fold = chunk // at_rows.folds
        for z in range(line):
            begin = z * at_rows.total
            token_out[begin : begin + chunk, :] = product[z * chunk : (z + 1) * chunk, :lanes]
            row = begin + at_rows.folded
            for i in range(at_rows.folds):
                first = z * chunk + i * fold
                token_out[row : row + fold, i * left : (i + 1) * left] = product[
                    first : first + fold, lanes:
                ]
            for third in range(3):
                row = begin + at_rows.projection + third * at_rows.piece
                token_out[row : row + at_rows.piece, :] = projection[
                    z * at_rows.piece : (z + 1) * at_rows.piece, third * size : (third + 1) * size
                ]
            row = begin + at_rows.table
            token_out[row : begin + at_rows.total, :] = jnp.zeros(
                (at_rows.total - at_rows.table, lanes), FULL
            )
            for head in range(heads):
                token_out[row + head : row + head + 1, :cells] = tables[head][
                    :, z * cells : (z + 1) * cells
                ]
            row = begin + at_rows.vectors
            for i, (ref, r) in enumerate(vector_places(vectors)):
                token_out[row + i : row + i + 1, :chunk] = ref[
                    r : r + 1, z * chunk : (z + 1) * chunk
                ]


def vector_places(vectors):
    if not vectors:
        return []
    depth = (len(vectors) - 1) // 2
    feeds, middles = vectors[1 : 1 + depth], vectors[1 + depth :]
    firsts = [vectors[0], *feeds]
    return (
        [place for l in range(depth) for place in ((firsts[l], 1), (middles[l], 1))]
        + [place for l in range(depth) for place in ((firsts[l], 2), (middles[l], 2))]
        + [place for l in range(depth) for place in ((middles[l], 0), (feeds[l], 0))]
    )


def attention_gradients(layer, line, ids, kinds, near_x, near_y, token_rows, images, out_proj, wide, small, vectors, after=()):
    count, width = near_x[0].shape
    depth, _, local, _ = token_rows.shape
    own, heads = local // GROUP, wide.shape[0] // depth // GROUP
    near = [HBM] * (len(near_x) + len(near_y))
    at_rows = Rows(own, width, heads, VECTORS if vectors else 0, line)

    def own_heads(slot, ids, kinds):
        return (layer * GROUP + 2 * ids[AT_COL] + ids[AT_ROW], 0, 0)

    outs = [
        shape_of((line * at_rows.total, at_rows.LANES)),
        shape_of((GROUP, 2, IMAGES, own)),
    ]
    return call(
        functools.partial(attention_gradients_kernel, layer, heads, line, len(vectors)),
        f"attention_gradients_{layer}",
        (GROUP,),
        [
            *near,
            *[HBM] * (2 + GROUP),
            pl.BlockSpec((heads, *wide.shape[1:]), own_heads),
            pl.BlockSpec((heads, *small.shape[1:]), own_heads),
            *[whole(vector.shape) for vector in vectors],
        ],
        [
            whole_once(outs[0].shape),
            pl.BlockSpec((1, 2, IMAGES, own), lambda s, ids, kinds: (s, 0, 0, 0)),
        ],
        outs,
        [
            pltpu.VMEM((2, GROUP * IMAGES, own), FULL),
            pltpu.VMEM((GROUP, count, width), LOW),
            pltpu.VMEM((GROUP, count, width), LOW),
            pltpu.VMEM((GROUP, count, 3 * own), LOW),
            pltpu.VMEM((GROUP, count, own), LOW),
            pltpu.VMEM((4, count, own), LOW),
            pltpu.VMEM((heads, count, count), FULL),
            pltpu.VMEM((3, count, own), FULL),
            pltpu.VMEM((count, own), FULL),
            pltpu.VMEM((heads, *wide.shape[1:]), FULL),
            pltpu.VMEM((heads, *small.shape[1:]), FULL),
            pltpu.VMEM((2, GROUP, count, width), FULL),
            pltpu.VMEM((3, own, width), LOW),
            pltpu.VMEM((own, width), LOW),
            pltpu.VMEM((heads, count, count), FULL),
            pltpu.VMEM((GROUP, *images[0].shape), FULL),
            pltpu.SemaphoreType.DMA((2, 2 * GROUP)),
            pltpu.SemaphoreType.DMA((2 + GROUP,)),
        ],
        2 * GROUP * count * width * own * 8 + GROUP * heads * count * count * 4096,
        8 * GROUP * count * width + 8 * width * local,
        2,
        after,
    )(
        ids, kinds, *map(in_hbm, (*near_x, *near_y, token_rows, out_proj, *images)), wide, small, *vectors
    )


def swap(value, axis):
    return lax.ppermute(value, axis, [(0, 1), (1, 0)])


def shift(value, line, by=1):
    return lax.ppermute(value, "line", [(i, (i + by) % line) for i in range(line)])


def gather_line(half):
    return lax.all_gather(half, ("line", "tensor"), tiled=True)


def plane_steps(value, half, slow=False):
    if slow:
        far = yield [swap(half, "row"), swap(half, "col"), swap_corner(half)]
        others = yield [swap(part, "tensor") for part in far]
        return [value, *far, *others]
    across, along = yield [swap(half, "row"), swap(half, "col")]
    corner, *others = yield [swap_corner(half), swap(across, "tensor"), swap(along, "tensor")]
    others += yield [swap(corner, "tensor")]
    return [value, across, along, corner, *others]


def swap_corner(value):
    return lax.ppermute(value, ("col", "row"), [(0, 3), (3, 0), (1, 2), (2, 1)])


def plane_all(value):
    across, along, corner = yield [swap(value, "row"), swap(value, "col"), swap_corner(value)]
    return [value, across, along, corner]


def line_all(value, line):
    far = yield [shift(value, line, by) for by in range(1, line)]
    return [value, *far]


def local(
    tokens,
    segment_ids,
    timesteps,
    norm_gain,
    norm_bias,
    token_proj,
    time_proj,
    bias_table,
    out_proj,
    hidden_in,
    hidden_out,
    branch_bias,
    cotangent,
    *,
    line,
):
    count, width = tokens.shape
    depth, _, _, local_width = token_proj.shape
    heads = bias_table.shape[1]
    units = hidden_in.shape[2]
    own = local_width // GROUP
    n_dp = GROUP * line
    features = width // n_dp
    line_at = lax.axis_index("line")
    ids = jnp.stack(
        [segment_ids[-1], line_at, lax.axis_index("col"), lax.axis_index("row"), lax.axis_index("tensor")]
    ).astype(jnp.int32)
    embedded = sinusoid(timesteps[0], jnp.arange(width, dtype=jnp.int32), width)
    per_image = lax.dot_general(
        time_proj, embedded, (((2,), (1,)), ((), ())), preferred_element_type=FULL
    )
    per_image = jnp.swapaxes(per_image, 2, 3)
    info = jnp.concatenate([timesteps[0], segment_ids[-1:]]).astype(FULL)
    packed = jnp.concatenate(
        [
            per_image.reshape(2 * depth * IMAGES, local_width),
            jnp.pad(info[None], ((0, 7), (0, local_width - IMAGES - 1))),
        ]
    )
    own_feature = line_at * (GROUP * features) + jnp.arange(GROUP * features, dtype=jnp.int32)
    token_rows = jnp.swapaxes(token_proj, 2, 3)
    wide, small = expand_table(bias_table.reshape(depth * heads, -1))

    stream = (tokens,)
    saved = []
    moves = Moves()
    moves.start("packed", plane_all(packed))
    half = lax.dynamic_slice_in_dim(cotangent, lax.axis_index("tensor") * (count // 2), count // 2, 0)
    gathered_up = gather_line(half.astype(FULL))
    for layer in range(depth):
        held, normed, half, rows, partial, bias = attend(
            layer, ids, stream, norm_gain, norm_bias, branch_bias, token_rows, per_image, out_proj, wide, small
        )
        if layer == depth - 1:
            partial, other, gathered_up = moves.chain(partial, [gathered_up])
        else:
            partial, other = moves.chain(partial)
        moves.start(("first", layer), plane_steps(normed, half))
        if layer == depth - 1:
            near = jnp.stack(
                [part[2 * depth * IMAGES, : IMAGES + 1] for part in moves.found["packed"]]
            )
            kinds = near[:, IMAGES].astype(jnp.int32)
            info = jnp.pad(near, ((0, 8 - GROUP), (0, 128 - IMAGES - 1)))
            moves.start("info", line_all(info, line))
        middle, half_second, slope, partial = feed(
            layer,
            ids,
            held,
            partial,
            other,
            branch_bias,
            norm_gain,
            norm_bias,
            hidden_in,
            hidden_out,
        )
        partial, other = moves.chain(partial)
        line_second = gather_line(half_second)
        saved.append((held, rows, middle, slope, line_second, bias))
        stream = (middle, partial, other)
    output = (stream[0] + (stream[1] + stream[2]) + branch_bias[depth - 1, 1]).astype(LOW)

    upstream = (cotangent,)
    collected = [None] * depth
    vectors = [None] * depth
    gathered = [None] * depth
    gathered_line = [None] * depth
    for layer in reversed(range(depth)):
        held, rows, middle, slope, _, bias = saved[layer]
        current, half_up, feed_sums, partial = feed_back(
            layer, ids, upstream, slope, hidden_in, hidden_out, norm_gain
        )
        partial, other = moves.chain(partial)
        if layer < depth - 1:
            gathered_up = gather_line(half_up)
        back_middle, half, middle_sums, back_partial = attend_back(
            layer,
            ids,
            current,
            partial,
            other,
            middle,
            norm_gain,
            rows,
            bias,
            out_proj,
            token_rows,
        )
        if layer > 0:
            back_partial, other, gathered_line[0] = moves.chain(back_partial, [saved[0][4]])
        else:
            back_partial, other = moves.chain(back_partial)
        moves.start(("branch", layer), plane_steps(back_middle, half, layer == 0))
        upstream = (back_middle, back_partial, other, held)
        vectors[layer] = (feed_sums, middle_sums)
        gathered[layer] = gathered_up
    gradient_tokens, last_sums = finish(*upstream, norm_gain)
    gathered_line[depth - 1] = saved[depth - 1][4]
    sums = [last_sums, *[pair[0] for pair in vectors], *[pair[1] for pair in vectors]]
    packed = moves.found["packed"]
    tokens_of = {}


    def run_feed(layer, turn, due=()):
        pieces = feed_gradients(
            layer, line, ids, gathered_line[layer], gathered[layer], hidden_in, hidden_out, after=turn
        )
        turn, *due = moves.kernel(pieces[0], due)
        moves.start(("feed", layer), feed_scatter(layer, ids, (turn, *pieces[1:]), line))
        return turn, due

    def run_attention(layer, turn, due=()):
        token, found = attention_gradients(
            layer,
            line,
            ids,
            kinds,
            moves.found["first", layer],
            moves.hurry(("branch", layer)),
            token_rows,
            packed,
            out_proj,
            wide,
            small,
            sums if layer == 0 else (),
            after=turn,
        )
        turn, *due = moves.kernel(found, due)
        tokens_of[layer] = lax.psum_scatter(token, "line", scatter_dimension=0, tiled=True)
        moved = jnp.swapaxes(turn, 0, 1).reshape(2 * GROUP * IMAGES, own)
        moves.start(("images", layer), line_all(moved, line))
        return turn, due

    top = depth - 1
    turn, _ = run_feed(top, (last_sums,))
    turn, (gathered[0],) = run_attention(top, (turn,), [gathered[0]])
    turn, _ = run_attention(0, (turn,))
    _, (tokens_of[top],) = run_feed(0, (turn,), [tokens_of[top]])
    every = jnp.concatenate([part[:GROUP, :IMAGES].reshape(-1) for part in moves.found["info"]])
    embedded_every = sinusoid(every, own_feature, width)
    def deal(layer):
        moves.start(
            ("attention", layer),
            attention_deal(
                layer,
                line,
                ids,
                tokens_of[layer],
                embedded_every,
                moves.hurry(("images", layer)),
                heads // GROUP,
                width,
                own,
            ),
        )

    for layer in range(1, depth):
        deal(layer)
    moves.hurry(("images", 0))
    moves.finish()
    feeds = [moves.found["feed", layer] for layer in range(depth)]
    blocks = feed_deal(depth, line, ids, [part for inner, _ in feeds for part in inner])
    tokens_of[0], own_block, first_block, *blocks = gate(
        [tokens_of[0], blocks[0], shift(blocks[1], line), *blocks[2:]]
    )
    blocks = [own_block, first_block, *[shift(block, line, by) for by, block in enumerate(blocks, 2)]]
    deal(0)
    moves.finish()
    token, time, table, projection, gain, shifts, bias = join_attention(
        depth,
        line,
        ids,
        [moves.found["attention", layer] for layer in range(depth)],
        heads,
        local_width,
        width,
    )
    projection = jnp.swapaxes(projection, 0, 1)
    gain, *blocks = gate([gain, *blocks])
    inner, outer = join_feed(line, ids, blocks, [part for _, outer in feeds for part in outer], units)
    return (
        output,
        gradient_tokens,
        gain,
        shifts,
        token,
        time,
        table,
        projection,
        inner,
        outer,
        bias,
    )


def solution(mesh):
    line = mesh.shape["dp"] // GROUP
    fine = Mesh(mesh.devices.reshape(line, 2, 2, mesh.shape["tensor"]), (*LINES, "tensor"))
    return jax.shard_map(
        functools.partial(local, line=line),
        mesh=fine,
        in_specs=(
            P(LINES, None),
            P(LINES),
            P(LINES, None),
            P(),
            P(),
            P(None, None, None, "tensor"),
            P(None, None, None, "tensor"),
            P(None, "tensor", None),
            P(None, "tensor", None),
            P(None, None, "tensor"),
            P(None, "tensor", None),
            P(),
            P(LINES, None),
        ),
        out_specs=(
            P(LINES, None),
            P(LINES, None),
            P(None, None, LINES),
            P(None, None, LINES),
            P(None, None, LINES, "tensor"),
            P(None, None, LINES, "tensor"),
            P(None, "tensor", LINES),
            P(None, ("tensor", *LINES), None),
            P(None, LINES, "tensor"),
            P(None, ("tensor", *LINES), None),
            P(None, None, LINES),
        ),
        check_vma=False,
    )
```

```python
import functools
import math

import jax
import jax.numpy as jnp
from jax import lax
from jax.experimental import pallas as pl
from jax.experimental.pallas import tpu as pltpu
from jax.sharding import Mesh
from jax.sharding import PartitionSpec as P

SIDE = 16
HALF = 8
SPAN = SIDE * SIDE
IMAGES = 4
BLOCK = SPAN // IMAGES
GROUP = 4
WEIGHT, GRADIENT_WEIGHT, WHOLE_COST = 10, 6, 20_000_000_000
EPSILON = 1e-06
MASKED = -1e30
ROOT_HALF = 0.7071067811865476
SLOPE_NORM = 0.3989422804014327
LINES = ("line", "col", "row")
LOW = jnp.bfloat16
FULL = jnp.float32
KIND, AT_LINE, AT_COL, AT_ROW, AT_CORE = range(5)


def matmul(left, right, dims=((1,), (0,))):
    return lax.dot_general(left, right, (dims, ((), ())), preferred_element_type=FULL)


NT = ((1,), (1,))
TN = ((0,), (0,))


def normal_of(stream):
    center = stream - jnp.mean(stream, axis=-1, keepdims=True)
    inverse = lax.rsqrt(jnp.mean(center * center, axis=-1, keepdims=True) + EPSILON)
    return center * inverse, inverse


def norm_backward(stream, gain, upstream):
    normal, inverse = normal_of(stream)
    gain_part = jnp.sum(upstream * normal, axis=0, keepdims=True)
    shift_part = jnp.sum(upstream, axis=0, keepdims=True)
    scaled = upstream * gain
    inner = (
        scaled
        - jnp.mean(scaled, axis=-1, keepdims=True)
        - normal * jnp.mean(scaled * normal, axis=-1, keepdims=True)
    )
    return inner * inverse, gain_part, shift_part


def sinusoid(steps, feature, width):
    half = width // 2
    rates = jnp.exp(-math.log(10000.0) * (feature % half).astype(FULL) / half)
    angles = steps.astype(FULL)[:, None] * rates[None, :]
    wave = jnp.where(feature[None, :] < half, jnp.cos(angles), jnp.sin(angles))
    return wave.astype(LOW)


def whole(shape):
    return pl.BlockSpec(shape, lambda *_: (0,) * len(shape))


def whole_once(shape):
    return pl.BlockSpec(shape, lambda *_: (0,) * len(shape), pipeline_mode=pl.Buffered(1))


def call(kernel, name, grid, in_specs, out_specs, out_shape, scratch, flops, size, scalars=1, after=()):
    first = scalars + len(in_specs)

    def body(*refs):
        kernel(*refs[:first], *refs[first + len(after) :])

    made = pl.pallas_call(
        body,
        grid_spec=pltpu.PrefetchScalarGridSpec(
            num_scalar_prefetch=scalars,
            grid=grid,
            in_specs=[*in_specs, *[pl.BlockSpec(memory_space=pl.ANY)] * len(after)],
            out_specs=out_specs,
            scratch_shapes=scratch,
        ),
        out_shape=[pltpu.HBM(out.shape, out.dtype) for out in out_shape],
        compiler_params=pltpu.CompilerParams(vmem_limit_bytes=40 << 20),
        cost_estimate=pl.CostEstimate(
            flops=int(flops * GRADIENT_WEIGHT), bytes_accessed=int(size * GRADIENT_WEIGHT), transcendentals=0
        ),
        name=name,
    )
    return lambda *operands: made(*operands, *map(in_hbm, after))


def shape_of(shape, kind=FULL):
    return jax.ShapeDtypeStruct(shape, kind)


def regroup(value, pieces):
    lane = lax.broadcasted_iota(jnp.int32, (value.shape[0], 128), 1)
    total = jnp.zeros((value.shape[0], 128), FULL)
    for tile, source, place, lanes in pieces:
        part = value[:, tile * 128 : tile * 128 + 128]
        turn = (place - source) % 128
        part = part if turn == 0 else pltpu.roll(part, turn, 1)
        total = jnp.where((lane >= place) & (lane < place + lanes), part, total)
    return total


def expand_kernel(table_ref, wide_ref, small_ref):
    size = table_ref.shape[1]
    table = table_ref[...]
    for c in range(SIDE):
        turned = pltpu.roll(table, size - SIDE + c, 1)
        wide = jnp.concatenate(
            [
                regroup(
                    turned,
                    [(2 * o + p // 4, 32 * (p % 4), 16 * p, 16) for p in range(8)],
                )
                for o in range(4)
            ],
            axis=1,
        )
        wide_ref[:, c, :] = wide
        if c < HALF:
            small_ref[:, c, :] = regroup(
                wide, [(1 + k // 8, 16 * (k % 8), 8 * k, 8) for k in range(16)]
            )


def expand_table(table):
    rows, size = table.shape
    return pl.pallas_call(
        expand_kernel,
        out_shape=[shape_of((rows, SIDE, size // 2)), shape_of((rows, HALF, size // 8))],
        name="expand_table",
    )(table)


def fold_table(wide, small):
    inner = jnp.concatenate([small, jnp.zeros_like(small)], axis=0)
    tiles = [wide[:, 128 * t : 128 * t + 128] for t in range(4)]
    for t in range(2):
        tiles[1 + t] = tiles[1 + t] + regroup(
            inner, [(0, 8 * (8 * t + q), 16 * q, 8) for q in range(8)]
        )
    wide = jnp.concatenate(tiles, axis=1)
    spread = jnp.concatenate(
        [
            regroup(
                wide,
                [(o // 2, 64 * (o % 2) + 16 * q, 32 * q, 16) for q in range(4)],
            )
            for o in range(8)
        ],
        axis=1,
    )
    return functools.reduce(
        jnp.add, [pltpu.roll(spread[c : c + 1], SIDE - c, 1) for c in range(SIDE)]
    )


def fill_bias(heads, kind, wide_ref, small_ref, bias):
    @pl.when(kind == 0)
    def _():
        for head in range(heads):
            wide = wide_ref[head]
            for r in range(SIDE):
                turned = pltpu.roll(wide, 2 * SPAN - SIDE * (SIDE - r), 1)
                bias[head, r * SIDE : (r + 1) * SIDE, :] = turned[:, :SPAN]

    @pl.when(kind != 0)
    def _():
        image = lax.broadcasted_iota(jnp.int32, (HALF, SPAN), 1) // BLOCK
        lane = lax.broadcasted_iota(jnp.int32, (HALF, 2 * BLOCK), 1)
        for head in range(heads):
            small = small_ref[head]
            for r in range(HALF):
                turned = pltpu.roll(small, 2 * BLOCK - HALF * (HALF - r), 1)
                turned = jnp.where(lane < BLOCK, turned, 0.0)
                pair = turned + pltpu.roll(turned, BLOCK, 1)
                line = jnp.concatenate([pair, pair], axis=1)
                for i in range(IMAGES):
                    start = i * BLOCK + r * HALF
                    bias[head, start : start + HALF, :] = jnp.where(image == i, line, MASKED)


def collect_table(heads, kind, back, wide_sum, small_sum):
    @pl.when(kind == 0)
    def _():
        for head in range(heads):
            total = wide_sum[head]
            for r in range(SIDE):
                part = back[head, r * SIDE : (r + 1) * SIDE, :]
                part = jnp.concatenate([part, jnp.zeros_like(part)], axis=1)
                total = total + pltpu.roll(part, SIDE * (SIDE - r), 1)
            wide_sum[head] = total

    @pl.when(kind != 0)
    def _():
        for head in range(heads):
            total = small_sum[head]
            lane = lax.broadcasted_iota(jnp.int32, total.shape, 1)
            for r in range(HALF):
                part = functools.reduce(
                    jnp.add,
                    [
                        back[head, i * BLOCK + r * HALF : i * BLOCK + (r + 1) * HALF, :]
                        for i in range(IMAGES)
                    ],
                )
                part = part[:, : SPAN // 2] + part[:, SPAN // 2 :]
                part = jnp.where(lane < BLOCK, part + pltpu.roll(part, BLOCK, 1), 0.0)
                total = total + pltpu.roll(part, HALF * (HALF - r), 1)
            small_sum[head] = total


def window_of(head, head_dim, width):
    if width <= 256:
        return 0, width
    return head * head_dim // 128 * 128, min(-(-(head + 1) * head_dim // 128) * 128, width)


def mine_of(head, head_dim, first, last, rows):
    lane = lax.broadcasted_iota(jnp.int32, (rows, last - first), 1) + first
    return (lane >= head * head_dim) & (lane < (head + 1) * head_dim)


def softmax_of(queries, keys, bias, scale):
    scores = matmul(keys, queries, NT) * scale + bias
    expo = jnp.exp(scores - jnp.max(scores, axis=0, keepdims=True))
    return expo * (1.0 / jnp.sum(expo, axis=0, keepdims=True))


def attention_forward(heads, row, bias, total):
    count, width = total.shape
    head_dim = width // heads
    scale = 1.0 / math.sqrt(head_dim)
    zero = jnp.zeros((), LOW)
    total[...] = jnp.zeros_like(total)
    for head in range(heads):
        first, last = window_of(head, head_dim, width)
        mine = mine_of(head, head_dim, first, last, count)
        queries = jnp.where(mine, row(0, first, last), zero)
        values = jnp.where(mine, row(2, first, last), zero)
        weights = softmax_of(queries, row(1, first, last), bias[head], scale)
        total[:, first:last] += matmul(weights.astype(LOW), values, TN)


def attention_backward(heads, row, bias, steps, attended, scores_out):
    count, width = steps.shape[1:]
    head_dim = width // heads
    scale = 1.0 / math.sqrt(head_dim)
    zero = jnp.zeros((), LOW)
    steps[...] = jnp.zeros_like(steps)
    if attended is not None:
        attended[...] = jnp.zeros_like(attended)
    for head in range(heads):
        first, last = window_of(head, head_dim, width)
        mine = mine_of(head, head_dim, first, last, count)
        queries, keys, values, upstream = (
            jnp.where(mine, row(member, first, last), zero) for member in range(4)
        )
        weights = softmax_of(queries, keys, bias[head], scale)
        low = weights.astype(LOW)
        back_weights = matmul(values, upstream, NT)
        inner = jnp.sum(weights * back_weights, axis=0, keepdims=True)
        back_scores = (weights * (back_weights - inner)).astype(LOW)
        steps[0, :, first:last] += matmul(back_scores, keys, TN) * scale
        steps[1, :, first:last] += matmul(back_scores, queries) * scale
        steps[2, :, first:last] += matmul(low, upstream)
        if attended is not None:
            attended[:, first:last] += matmul(low, values, TN)
        if scores_out is not None:
            scores_out[head] = back_scores.astype(FULL)


def in_hbm(value):
    return pltpu.with_memory_space_constraint(value, pltpu.HBM)


HBM = pl.BlockSpec(memory_space=pltpu.HBM)
NEAR = pl.BlockSpec(memory_space=pltpu.VMEM)


def plain(kernel, name, scalars, near, far, outs, scratch, flops, size, limit, after=()):
    first = len(scalars) + len(near) + len(far)

    def body(*refs):
        kernel(*refs[:first], *refs[first + len(after) :])

    return pl.pallas_call(
        body,
        in_specs=[
            *[pl.BlockSpec(memory_space=pltpu.SMEM)] * len(scalars),
            *[NEAR] * len(near),
            *[HBM] * (len(far) + len(after)),
        ],
        out_specs=[HBM] * len(outs),
        out_shape=[pltpu.HBM(out.shape, out.dtype) for out in outs],
        scratch_shapes=[*scratch, pltpu.SemaphoreType.DMA((24,))],
        compiler_params=pltpu.CompilerParams(vmem_limit_bytes=limit << 20),
        cost_estimate=pl.CostEstimate(
            flops=int(flops * WEIGHT), bytes_accessed=int(size * WEIGHT), transcendentals=0
        ),
        name=name,
    )(*scalars, *near, *map(in_hbm, (*far, *after)))


def gate(values):
    def body(*refs):
        del refs

    return pl.pallas_call(
        body,
        in_specs=[HBM] * len(values),
        out_specs=[HBM] * len(values),
        out_shape=[pltpu.HBM(value.shape, value.dtype) for value in values],
        input_output_aliases={i: i for i in range(len(values))},
        name="gate",
    )(*map(in_hbm, values))


class Moves:
    def __init__(self):
        self.running, self.found = [], {}

    def start(self, name, steps):
        self.running.append((name, steps, next(steps)))

    def kernel(self, output, due=()):
        arrived = [array for _, _, arrays in self.running for array in arrays]
        held = gate([output, *due, *arrived])
        self.step(iter(held[1 + len(due) :]))
        return held[: 1 + len(due)]

    def chain(self, partial, due=()):
        arrived = [array for _, _, arrays in self.running for array in arrays]
        partial, *rest = gate([partial, *due, *arrived])
        partial, other, *rest = gate([partial, swap(partial, "tensor"), *rest])
        self.step(iter(rest[len(due) :]))
        return partial, other, *rest[: len(due)]

    def hurry(self, name):
        if name in self.found:
            return self.found[name]
        others = [entry for entry in self.running if entry[0] != name]
        self.running = [entry for entry in self.running if entry[0] == name]
        self.finish()
        self.running = others
        return self.found[name]

    def step(self, arrived=None):
        before, self.running = self.running, []
        for name, steps, arrays in before:
            if arrived is not None:
                arrays = [next(arrived) for _ in arrays]
            try:
                self.running.append((name, steps, steps.send(arrays)))
            except StopIteration as stop:
                self.found[name] = stop.value

    def finish(self):
        while self.running:
            self.step()


class Copies:
    def __init__(self, sems):
        self.sems, self.count, self.leaving = sems, 0, []

    def start(self, source, target):
        copy = pltpu.make_async_copy(source, target, self.sems.at[self.count])
        self.count += 1
        copy.start()
        return copy

    def leave(self, source, target):
        self.leaving.append(self.start(source, target))

    def finish(self):
        for copy in self.leaving:
            copy.wait()


def core_half(ref, ids):
    half = ref.shape[0] // 2
    return ref.at[pl.ds(pl.multiple_of(ids[AT_CORE] * half, half), half)]


def attend_kernel(layer, heads, ids, gain_ref, shift_ref, biases_ref, *refs):
    parts = 1 if layer == 0 else 3
    stream_hbm, refs = refs[:parts], refs[parts:]
    token_hbm, out_hbm, image_hbm, wide_hbm, small_hbm = refs[:5]
    stream_out, normed_out, half_out, row_out, partial_out, bias_out = refs[5:11]
    stream_in, token, outer, image, wide, small, normed, low, rows, bias, total, partial, sems = refs[11:]
    copies = Copies(sems)
    per = pl.ds(layer * heads, heads)
    near = [copies.start(source, stream_in.at[i]) for i, source in enumerate(stream_hbm)]
    tables = [copies.start(wide_hbm.at[per], wide), copies.start(small_hbm.at[per], small)]
    tokens = [copies.start(token_hbm.at[layer, 0], token.at[0])]
    images = copies.start(image_hbm.at[layer], image)
    tokens += [copies.start(token_hbm.at[layer, m], token.at[m]) for m in (1, 2)]
    outers = copies.start(out_hbm.at[layer], outer)
    kind = ids[KIND]
    count = low.shape[0]
    for copy in near:
        copy.wait()
    if layer == 0:
        stream = stream_in[0].astype(FULL)
    else:
        stream = stream_in[0] + (stream_in[1] + stream_in[2]) + biases_ref[layer - 1, 1:2, :]
    normed[...] = normal_of(stream)[0] * gain_ref[layer, 0:1, :] + shift_ref[layer, 0:1, :]
    if layer == 0:
        partial[...] = stream
        copies.leave(partial, stream_out)
    else:
        stream_in[0] = stream
        copies.leave(stream_in.at[0], stream_out)
    copies.leave(normed, normed_out)
    copies.leave(core_half(normed, ids), half_out)
    low[...] = normed[...].astype(LOW)
    for copy in tables:
        copy.wait()
    fill_bias(heads, kind, wide, small, bias)
    copies.leave(bias, bias_out)
    for member in range(3):
        tokens[member].wait()
        projected = matmul(low[...], token[member], NT)
        if member == 0:
            images.wait()
        if member == 1:
            rows[member] = projected.astype(LOW)
            continue
        for i in range(IMAGES):
            mine = image[member // 2, i : i + 1, :]
            mine = jnp.where(kind != 0, mine, image[member // 2, 0:1, :])
            here = slice(i * (count // IMAGES), (i + 1) * (count // IMAGES))
            rows[member, here, :] = (projected[here] + mine).astype(LOW)
    copies.leave(rows, row_out)

    def row(index, first, last):
        return rows[index, :, first:last]

    attention_forward(heads, row, bias, total)
    outers.wait()
    if layer == 0:
        copies.leaving.pop(0).wait()
    partial[...] = matmul(total[...].astype(LOW), outer[...])
    copies.leave(partial, partial_out)
    copies.finish()


def attend(layer, ids, stream, gains, shifts, biases, token_rows, per_image, out_proj, wide, small, after=()):
    count, width = stream[0].shape
    depth, _, local, _ = token_rows.shape
    heads = wide.shape[0] // depth
    full = shape_of((count, width))
    outs = [
        full,
        full,
        shape_of((count // 2, width)),
        shape_of((3, count, local), LOW),
        full,
        shape_of((heads, count, count)),
    ]
    return plain(
        functools.partial(attend_kernel, layer, heads),
        f"attend_{layer}",
        (ids,),
        (gains, shifts, biases),
        (*stream, token_rows, out_proj, per_image, wide, small),
        outs,
        [
            pltpu.VMEM((len(stream), count, width), stream[0].dtype),
            pltpu.VMEM((3, local, width), LOW),
            pltpu.VMEM((local, width), LOW),
            pltpu.VMEM(per_image.shape[1:], FULL),
            pltpu.VMEM((heads, *wide.shape[1:]), FULL),
            pltpu.VMEM((heads, *small.shape[1:]), FULL),
            pltpu.VMEM((count, width), FULL),
            pltpu.VMEM((count, width), LOW),
            pltpu.VMEM((3, count, local), LOW),
            pltpu.VMEM((heads, count, count), FULL),
            pltpu.VMEM((count, local), FULL),
            pltpu.VMEM((count, width), FULL),
        ],
        2 * count * width * local * 4,
        8 * width * local + 16 * count * width,
        40,
        after,
    )


CHUNK = 768


def feed_kernel(layer, ids, gain_ref, shift_ref, biases_ref, stream_hbm, part_hbm, other_hbm, in_hbm_ref, out_hbm_ref, middle_out, half_out, slope_out, partial_out, stream_in, inner, outer, normed, low, slope, partial, sems):
    units = inner.shape[1]
    chunks = [slice(at, at + CHUNK) for at in range(0, units, CHUNK)]
    copies = Copies(sems)
    near = [
        copies.start(source, stream_in.at[i])
        for i, source in enumerate((stream_hbm, part_hbm, other_hbm))
    ]
    weights = [
        (
            copies.start(in_hbm_ref.at[layer, :, chunk], inner.at[:, chunk]),
            copies.start(out_hbm_ref.at[layer, chunk, :], outer.at[chunk, :]),
        )
        for chunk in chunks
    ]
    for copy in near:
        copy.wait()
    middle = stream_in[0] + (stream_in[1] + stream_in[2]) + biases_ref[layer, 0:1, :]
    stream_in[0] = middle
    copies.leave(stream_in.at[0], middle_out)
    normed[...] = normal_of(middle)[0] * gain_ref[layer, 1:2, :] + shift_ref[layer, 1:2, :]
    copies.leave(core_half(normed, ids), half_out)
    low[...] = normed[...].astype(LOW)
    for at, chunk in enumerate(chunks):
        weights[at][0].wait()
        hidden = matmul(low[...], inner[:, chunk])
        rise = 0.5 * (1.0 + lax.erf(hidden * ROOT_HALF))
        slope[:, chunk] = rise + hidden * jnp.exp(-0.5 * hidden * hidden) * SLOPE_NORM
        copies.leave(slope.at[:, chunk], slope_out.at[:, chunk])
        weights[at][1].wait()
        product = matmul((hidden * rise).astype(LOW), outer[chunk, :])
        partial[...] = product if at == 0 else partial[...] + product
    copies.leave(partial, partial_out)
    copies.finish()


def feed(layer, ids, stream, partial, other, biases, gains, shifts, hidden_in, hidden_out, after=()):
    count, width = stream.shape
    units = hidden_in.shape[2]
    full = shape_of((count, width))
    return plain(
        functools.partial(feed_kernel, layer),
        f"feed_{layer}",
        (ids,),
        (gains, shifts, biases),
        (stream, partial, other, hidden_in, hidden_out),
        [full, shape_of((count // 2, width)), shape_of((count, units)), full],
        [
            pltpu.VMEM((3, count, width), FULL),
            pltpu.VMEM((width, units), LOW),
            pltpu.VMEM((units, width), LOW),
            pltpu.VMEM((count, width), FULL),
            pltpu.VMEM((count, width), LOW),
            pltpu.VMEM((count, units), FULL),
            pltpu.VMEM((count, width), FULL),
        ],
        4 * count * width * units,
        4 * width * units + 4 * count * (units + 6 * width),
        48,
        after,
    )


def feed_back_kernel(layer, last, ids, gain_ref, *refs):
    parts = 1 if last else 4
    up_hbm, refs = refs[:parts], refs[parts:]
    slope_hbm, in_hbm_ref, out_hbm_ref, upstream_out, half_out, sums_out, partial_out = refs[:7]
    up_in, inner, outer, upstream, low, slope, sums, partial, sems = refs[7:]
    units = inner.shape[1]
    chunks = [slice(at, at + CHUNK) for at in range(0, units, CHUNK)]
    copies = Copies(sems)
    near = [copies.start(source, up_in.at[i]) for i, source in enumerate(up_hbm)]
    weights = [
        (
            copies.start(out_hbm_ref.at[layer, chunk, :], outer.at[chunk, :]),
            copies.start(slope_hbm.at[:, chunk], slope.at[:, chunk]),
            copies.start(in_hbm_ref.at[layer, :, chunk], inner.at[:, chunk]),
        )
        for chunk in chunks
    ]
    for copy in near:
        copy.wait()
    sums[...] = jnp.zeros_like(sums)
    if last:
        upstream[...] = up_in[0].astype(FULL)
    else:
        step, gain_part, shift_part = norm_backward(
            up_in[3], gain_ref[layer + 1, 0:1, :], up_in[1] + up_in[2]
        )
        upstream[...] = up_in[0] + step
        sums[1:2, :] = gain_part
        sums[2:3, :] = shift_part
    copies.leave(upstream, upstream_out)
    copies.leave(core_half(upstream, ids), half_out)
    low[...] = upstream[...].astype(LOW)
    sums[0:1, :] = jnp.sum(low[...].astype(FULL), axis=0, keepdims=True)
    copies.leave(sums, sums_out)
    for at, chunk in enumerate(chunks):
        weights[at][0].wait()
        back = matmul(low[...], outer[chunk, :], NT)
        weights[at][1].wait()
        weights[at][2].wait()
        product = matmul((back * slope[:, chunk]).astype(LOW), inner[:, chunk], NT)
        partial[...] = product if at == 0 else partial[...] + product
    copies.leave(partial, partial_out)
    copies.finish()


def feed_back(layer, ids, upstream, slope, hidden_in, hidden_out, gains, after=()):
    count, width = upstream[0].shape
    units = hidden_in.shape[2]
    full = shape_of((count, width))
    return plain(
        functools.partial(feed_back_kernel, layer, len(upstream) == 1),
        f"feed_back_{layer}",
        (ids,),
        (gains,),
        (*upstream, slope, hidden_in, hidden_out),
        [full, shape_of((count // 2, width)), shape_of((8, width)), full],
        [
            pltpu.VMEM((len(upstream), count, width), upstream[0].dtype),
            pltpu.VMEM((width, units), LOW),
            pltpu.VMEM((units, width), LOW),
            pltpu.VMEM((count, width), FULL),
            pltpu.VMEM((count, width), LOW),
            pltpu.VMEM((count, units), FULL),
            pltpu.VMEM((8, width), FULL),
            pltpu.VMEM((count, width), FULL),
        ],
        4 * count * width * units,
        4 * width * units + 4 * count * (units + 6 * width),
        48,
        after,
    )


def attend_back_kernel(layer, heads, ids, gain_ref, up_hbm, part_hbm, other_hbm, middle_hbm, row_hbm, bias_hbm, out_hbm, token_hbm, back_out, half_out, sums_out, partial_out, up_in, rows, bias, token, outer, back, sums, upstream, steps, partial, sems):
    copies = Copies(sems)
    near = [
        copies.start(source, up_in.at[i])
        for i, source in enumerate((up_hbm, part_hbm, other_hbm, middle_hbm))
    ]
    outers = copies.start(out_hbm.at[layer], outer)
    saved = [copies.start(row_hbm, rows), copies.start(bias_hbm, bias)]
    tokens = [copies.start(token_hbm.at[layer, member], token.at[member]) for member in range(3)]
    for copy in near:
        copy.wait()
    step, gain_part, shift_part = norm_backward(
        up_in[3], gain_ref[layer, 1:2, :], up_in[1] + up_in[2]
    )
    back[...] = up_in[0] + step
    copies.leave(back, back_out)
    copies.leave(core_half(back, ids), half_out)
    rounded = back[...].astype(LOW)
    sums[...] = jnp.zeros_like(sums)
    sums[0:1, :] = jnp.sum(rounded.astype(FULL), axis=0, keepdims=True)
    sums[1:2, :] = gain_part
    sums[2:3, :] = shift_part
    copies.leave(sums, sums_out)
    outers.wait()
    upstream[...] = matmul(rounded, outer[...], NT).astype(LOW)

    def row(index, first, last):
        return upstream[:, first:last] if index == 3 else rows[index, :, first:last]

    for copy in saved:
        copy.wait()
    attention_backward(heads, row, bias, steps, None, None)
    for member in range(3):
        tokens[member].wait()
        product = matmul(steps[member].astype(LOW), token[member])
        partial[...] = product if member == 0 else partial[...] + product
    copies.leave(partial, partial_out)
    copies.finish()


def attend_back(layer, ids, upstream, partial, other, middle, gains, rows, bias, out_proj, token_rows, after=()):
    count, width = upstream.shape
    local = token_rows.shape[2]
    heads = bias.shape[0]
    full = shape_of((count, width))
    return plain(
        functools.partial(attend_back_kernel, layer, heads),
        f"attend_back_{layer}",
        (ids,),
        (gains,),
        (upstream, partial, other, middle, rows, bias, out_proj, token_rows),
        [full, shape_of((count // 2, width)), shape_of((8, width)), full],
        [
            pltpu.VMEM((4, count, width), FULL),
            pltpu.VMEM((3, count, local), LOW),
            pltpu.VMEM((heads, count, count), FULL),
            pltpu.VMEM((3, local, width), LOW),
            pltpu.VMEM((local, width), LOW),
            pltpu.VMEM((count, width), FULL),
            pltpu.VMEM((8, width), FULL),
            pltpu.VMEM((count, local), LOW),
            pltpu.VMEM((3, count, local), FULL),
            pltpu.VMEM((count, width), FULL),
        ],
        2 * count * width * local * 4 + heads * count * count * 4096,
        8 * width * local + 24 * count * width,
        40,
        after,
    )


def finish_kernel(gain_ref, up_hbm, part_hbm, other_hbm, stream_hbm, gradient_out, sums_out, up_in, gradient, sums, sems):
    copies = Copies(sems)
    near = [
        copies.start(source, up_in.at[i])
        for i, source in enumerate((up_hbm, part_hbm, other_hbm, stream_hbm))
    ]
    for copy in near:
        copy.wait()
    step, gain_part, shift_part = norm_backward(up_in[3], gain_ref[0, 0:1, :], up_in[1] + up_in[2])
    gradient[...] = (up_in[0] + step).astype(LOW)
    copies.leave(gradient, gradient_out)
    sums[...] = jnp.zeros_like(sums)
    sums[1:2, :] = gain_part
    sums[2:3, :] = shift_part
    copies.leave(sums, sums_out)
    copies.finish()


def finish(upstream, partial, other, stream, gains):
    count, width = stream.shape
    return plain(
        finish_kernel,
        "finish",
        (),
        (gains,),
        (upstream, partial, other, stream),
        [shape_of((count, width), LOW), shape_of((8, width))],
        [
            pltpu.VMEM((4, count, width), FULL),
            pltpu.VMEM((count, width), LOW),
            pltpu.VMEM((8, width), FULL),
        ],
        0,
        20 * count * width,
        24,
    )


def line_window(units, line):
    own = units // line
    offsets = [z * own % 128 for z in range(line)]
    size = -(-(max(offsets) + own) // 128) * 128
    starts = [min(z * own // 128 * 128, units - size) for z in range(line)]
    return starts, [z * own - starts[z] for z in range(line)], size


def feed_gradients_kernel(layer, line, ids, x_hbm, y_hbm, in_hbm, out_hbm, outer_keep, outer_send, inner_keep, inner_send, stage, part_in, part_out, low_x, low_y, active, back, outer, inner, sems):
    units = in_hbm.shape[2]
    width = low_x.shape[1]
    rows = stage.shape[2]
    own = units // line
    starts, offsets, size = line_window(units, line)
    at = ids[AT_LINE]
    start, offset = jnp.int32(starts[0]), jnp.int32(offsets[0])
    for z in range(1, line):
        start = jnp.where(at == z, starts[z], start)
        offset = jnp.where(at == z, offsets[z], offset)
    start = pl.multiple_of(start, 128)
    copies = [
        pltpu.make_async_copy(in_hbm.at[layer, :, pl.ds(start, size)], part_in, sems.at[0, 2]),
        pltpu.make_async_copy(out_hbm.at[layer, pl.ds(start, size), :], part_out, sems.at[1, 2]),
    ]

    def fetch(tile):
        slot = tile % 2
        return [
            pltpu.make_async_copy(
                source.at[pl.ds(tile * rows, rows)], stage.at[side, slot], sems.at[side, slot]
            )
            for side, source in enumerate((x_hbm, y_hbm))
        ]

    flying = {0: fetch(0)}
    for copy in (*flying[0], *copies):
        copy.start()
    for tile in range(line):
        if tile + 1 < line:
            flying[tile + 1] = fetch(tile + 1)
            for copy in flying[tile + 1]:
                copy.start()
        for copy in flying[tile]:
            copy.wait()
        if tile == 0:
            for copy in copies:
                copy.wait()
        here = slice(tile * rows, (tile + 1) * rows)
        low_x[here, :] = stage[0, tile % 2].astype(LOW)
        low_y[here, :] = stage[1, tile % 2].astype(LOW)
        hidden = matmul(low_x[here, :], part_in[...])
        rise = 0.5 * (1.0 + lax.erf(hidden * ROOT_HALF))
        active[here, :] = (hidden * rise).astype(LOW)
        slope = rise + hidden * jnp.exp(-0.5 * hidden * hidden) * SLOPE_NORM
        back[here, :] = (matmul(low_y[here, :], part_out[...], NT) * slope).astype(LOW)

    @pl.loop(0, size // 128)
    def _(tile):
        lanes = pl.ds(pl.multiple_of(tile * 128, 128), 128)
        outer[lanes, :] = matmul(active[:, lanes], low_y[...], TN)

    @pl.loop(0, width // 128)
    def _(tile):
        lanes = pl.ds(pl.multiple_of(tile * 128, 128), 128)
        inner[lanes, :] = matmul(low_x[:, lanes], back[...], TN)

    pair = own // 2
    step = width // (GROUP * line)
    for z in range(len(set(offsets))):
        shifted = sorted(set(offsets))[z]
        for col in range(2):

            @pl.when((offset == shifted) & (ids[AT_COL] == col))
            def _(shifted=shifted, col=col):
                for target, part in ((outer_keep, col), (outer_send, 1 - col)):
                    first = shifted + part * pair
                    for r in range(2):
                        begin = first + r * (pair // 2)
                        target[r] = outer[begin : begin + pair // 2, :]

    for row in range(2):

        @pl.when(ids[AT_ROW] == row)
        def _(row=row):
            for z in range(line):
                for c in range(2):
                    for target, part in ((inner_keep, row), (inner_send, 1 - row)):
                        begin = (GROUP * z + 2 * c + part) * step
                        target[c, z] = inner[begin : begin + step, :]


def feed_gradients(layer, line, ids, xs, ys, hidden_in, hidden_out, after=()):
    count, width = xs.shape
    rows = count // line
    units = hidden_in.shape[2]
    own = units // line
    size = line_window(units, line)[2]
    anywhere = pl.BlockSpec(memory_space=pl.ANY)
    outs = [shape_of((2, own // 4, width))] * 2 + [shape_of((2, line, width // (GROUP * line), size))] * 2
    return call(
        functools.partial(feed_gradients_kernel, layer, line),
        f"feed_gradients_{layer}",
        (1,),
        [anywhere] * 2 + [pl.BlockSpec(memory_space=pltpu.HBM)] * 2,
        [whole_once(out.shape) for out in outs],
        outs,
        [
            pltpu.VMEM((2, 2, rows, width), FULL),
            pltpu.VMEM((width, size), LOW),
            pltpu.VMEM((size, width), LOW),
            pltpu.VMEM((line * rows, width), LOW),
            pltpu.VMEM((line * rows, width), LOW),
            pltpu.VMEM((line * rows, size), LOW),
            pltpu.VMEM((line * rows, size), LOW),
            pltpu.VMEM((size, width), FULL),
            pltpu.VMEM((width, size), FULL),
            pltpu.SemaphoreType.DMA((2, 3)),
        ],
        8 * line * rows * width * size,
        8 * line * rows * width + 16 * width * size,
        after=after,
    )(ids, *map(in_hbm, (xs, ys, hidden_in, hidden_out)))


def whole_call(kernel, name, scalars, near, outs, scratch=(), limit=40):
    return pl.pallas_call(
        kernel,
        in_specs=[
            *[pl.BlockSpec(memory_space=pltpu.SMEM)] * len(scalars),
            *[NEAR] * len(near),
        ],
        out_specs=[NEAR] * len(outs),
        out_shape=[pltpu.HBM(out.shape, out.dtype) for out in outs],
        scratch_shapes=list(scratch),
        compiler_params=pltpu.CompilerParams(vmem_limit_bytes=limit << 20),
        cost_estimate=pl.CostEstimate(
            flops=WHOLE_COST, bytes_accessed=WHOLE_COST // 300, transcendentals=0
        ),
        name=name,
    )(*scalars, *map(in_hbm, near))


def feed_halve_kernel(ids, outer_keep, outer_half, inner_keep, inner_half, outer_own, outer_send, inner_own, inner_send):
    row, col = ids[AT_ROW], ids[AT_COL]
    outer_own[...] = outer_keep[row] + outer_half[row]
    outer_send[...] = outer_keep[1 - row] + outer_half[1 - row]
    inner_own[...] = inner_keep[col] + inner_half[col]
    inner_send[...] = inner_keep[1 - col] + inner_half[1 - col]


def feed_deal_kernel(depth, line, ids, *refs):
    parts, outs = refs[: 2 * depth], refs[2 * depth :]
    place = ids[AT_LINE]
    for by in range(line):
        to = lax.rem(place + by, line)
        for layer in range(depth):
            outs[by][layer] = parts[2 * layer][to] + parts[2 * layer + 1][to]


def feed_deal(depth, line, ids, parts):
    block = parts[0].shape[1:]
    return whole_call(
        functools.partial(feed_deal_kernel, depth, line),
        "feed_deal",
        (ids,),
        parts,
        [shape_of((depth, *block))] * line,
    )


def feed_scatter(layer, ids, pieces, line):
    outer_keep, outer_send, inner_keep, inner_send = pieces
    outer_half, inner_half = yield [swap(outer_send, "col"), swap(inner_send, "row")]
    outer_part, inner_part = shape_of(outer_keep.shape[1:]), shape_of(inner_keep.shape[1:])
    outer_own, outer_send, inner_own, inner_send = whole_call(
        feed_halve_kernel,
        f"feed_halve_{layer}",
        (ids,),
        (outer_keep, outer_half, inner_keep, inner_half),
        [outer_part, outer_part, inner_part, inner_part],
    )
    outer_other, inner_other = yield [swap(outer_send, "row"), swap(inner_send, "col")]
    return [inner_own, inner_other], [outer_own, outer_other]


def attention_deal_kernel(layer, line, heads, at_rows, ids, summed, embedded, *refs):
    images, projection, outs = refs[:line], refs[line], refs[line + 1 :]
    own = images[0].shape[1]
    chunk, lanes, left = at_rows.chunk, at_rows.LANES, at_rows.left
    features = chunk // GROUP
    for third in range(3):
        row = at_rows.projection + third * at_rows.piece
        projection[:, third * lanes : (third + 1) * lanes] = summed[row : row + at_rows.piece, :]
    time = []
    for member in range(2):
        every = jnp.concatenate(
            [ref[member * GROUP * IMAGES : (member + 1) * GROUP * IMAGES, :] for ref in images],
            axis=0,
        )
        high = every.astype(LOW)
        middle = (every - high.astype(FULL)).astype(LOW)
        low = (every - high.astype(FULL) - middle.astype(FULL)).astype(LOW)
        time.append(
            matmul(embedded[...], high, TN)
            + (matmul(embedded[...], middle, TN) + matmul(embedded[...], low, TN))
        )
    at = 2 * ids[AT_COL] + ids[AT_ROW]
    entries = 4 * SPAN // line // GROUP
    fold = chunk // at_rows.folds
    for j in range(GROUP):

        @pl.when(at == j)
        def _(j=j):
            for by in range(GROUP):
                to, out = j ^ by, outs[by]
                here = slice(to * features, (to + 1) * features)
                out[:features, :lanes] = summed[here, :]
                for i in range(at_rows.folds):
                    first, last = max(i * fold, here.start), min((i + 1) * fold, here.stop)
                    if first < last:
                        row = at_rows.folded - i * fold
                        out[first - here.start : last - here.start, lanes : 3 * own] = summed[
                            row + first : row + last, i * left : (i + 1) * left
                        ]
                for member in range(2):
                    out[:features, (3 + member) * own : (4 + member) * own] = time[member][here]
                out[features:, :] = jnp.zeros((out.shape[0] - features, 5 * own), FULL)
                out[features : features + heads, :entries] = summed[
                    at_rows.table : at_rows.table + heads, to * entries : (to + 1) * entries
                ]
                if layer == 0:
                    first = features + TABLE_ROWS
                    out[first : first + VECTORS, :features] = summed[
                        at_rows.vectors : at_rows.vectors + VECTORS, here
                    ]


def attention_deal(layer, line, ids, summed, embedded, images, heads, width, own):
    at_rows = Rows(own, width, heads, VECTORS if layer == 0 else 0, line)
    rows = width // line // GROUP + TABLE_ROWS + (VECTOR_ROWS if layer == 0 else 0)
    projection, *blocks = whole_call(
        functools.partial(attention_deal_kernel, layer, line, heads, at_rows),
        f"attention_deal_{layer}",
        (ids,),
        (summed, embedded, *images),
        [shape_of((own // line, width))] + [shape_of((rows, 5 * own))] * GROUP,
    )
    moved = lax.ppermute(
        projection,
        LINES,
        [(GROUP * z + j, line * j + z) for z in range(line) for j in range(GROUP)],
    )
    projection, across, along, corner = yield [
        moved,
        swap(blocks[1], "row"),
        swap(blocks[2], "col"),
        swap_corner(blocks[3]),
    ]
    return projection, [blocks[0], across, along, corner]


def join_feed_kernel(depth, line, ids, *refs):
    inners, outers, (inner, outer, order) = refs[:line], refs[line : line + 2 * depth], refs[line + 2 * depth :]
    part = inner.shape[2] // line
    offsets = line_window(inner.shape[2], line)[1]
    for by in range(line):
        order[lax.rem(ids[AT_LINE] + line - by, line)] = inners[by][...]
    for layer in range(depth):
        outer[layer] = outers[2 * layer][...] + outers[2 * layer + 1][...]
        for z in range(line):
            inner[layer, :, z * part : (z + 1) * part] = order[
                z, layer, :, offsets[z] : offsets[z] + part
            ]


def join_feed(line, ids, blocks, outers, units):
    depth, features, size = blocks[0].shape
    rows, width = outers[0].shape
    return whole_call(
        functools.partial(join_feed_kernel, depth, line),
        "join_feed",
        (ids,),
        (*blocks, *outers),
        [shape_of((depth, features, units)), shape_of((depth, rows, width))],
        [pltpu.VMEM((line, depth, features, size), FULL)],
    )


def join_attention_kernel(depth, heads, ids, *refs):
    blocks, refs = refs[: depth * GROUP], refs[depth * GROUP :]
    projections, refs = refs[:depth], refs[depth:]
    token, time, table, projection, gain, shift_out, bias = refs
    features, local = token.shape[2:]
    own = local // GROUP
    entries = table.shape[2]
    at = 2 * ids[AT_COL] + ids[AT_ROW]
    for layer in range(depth):
        projection[:, layer, :] = projections[layer][...]
    for j in range(GROUP):

        @pl.when(at == j)
        def _(j=j):
            for layer in range(depth):
                for by in range(GROUP):
                    ref, source = blocks[layer * GROUP + by], j ^ by
                    lanes = slice(source * own, (source + 1) * own)
                    for member in range(3):
                        token[layer, member, :, lanes] = ref[
                            :features, member * own : (member + 1) * own
                        ]
                    for member in range(2):
                        time[layer, member, :, lanes] = ref[
                            :features, (3 + member) * own : (4 + member) * own
                        ]
                    table[layer, source * heads : (source + 1) * heads, :] = ref[
                        features : features + heads, :entries
                    ]

    first = features + TABLE_ROWS
    total = functools.reduce(
        jnp.add, [blocks[by][first : first + 6 * depth, :features] for by in range(GROUP)]
    )
    for kind, out in enumerate((gain, shift_out, bias)):
        for layer in range(depth):
            begin = (kind * depth + layer) * 2
            out[layer] = total[begin : begin + 2]


def join_attention(depth, line, ids, attention, heads, local, width):
    features = width // (GROUP * line)
    vector = shape_of((depth, 2, features))
    return whole_call(
        functools.partial(join_attention_kernel, depth, heads // GROUP),
        "join_attention",
        (ids,),
        (
            *[block for layer in range(depth) for block in attention[layer][1]],
            *[attention[layer][0] for layer in range(depth)],
        ),
        [
            shape_of((depth, 3, features, local)),
            shape_of((depth, 2, features, local)),
            shape_of((depth, heads, 4 * SPAN // (GROUP * line))),
            shape_of((local // (GROUP * line), depth, width)),
            vector,
            vector,
            vector,
        ],
    )


class Rows:
    LANES = 384

    def __init__(self, own, width, heads, vectors, line):
        self.chunk, self.piece = width // line, own // line
        self.left = 3 * own - self.LANES
        self.folds = self.LANES // self.left
        self.folded = self.chunk
        self.projection = self.folded + self.chunk // self.folds
        self.table = self.projection + 3 * self.piece
        self.vectors = self.table + heads
        self.total = -(-(self.vectors + vectors) // 8) * 8


VECTORS = 12
TABLE_ROWS, VECTOR_ROWS = 8, 16


def attention_gradients_kernel(layer, heads, line, vector_count, ids, kinds, *refs):
    parts = 2 * GROUP - 1
    sources = refs[:parts], refs[parts : 2 * parts]
    token_hbm, out_hbm = refs[2 * parts : 2 * parts + 2]
    image_hbm = refs[2 * parts + 2 : 2 * parts + 2 + GROUP]
    refs = refs[2 * parts + 2 + GROUP :]
    wide_ref, small_ref = refs[:2]
    vectors, refs = refs[2 : 2 + vector_count], refs[2 + vector_count :]
    token_out, images_out = refs[:2]
    (images, low_x, low_y, joined, attended_low, rows, bias, steps, attended) = refs[2:11]
    wide_sum, small_sum, stage, token, outer, scores, image_all, sems, weight_sems = refs[11:]
    slot = pl.program_id(0)
    kind = kinds[slot]
    count = low_x.shape[1]
    half = count // 2
    own = images.shape[2]
    at = 2 * ids[AT_COL] + ids[AT_ROW]

    def fetch(near):
        if near == 0:
            return [
                pltpu.make_async_copy(sources[side][0], stage.at[side, 0], sems.at[side, 0])
                for side in range(2)
            ]
        return [
            pltpu.make_async_copy(
                sources[side][(far + 1) * (GROUP - 1) + near - GROUP + 1],
                stage.at[side, near, pl.ds(pl.multiple_of(place * half, half), half)],
                sems.at[side, 2 * near + far - 1],
            )
            for side in range(2)
            for far, place in enumerate((ids[AT_CORE], 1 - ids[AT_CORE]))
        ]

    mine = pl.ds(pl.multiple_of(at * own, 16), own)
    weights = [
        pltpu.make_async_copy(token_hbm.at[layer, :, mine, :], token, weight_sems.at[0]),
        pltpu.make_async_copy(out_hbm.at[layer, mine, :], outer, weight_sems.at[1]),
        *[
            pltpu.make_async_copy(image_hbm[near], image_all.at[near], weight_sems.at[2 + near])
            for near in range(GROUP)
        ],
    ]

    @pl.when(slot == 0)
    def _():
        for copy in (*fetch(0), *weights):
            copy.start()
        for near in range(1, GROUP):
            for copy in fetch(near):
                copy.start()
        wide_sum[...] = jnp.zeros_like(wide_sum)
        small_sum[...] = jnp.zeros_like(small_sum)
    for near in range(GROUP):

        @pl.when(slot == near)
        def _(near=near):
            for copy in fetch(near):
                copy.wait()

    @pl.when(slot == 0)
    def _():
        for copy in weights:
            copy.wait()
        for j in range(GROUP):

            @pl.when(at == j)
            def _(j=j):
                for member in range(2):
                    first = (2 * layer + member) * IMAGES
                    for near in range(GROUP):
                        images[member, near * IMAGES : (near + 1) * IMAGES, :] = image_all[
                            near, first : first + IMAGES, j * own : (j + 1) * own
                        ]

    fill_bias(heads, kind, wide_ref, small_ref, bias)
    low_x[slot] = stage[0, slot].astype(LOW)
    low_y[slot] = stage[1, slot].astype(LOW)
    for member in range(3):
        projected = matmul(low_x[slot], token[member], NT)
        for i in range(IMAGES):
            here = slice(i * (count // IMAGES), (i + 1) * (count // IMAGES))
            if member == 1:
                rows[member, here, :] = projected[here].astype(LOW)
            else:
                near = images[member // 2]
                first = near[0:1, :]
                mine = near[i : i + 1, :]
                for other in range(1, GROUP):
                    begin = other * IMAGES
                    first = jnp.where(slot == other, near[begin : begin + 1, :], first)
                    mine = jnp.where(slot == other, near[begin + i : begin + i + 1, :], mine)
                mine = jnp.where(kind != 0, mine, first)
                rows[member, here, :] = (projected[here] + mine).astype(LOW)
    rows[3] = matmul(low_y[slot], outer[...], NT).astype(LOW)

    def row(index, first, last):
        return rows[index, :, first:last]

    attention_backward(heads, row, bias, steps, attended, scores)
    collect_table(heads, kind, scores, wide_sum, small_sum)
    attended_low[slot] = attended[...].astype(LOW)
    for member in range(3):
        rounded = steps[member].astype(LOW)
        joined[slot, :, member * own : (member + 1) * own] = rounded
        if member != 1:
            sums = [
                jnp.sum(
                    rounded[i * (count // IMAGES) : (i + 1) * (count // IMAGES)].astype(FULL),
                    axis=0,
                    keepdims=True,
                )
                for i in range(IMAGES)
            ]
            everything = sums[0] + sums[1] + sums[2] + sums[3]
            for i in range(IMAGES):
                alone = everything if i == 0 else jnp.zeros_like(everything)
                images_out[0, member // 2, i : i + 1, :] = jnp.where(kind != 0, sums[i], alone)

    @pl.when(slot == GROUP - 1)
    def _():
        flat = GROUP * count
        width = low_x.shape[2]

        product = matmul(low_x[...].reshape(flat, width), joined[...].reshape(flat, -1), TN)
        projection = matmul(
            attended_low[...].reshape(flat, -1), low_y[...].reshape(flat, -1), TN
        )
        tables = [fold_table(wide_sum[head], small_sum[head]) for head in range(heads)]
        size, cells = width // 3, 4 * SPAN // line
        at_rows = Rows(own, width, heads, VECTORS if vectors else 0, line)
        chunk, lanes, left = at_rows.chunk, at_rows.LANES, at_rows.left
        fold = chunk // at_rows.folds
        for z in range(line):
            begin = z * at_rows.total
            token_out[begin : begin + chunk, :] = product[z * chunk : (z + 1) * chunk, :lanes]
            row = begin + at_rows.folded
            for i in range(at_rows.folds):
                first = z * chunk + i * fold
                token_out[row : row + fold, i * left : (i + 1) * left] = product[
                    first : first + fold, lanes:
                ]
            for third in range(3):
                row = begin + at_rows.projection + third * at_rows.piece
                token_out[row : row + at_rows.piece, :] = projection[
                    z * at_rows.piece : (z + 1) * at_rows.piece, third * size : (third + 1) * size
                ]
            row = begin + at_rows.table
            token_out[row : begin + at_rows.total, :] = jnp.zeros(
                (at_rows.total - at_rows.table, lanes), FULL
            )
            for head in range(heads):
                token_out[row + head : row + head + 1, :cells] = tables[head][
                    :, z * cells : (z + 1) * cells
                ]
            row = begin + at_rows.vectors
            for i, (ref, r) in enumerate(vector_places(vectors)):
                token_out[row + i : row + i + 1, :chunk] = ref[
                    r : r + 1, z * chunk : (z + 1) * chunk
                ]


def vector_places(vectors):
    if not vectors:
        return []
    depth = (len(vectors) - 1) // 2
    feeds, middles = vectors[1 : 1 + depth], vectors[1 + depth :]
    firsts = [vectors[0], *feeds]
    return (
        [place for l in range(depth) for place in ((firsts[l], 1), (middles[l], 1))]
        + [place for l in range(depth) for place in ((firsts[l], 2), (middles[l], 2))]
        + [place for l in range(depth) for place in ((middles[l], 0), (feeds[l], 0))]
    )


def attention_gradients(layer, line, ids, kinds, near_x, near_y, token_rows, images, out_proj, wide, small, vectors, after=()):
    count, width = near_x[0].shape
    depth, _, local, _ = token_rows.shape
    own, heads = local // GROUP, wide.shape[0] // depth // GROUP
    near = [HBM] * (len(near_x) + len(near_y))
    at_rows = Rows(own, width, heads, VECTORS if vectors else 0, line)

    def own_heads(slot, ids, kinds):
        return (layer * GROUP + 2 * ids[AT_COL] + ids[AT_ROW], 0, 0)

    outs = [
        shape_of((line * at_rows.total, at_rows.LANES)),
        shape_of((GROUP, 2, IMAGES, own)),
    ]
    return call(
        functools.partial(attention_gradients_kernel, layer, heads, line, len(vectors)),
        f"attention_gradients_{layer}",
        (GROUP,),
        [
            *near,
            *[HBM] * (2 + GROUP),
            pl.BlockSpec((heads, *wide.shape[1:]), own_heads),
            pl.BlockSpec((heads, *small.shape[1:]), own_heads),
            *[whole(vector.shape) for vector in vectors],
        ],
        [
            whole_once(outs[0].shape),
            pl.BlockSpec((1, 2, IMAGES, own), lambda s, ids, kinds: (s, 0, 0, 0)),
        ],
        outs,
        [
            pltpu.VMEM((2, GROUP * IMAGES, own), FULL),
            pltpu.VMEM((GROUP, count, width), LOW),
            pltpu.VMEM((GROUP, count, width), LOW),
            pltpu.VMEM((GROUP, count, 3 * own), LOW),
            pltpu.VMEM((GROUP, count, own), LOW),
            pltpu.VMEM((4, count, own), LOW),
            pltpu.VMEM((heads, count, count), FULL),
            pltpu.VMEM((3, count, own), FULL),
            pltpu.VMEM((count, own), FULL),
            pltpu.VMEM((heads, *wide.shape[1:]), FULL),
            pltpu.VMEM((heads, *small.shape[1:]), FULL),
            pltpu.VMEM((2, GROUP, count, width), FULL),
            pltpu.VMEM((3, own, width), LOW),
            pltpu.VMEM((own, width), LOW),
            pltpu.VMEM((heads, count, count), FULL),
            pltpu.VMEM((GROUP, *images[0].shape), FULL),
            pltpu.SemaphoreType.DMA((2, 2 * GROUP)),
            pltpu.SemaphoreType.DMA((2 + GROUP,)),
        ],
        2 * GROUP * count * width * own * 8 + GROUP * heads * count * count * 4096,
        8 * GROUP * count * width + 8 * width * local,
        2,
        after,
    )(
        ids, kinds, *map(in_hbm, (*near_x, *near_y, token_rows, out_proj, *images)), wide, small, *vectors
    )


def swap(value, axis):
    return lax.ppermute(value, axis, [(0, 1), (1, 0)])


def shift(value, line, by=1):
    return lax.ppermute(value, "line", [(i, (i + by) % line) for i in range(line)])


def gather_line(half):
    return lax.all_gather(half, ("line", "tensor"), tiled=True)


def plane_steps(value, half, slow=False):
    if slow:
        far = yield [swap(half, "row"), swap(half, "col"), swap_corner(half)]
        others = yield [swap(part, "tensor") for part in far]
        return [value, *far, *others]
    across, along = yield [swap(half, "row"), swap(half, "col")]
    corner, *others = yield [swap_corner(half), swap(across, "tensor"), swap(along, "tensor")]
    others += yield [swap(corner, "tensor")]
    return [value, across, along, corner, *others]


def swap_corner(value):
    return lax.ppermute(value, ("col", "row"), [(0, 3), (3, 0), (1, 2), (2, 1)])


def plane_all(value):
    across, along, corner = yield [swap(value, "row"), swap(value, "col"), swap_corner(value)]
    return [value, across, along, corner]


def line_all(value, line):
    far = yield [shift(value, line, by) for by in range(1, line)]
    return [value, *far]


def local(
    tokens,
    segment_ids,
    timesteps,
    norm_gain,
    norm_bias,
    token_proj,
    time_proj,
    bias_table,
    out_proj,
    hidden_in,
    hidden_out,
    branch_bias,
    cotangent,
    *,
    line,
):
    count, width = tokens.shape
    depth, _, _, local_width = token_proj.shape
    heads = bias_table.shape[1]
    units = hidden_in.shape[2]
    own = local_width // GROUP
    n_dp = GROUP * line
    features = width // n_dp
    line_at = lax.axis_index("line")
    ids = jnp.stack(
        [segment_ids[-1], line_at, lax.axis_index("col"), lax.axis_index("row"), lax.axis_index("tensor")]
    ).astype(jnp.int32)
    embedded = sinusoid(timesteps[0], jnp.arange(width, dtype=jnp.int32), width)
    per_image = lax.dot_general(
        time_proj, embedded, (((2,), (1,)), ((), ())), preferred_element_type=FULL
    )
    per_image = jnp.swapaxes(per_image, 2, 3)
    info = jnp.concatenate([timesteps[0], segment_ids[-1:]]).astype(FULL)
    packed = jnp.concatenate(
        [
            per_image.reshape(2 * depth * IMAGES, local_width),
            jnp.pad(info[None], ((0, 7), (0, local_width - IMAGES - 1))),
        ]
    )
    own_feature = line_at * (GROUP * features) + jnp.arange(GROUP * features, dtype=jnp.int32)
    token_rows = jnp.swapaxes(token_proj, 2, 3)
    wide, small = expand_table(bias_table.reshape(depth * heads, -1))

    stream = (tokens,)
    saved = []
    moves = Moves()
    moves.start("packed", plane_all(packed))
    half = lax.dynamic_slice_in_dim(cotangent, lax.axis_index("tensor") * (count // 2), count // 2, 0)
    gathered_up = gather_line(half.astype(FULL))
    for layer in range(depth):
        held, normed, half, rows, partial, bias = attend(
            layer, ids, stream, norm_gain, norm_bias, branch_bias, token_rows, per_image, out_proj, wide, small
        )
        if layer == depth - 1:
            partial, other, gathered_up = moves.chain(partial, [gathered_up])
        else:
            partial, other = moves.chain(partial)
        moves.start(("first", layer), plane_steps(normed, half))
        if layer == depth - 1:
            near = jnp.stack(
                [part[2 * depth * IMAGES, : IMAGES + 1] for part in moves.found["packed"]]
            )
            kinds = near[:, IMAGES].astype(jnp.int32)
            info = jnp.pad(near, ((0, 8 - GROUP), (0, 128 - IMAGES - 1)))
            moves.start("info", line_all(info, line))
        middle, half_second, slope, partial = feed(
            layer,
            ids,
            held,
            partial,
            other,
            branch_bias,
            norm_gain,
            norm_bias,
            hidden_in,
            hidden_out,
        )
        partial, other = moves.chain(partial)
        line_second = gather_line(half_second)
        saved.append((held, rows, middle, slope, line_second, bias))
        stream = (middle, partial, other)
    output = (stream[0] + (stream[1] + stream[2]) + branch_bias[depth - 1, 1]).astype(LOW)

    upstream = (cotangent,)
    collected = [None] * depth
    vectors = [None] * depth
    gathered = [None] * depth
    gathered_line = [None] * depth
    for layer in reversed(range(depth)):
        held, rows, middle, slope, _, bias = saved[layer]
        current, half_up, feed_sums, partial = feed_back(
            layer, ids, upstream, slope, hidden_in, hidden_out, norm_gain
        )
        partial, other = moves.chain(partial)
        if layer < depth - 1:
            gathered_up = gather_line(half_up)
        back_middle, half, middle_sums, back_partial = attend_back(
            layer,
            ids,
            current,
            partial,
            other,
            middle,
            norm_gain,
            rows,
            bias,
            out_proj,
            token_rows,
        )
        if layer > 0:
            back_partial, other, gathered_line[0] = moves.chain(back_partial, [saved[0][4]])
        else:
            back_partial, other = moves.chain(back_partial)
        moves.start(("branch", layer), plane_steps(back_middle, half, layer == 0))
        upstream = (back_middle, back_partial, other, held)
        vectors[layer] = (feed_sums, middle_sums)
        gathered[layer] = gathered_up
    gradient_tokens, last_sums = finish(*upstream, norm_gain)
    gathered_line[depth - 1] = saved[depth - 1][4]
    sums = [last_sums, *[pair[0] for pair in vectors], *[pair[1] for pair in vectors]]
    packed = moves.found["packed"]
    tokens_of = {}


    def run_feed(layer, turn, due=()):
        pieces = feed_gradients(
            layer, line, ids, gathered_line[layer], gathered[layer], hidden_in, hidden_out, after=turn
        )
        turn, *due = moves.kernel(pieces[0], due)
        moves.start(("feed", layer), feed_scatter(layer, ids, (turn, *pieces[1:]), line))
        return turn, due

    def run_attention(layer, turn, due=()):
        token, found = attention_gradients(
            layer,
            line,
            ids,
            kinds,
            moves.found["first", layer],
            moves.hurry(("branch", layer)),
            token_rows,
            packed,
            out_proj,
            wide,
            small,
            sums if layer == 0 else (),
            after=turn,
        )
        turn, *due = moves.kernel(found, due)
        tokens_of[layer] = lax.psum_scatter(token, "line", scatter_dimension=0, tiled=True)
        moved = jnp.swapaxes(turn, 0, 1).reshape(2 * GROUP * IMAGES, own)
        moves.start(("images", layer), line_all(moved, line))
        return turn, due

    top = depth - 1
    turn, _ = run_feed(top, (last_sums,))
    turn, (gathered[0],) = run_attention(top, (turn,), [gathered[0]])
    turn, _ = run_attention(0, (turn,))
    _, (tokens_of[top],) = run_feed(0, (turn,), [tokens_of[top]])
    every = jnp.concatenate([part[:GROUP, :IMAGES].reshape(-1) for part in moves.found["info"]])
    embedded_every = sinusoid(every, own_feature, width)
    def deal(layer):
        moves.start(
            ("attention", layer),
            attention_deal(
                layer,
                line,
                ids,
                tokens_of[layer],
                embedded_every,
                moves.hurry(("images", layer)),
                heads // GROUP,
                width,
                own,
            ),
        )

    for layer in range(1, depth):
        deal(layer)
    moves.hurry(("images", 0))
    moves.finish()
    feeds = [moves.found["feed", layer] for layer in range(depth)]
    blocks = feed_deal(depth, line, ids, [part for inner, _ in feeds for part in inner])
    early = (1, line - 1)
    moved = {by: shift(blocks[by], line, by) for by in range(1, line) if by in early}
    tokens_of[0], *held = gate(
        [tokens_of[0], *[moved.get(by, block) for by, block in enumerate(blocks)]]
    )
    blocks = [
        block if by == 0 or by in early else shift(block, line, by) for by, block in enumerate(held)
    ]
    deal(0)
    moves.finish()
    token, time, table, projection, gain, shifts, bias = join_attention(
        depth,
        line,
        ids,
        [moves.found["attention", layer] for layer in range(depth)],
        heads,
        local_width,
        width,
    )
    projection = jnp.swapaxes(projection, 0, 1)
    gain, *blocks = gate([gain, *blocks])
    inner, outer = join_feed(line, ids, blocks, [part for _, outer in feeds for part in outer], units)
    return (
        output,
        gradient_tokens,
        gain,
        shifts,
        token,
        time,
        table,
        projection,
        inner,
        outer,
        bias,
    )


def solution(mesh):
    line = mesh.shape["dp"] // GROUP
    fine = Mesh(mesh.devices.reshape(line, 2, 2, mesh.shape["tensor"]), (*LINES, "tensor"))
    return jax.shard_map(
        functools.partial(local, line=line),
        mesh=fine,
        in_specs=(
            P(LINES, None),
            P(LINES),
            P(LINES, None),
            P(),
            P(),
            P(None, None, None, "tensor"),
            P(None, None, None, "tensor"),
            P(None, "tensor", None),
            P(None, "tensor", None),
            P(None, None, "tensor"),
            P(None, "tensor", None),
            P(),
            P(LINES, None),
        ),
        out_specs=(
            P(LINES, None),
            P(LINES, None),
            P(None, None, LINES),
            P(None, None, LINES),
            P(None, None, LINES, "tensor"),
            P(None, None, LINES, "tensor"),
            P(None, "tensor", LINES),
            P(None, ("tensor", *LINES), None),
            P(None, LINES, "tensor"),
            P(None, ("tensor", *LINES), None),
            P(None, None, LINES),
        ),
        check_vma=False,
    )
```
